32 devices in a mesh: groups: 2 (over y), sector: 4 (over z), blk: 2 (over x), op: 2 (over core).
Axes of the slice: x: 2, y: 2, z: 4, core: 2. Of those that a mesh axis runs over, the one named last changes fastest.
Arguments:
- psi: bfloat16 [384, 128, 128], P(('groups', 'sector', 'blk')), parts along dimension 0, may hold values from -6 to 6
- left_ops: bfloat16 [128, 2, 128, 128], P(('groups', 'op'), 'blk'), parts along dimension 0, may hold values from -0.0625 to 0.0625
- right_ops: bfloat16 [128, 2, 128, 128], P(('groups', 'op')), parts along dimension 0, may hold values from -0.5 to 0.5
- left_qn: int32 [384], P(('groups', 'sector', 'blk')), parts along dimension 0, may hold values from 0 to 1
- right_qn: int32 [384], P(('groups', 'sector', 'blk')), parts along dimension 0, may hold values from 0 to 1
- pair_slot: int32 [128, 192], P(('groups', 'op'), ('sector', 'blk')), parts along dimension 0, may hold values from 0 to 15
- slot_target: int32 [8, 2, 16], P(('groups', 'sector'), 'blk'), parts along dimension 0, may hold values from 0 to 23
Outputs:
- sigma: float32 [384, 128, 128], P(('groups', 'sector', 'blk')), parts along dimension 0
The draws below stay inside these ranges and needn't reach their ends.
There are 2 independent parts, one for each index of `groups`. The reference program is written for one: setup_inputs(seed, part) draws one part's arguments, and reference() takes and returns one part's arrays. A program takes and returns all parts, laid end to end along the dimension named above; each array names one. Nothing has to cross between parts.
Inputs may be any that keep to these rules, and one draw needn't show every extreme that they name: `pair_slot`: slot c leads to the owner of row c // 4; all pairs of one source device with equal slot have one target.
All inputs are finite; a program needn't handle non-finite values.
Results may differ from the reference program's by a relative error of at most 0.0029.
Values may be sent and summed in bfloat16 or wider, within the bound.
No kernel may reach another device: no remote copies, remote signals or barrier semaphores. Data moves between devices by JAX's collectives and lax.ppermute only.
A program may use at most 64 MiB of HBM per device.

```python
import jax
import jax.numpy as jnp
from jax import lax

W = 128
K = 64
SEC_DEV = 24
QR = 2
CAP = 4
NS = 4
NB = 2
QL = 2
NSEC = 192


def place_ends(values, key, smallest, largest):
    place = [jax.random.randint(jax.random.fold_in(key, axis), (), 0, length) for axis, length in enumerate(values.shape)]
    longest = values.shape.index(max(values.shape))
    beside = place[:longest] + [(place[longest] + 1) % values.shape[longest]] + place[longest + 1:]
    return values.at[tuple(place)].set(smallest).at[tuple(beside)].set(largest)


def levels(own_key, extent, split, low, high):
    level, own = 1.0, jax.random.fold_in(own_key, 6)
    for axis_at, blocks in split:
        draws = jnp.exp(jax.random.uniform(jax.random.fold_in(own, axis_at), (blocks,), jnp.float32, low / len(split), high / len(split)))
        level = level * jnp.repeat(draws, extent[axis_at] // blocks).reshape([-1 if axis == axis_at else 1 for axis in range(len(extent))])
    return level


def noise(rng, extent, deviation, limit, split=(), kind=jnp.bfloat16):
    level = levels(rng, extent, split, -0.22, 0.18) if split else 1.0
    array = jax.random.normal(rng, extent, jnp.float32) * deviation * level
    return jnp.minimum(jnp.maximum(array, -limit), limit).astype(kind)


def setup_inputs(seed: int = 0, part: int = 0) -> dict:
    seeds = jax.random.split(jax.random.key(seed), 8)
    own_keys = jax.random.split(jax.random.fold_in(seeds[7], part), 8)
    psi = noise(own_keys[0], (NSEC, W, W), 1.0, 6.0, ((0, 8),))
    left_ops = noise(own_keys[1], (K, QL, W, W), (W * K) ** -0.5, 0.0625, ((0, 2), (1, 2)))
    right_ops = noise(own_keys[2], (K, QR, W, W), W ** -0.5, 0.5, ((0, 2),))
    left_qn = place_ends(jax.random.randint(own_keys[3], (NSEC,), 0, QL), jax.random.fold_in(own_keys[3], 1), 0, QL - 1).astype(jnp.int32)
    right_qn = place_ends(jax.random.randint(own_keys[4], (NSEC,), 0, QR), jax.random.fold_in(own_keys[4], 1), 0, QR - 1).astype(jnp.int32)
    pair_slot = place_ends(jax.random.randint(own_keys[5], (K, NSEC), 0, NS * CAP), jax.random.fold_in(own_keys[5], 1), 0, (NS * CAP) - 1).astype(jnp.int32)
    slot_target = place_ends(jax.random.randint(own_keys[6], (NS, NB, NS * CAP), 0, SEC_DEV), jax.random.fold_in(own_keys[6], 1), 0, SEC_DEV - 1).astype(jnp.int32)
    return {"psi": psi, "left_ops": left_ops, "right_ops": right_ops, "left_qn": left_qn, "right_qn": right_qn, "pair_slot": pair_slot, "slot_target": slot_target}


def reference(psi, left_ops, right_ops, left_qn, right_qn, pair_slot, slot_target):
    nsec = psi.shape[0]
    per_row = NB * SEC_DEV
    source = jnp.arange(nsec, dtype=jnp.int32)
    row_index = source // per_row
    class_index = (source // SEC_DEV) % NB
    psi_wide = psi.astype(jnp.float32)

    def one_operator(total, inputs):
        left_k, right_k, slots = inputs
        chosen_right = right_k[right_qn].astype(jnp.float32)
        half = jnp.einsum("sab,scb->sac", psi_wide, chosen_right).astype(jnp.bfloat16)
        chosen_left = left_k[left_qn].astype(jnp.float32)
        term = jnp.einsum("sab,sbc->sac", chosen_left, half.astype(jnp.float32))
        owner = slots // CAP
        local = slot_target[row_index, class_index, slots]
        target = (owner * NB + class_index) * SEC_DEV + local
        return total + jax.ops.segment_sum(term, target.astype(jnp.int32), num_segments=nsec), None

    start = jnp.zeros(psi.shape, jnp.float32)
    sigma, unused = lax.scan(one_operator, start, (left_ops, right_ops, pair_slot))
    return sigma
```

```python
import functools

import jax
import jax.numpy as jnp
from jax import lax
from jax.experimental import pallas as pl
from jax.experimental.pallas import tpu as pltpu
from jax.sharding import PartitionSpec as P

CAP = 4
GROUP = 4
BLOCK_K = 16
NT = (((1,), (1,)), ((), ()))


def pick(left_qn, order, wanted):
    count = left_qn.shape[0]

    def step(s, n):
        order[n] = s
        return n + (left_qn[s] == wanted).astype(jnp.int32)

    n = lax.fori_loop(0, count, step, jnp.int32(0))
    for extra in range(GROUP - 1):
        order[n + extra] = jnp.int32(count)
    return lax.div(n + GROUP - 1, jnp.int32(GROUP))


def accumulate(wanted, left_qn, right_qn, slots, psi, right, left, half, total, order):
    sectors, width = psi.shape[0], psi.shape[1]
    operators, right_count = right.shape[0], right.shape[1]
    zero = jnp.zeros((width, width), jnp.bfloat16)

    def one_group(g, unused):
        members = [order[g * GROUP + j] for j in range(GROUP)]
        places = [jnp.minimum(s, sectors - 1) for s in members]
        quanta = [jnp.where(s < sectors, right_qn[at], -1) for s, at in zip(members, places)]
        sources = []
        for p in range(GROUP // 2):
            rows = []
            for e in (2 * p, 2 * p + 1):
                block = psi[places[e]]
                rows.append(
                    jnp.concatenate([jnp.where(quanta[e] == r, block, zero) for r in range(right_count)], axis=1)
                )
            sources.append(jnp.concatenate(rows, axis=0))
        for first in range(0, operators, BLOCK_K):
            stream = jnp.concatenate(
                [right[first : first + BLOCK_K, r].reshape(BLOCK_K * width, width) for r in range(right_count)], axis=1
            )
            for p in range(GROUP // 2):
                product = lax.dot_general(stream, sources[p], NT, preferred_element_type=jnp.float32)
                half[:, p] = product.astype(jnp.bfloat16).reshape(BLOCK_K, width, 2 * width)
            for k in range(BLOCK_K):
                block = left[first + k]
                weights = jnp.concatenate(
                    [jnp.concatenate([block, zero], axis=1), jnp.concatenate([zero, block], axis=1)], axis=0
                )
                term = lax.dot_general(
                    half[k].reshape(GROUP // 2 * width, 2 * width), weights, NT, preferred_element_type=jnp.float32
                )
                for j in range(GROUP):
                    p, e = j // 2, j % 2
                    total[slots[first + k, places[j]]] += term[
                        p * width : (p + 1) * width, e * width : (e + 1) * width
                    ]
        return unused

    lax.fori_loop(0, pick(left_qn, order, wanted), one_group, 0)


def own_kernel(left_local, left_qn, right_qn, slots, psi, right, left, total, half, order):
    total[...] = jnp.zeros_like(total)
    mine = lax.axis_index("blk")
    for l in range(left_local):
        accumulate(
            mine * left_local + l, left_qn, right_qn, slots, psi, right, left.at[:, l], half, total, order
        )


def other_kernel(left_qn, right_qn, slots, psi, right, start, lefts, *rest):
    outs, (half, total, order) = rest[:-3], rest[-3:]
    shifts, left_local = lefts.shape[0], lefts.shape[2]
    total[...] = start[...]
    mine = lax.axis_index("blk")

    def one_shift(d, unused):
        owner = lax.rem(mine + d + 1, jnp.int32(shifts + 1))
        for l in range(left_local):
            accumulate(
                owner * left_local + l, left_qn, right_qn, slots, psi, right, lefts.at[d, :, l], half, total, order
            )
        return unused

    lax.fori_loop(0, shifts, one_shift, 0)
    row = lax.axis_index("sector")
    for d, out in enumerate(outs):
        owner = lax.rem(row + d, jnp.int32(len(outs)))
        for m in range(CAP):
            out[m] = total[owner * CAP + m].astype(jnp.bfloat16)


def assemble_kernel(rows, targets, *rest):
    mine, theirs, out = rest[:rows], rest[rows : 2 * rows], rest[-1]
    out[...] = jnp.zeros_like(out)
    row = lax.axis_index("sector")
    for d in range(rows):
        source = lax.rem(row + rows - d, jnp.int32(rows))
        for m in range(CAP):
            block = mine[d][m].astype(jnp.float32) + theirs[d][m].astype(jnp.float32)
            out[targets[source, row * CAP + m]] += block.T


def shards(sizes, psi, left_ops, right_ops, left_qn, right_qn, pair_slot, slot_target):
    rows, blocks, halves = sizes
    sectors, width = psi.shape[0], psi.shape[1]
    operators, left_local = left_ops.shape[0], left_ops.shape[1]
    slot_count = rows * CAP
    smem = pl.BlockSpec(memory_space=pltpu.SMEM)
    vmem = pl.BlockSpec(memory_space=pltpu.VMEM)
    slot_shape = (slot_count, width, width)
    half_shape = pltpu.VMEM((BLOCK_K, GROUP // 2, width, 2 * width), jnp.bfloat16)
    order_shape = pltpu.SMEM((sectors + GROUP,), jnp.int32)
    cost = pl.CostEstimate(
        flops=4 * operators * sectors * width**3, bytes_accessed=8 * 2**20, transcendentals=0
    )
    params = pltpu.CompilerParams(vmem_limit_bytes=40 * 2**20)

    targets = lax.all_gather(slot_target[0, 0], "sector")
    shift_blk = [
        lax.ppermute(left_ops, "blk", [((b + d) % blocks, b) for b in range(blocks)]) for d in range(1, blocks)
    ]
    started = pl.pallas_call(
        functools.partial(own_kernel, left_local),
        out_shape=jax.ShapeDtypeStruct(slot_shape, jnp.float32),
        in_specs=[smem] * 3 + [vmem] * 3,
        out_specs=vmem,
        scratch_shapes=[half_shape, order_shape],
        compiler_params=params,
        cost_estimate=cost,
        name="own_left",
    )(left_qn, right_qn, pair_slot, psi, right_ops, left_ops)
    partial = pl.pallas_call(
        other_kernel,
        out_shape=[jax.ShapeDtypeStruct((CAP, width, width), jnp.bfloat16)] * rows,
        in_specs=[smem] * 3 + [vmem] * 4,
        out_specs=[vmem] * rows,
        scratch_shapes=[half_shape, pltpu.VMEM(slot_shape, jnp.float32), order_shape],
        compiler_params=params,
        cost_estimate=cost,
        name="other_left",
    )(left_qn, right_qn, pair_slot, psi, right_ops, started, jnp.stack(shift_blk))
    mine = [partial[0]] + [
        lax.ppermute(partial[d], "sector", [(i, (i + d) % rows) for i in range(rows)]) for d in range(1, rows)
    ]
    theirs = [lax.ppermute(block, "op", [(h, halves - 1 - h) for h in range(halves)]) for block in mine]
    return pl.pallas_call(
        functools.partial(assemble_kernel, rows),
        out_shape=jax.ShapeDtypeStruct((sectors, width, width), jnp.float32),
        in_specs=[smem] + [vmem] * (2 * rows),
        out_specs=vmem,
        compiler_params=params,
        name="assemble",
    )(targets, *mine, *theirs)


def solution(mesh):
    in_specs = (
        P(("groups", "sector", "blk"), None, None),
        P(("groups", "op"), "blk", None, None),
        P(("groups", "op"), None, None, None),
        P(("groups", "sector", "blk")),
        P(("groups", "sector", "blk")),
        P(("groups", "op"), ("sector", "blk")),
        P(("groups", "sector"), "blk", None),
    )
    out_specs = P(("groups", "sector", "blk"), None, None)
    sizes = tuple(mesh.shape[name] for name in ("sector", "blk", "op"))
    return jax.shard_map(
        functools.partial(shards, sizes), mesh=mesh, in_specs=in_specs, out_specs=out_specs, check_vma=False
    )
```

```python
import functools

import jax
import jax.numpy as jnp
from jax import lax
from jax.experimental import pallas as pl
from jax.experimental.pallas import tpu as pltpu
from jax.sharding import PartitionSpec as P

CAP = 4
GROUP = 4
BLOCK_K = 8
TAIL = 16
NT = (((1,), (1,)), ((), ()))


def pick(left_qn, order, wanted):
    count = left_qn.shape[0]

    def step(s, n):
        order[n] = s
        return n + (left_qn[s] == wanted).astype(jnp.int32)

    n = lax.fori_loop(0, count, step, jnp.int32(0))
    for extra in range(GROUP - 1):
        order[n + extra] = jnp.int32(count)
    return lax.div(n + GROUP - 1, jnp.int32(GROUP))


def accumulate(groups, first, pieces, right_qn, slots, psi, right, half, total, order):
    sectors, width = psi.shape[0], psi.shape[1]
    right_count = right.shape[1]
    zero = jnp.zeros((width, width), jnp.bfloat16)

    def one_group(g, unused):
        members = [order[g * GROUP + j] for j in range(GROUP)]
        places = [jnp.minimum(s, sectors - 1) for s in members]
        quanta = [jnp.where(s < sectors, right_qn[at], -1) for s, at in zip(members, places)]
        sources = []
        for p in range(GROUP // 2):
            rows = []
            for e in (2 * p, 2 * p + 1):
                block = psi[places[e]]
                rows.append(
                    jnp.concatenate([jnp.where(quanta[e] == r, block, zero) for r in range(right_count)], axis=1)
                )
            sources.append(jnp.concatenate(rows, axis=0))

        def right_side(i):
            at = pl.ds(first + i * BLOCK_K, BLOCK_K)
            stream = jnp.concatenate(
                [right[at, r].reshape(BLOCK_K * width, width) for r in range(right_count)], axis=1
            )
            for p in range(GROUP // 2):
                product = lax.dot_general(stream, sources[p], NT, preferred_element_type=jnp.float32)
                half[i % 2, :, p] = product.astype(jnp.bfloat16).reshape(BLOCK_K, width, 2 * width)

        def left_side(i):
            for k in range(BLOCK_K):
                block = pieces[i][k]
                weights = jnp.concatenate(
                    [jnp.concatenate([block, zero], axis=1), jnp.concatenate([zero, block], axis=1)], axis=0
                )
                term = lax.dot_general(
                    half[i % 2, k].reshape(GROUP // 2 * width, 2 * width),
                    weights,
                    NT,
                    preferred_element_type=jnp.float32,
                )
                for j in range(GROUP):
                    p, e = j // 2, j % 2
                    total[slots[places[j], first + i * BLOCK_K + k]] += term[
                        p * width : (p + 1) * width, e * width : (e + 1) * width
                    ]

        right_side(0)
        for i in range(len(pieces)):
            if i + 1 < len(pieces):
                right_side(i + 1)
            left_side(i)
        return unused

    lax.fori_loop(0, groups, one_group, 0)


def split_pieces(left):
    return [left.at[pl.ds(at, BLOCK_K)] for at in range(0, left.shape[0], BLOCK_K)]


def own_kernel(
    left_qn_in, right_qn_in, slots_in, psi_in, right_in, left_in, total,
    left_qn, right_qn, slots, psi, right, left, half, order, sems,
):
    left_local = left.shape[1]
    middle = left.shape[0] // 2
    parts = [pl.ds(0, middle), pl.ds(middle, middle)]
    pairs = [(left_qn_in, left_qn), (right_qn_in, right_qn), (slots_in, slots), (psi_in, psi)]
    for part in parts:
        pairs += [(right_in.at[part], right.at[part]), (left_in.at[part], left.at[part])]
    copies = [pltpu.make_async_copy(src, dst, sems.at[i]) for i, (src, dst) in enumerate(pairs)]
    for copy in copies:
        copy.start()
    total[...] = jnp.zeros_like(total)
    mine = lax.axis_index("blk")
    for copy in copies[:-2]:
        copy.wait()
    for i in range(2):
        if i == 1:
            for copy in copies[-2:]:
                copy.wait()
        for l in range(left_local):
            groups = pick(left_qn, order, mine * left_local + l)
            pieces = split_pieces(left.at[parts[i], l])
            accumulate(groups, i * middle, pieces, right_qn, slots, psi, right, half, total, order)


def other_kernel(last, offset, left_qn, right_qn, slots, slot_target, psi, right, start, *rest):
    if last:
        lefts, outs, (half, total, order) = rest[:2], rest[2:-3], rest[-3:]
    else:
        lefts, (total, half, order) = rest[:2], rest[2:]
    shifts, left_local = lefts[0].shape[0], lefts[0].shape[2]
    operators = slots.shape[1]
    total[...] = start[...]
    mine, row = lax.axis_index("blk"), lax.axis_index("sector")
    first = lax.rem(row + offset, jnp.int32(2)) * (operators // 2)

    def one_shift(d, unused):
        owner = lax.rem(mine + d + 1, jnp.int32(shifts + 1))
        for l in range(left_local):
            groups = pick(left_qn, order, owner * left_local + l)
            pieces = [piece for left in lefts for piece in split_pieces(left.at[d, :, l])]
            accumulate(groups, first, pieces, right_qn, slots, psi, right, half, total, order)
        return unused

    lax.fori_loop(0, shifts, one_shift, 0)
    if not last:
        return
    width = total.shape[1]
    line = lax.broadcasted_iota(jnp.int32, (TAIL, width), 0)
    for d, out in enumerate(outs):
        owner = lax.rem(row + d, jnp.int32(len(outs)))
        ids = jnp.zeros((TAIL, width), jnp.int32)
        for m in range(CAP):
            out[m * width : (m + 1) * width, :] = total[owner * CAP + m].astype(jnp.bfloat16)
            ids = jnp.where(line == m, slot_target[0, 0, owner * CAP + m], ids)
        out[CAP * width :, :] = ids.astype(jnp.float32).astype(jnp.bfloat16)


def assemble_kernel(rows, *rest):
    mine, theirs, out = rest[:rows], rest[rows : 2 * rows], rest[-1]
    width = out.shape[1]
    out[...] = jnp.zeros_like(out)
    for d in range(rows):
        ids = mine[d][CAP * width :, :].astype(jnp.float32)
        for m in range(CAP):
            at = pl.ds(m * width, width)
            block = mine[d][at, :].astype(jnp.float32) + theirs[d][at, :].astype(jnp.float32)
            target = jnp.max(ids[m : m + 1, :]).astype(jnp.int32)
            out[target] += block.T


def shards(sizes, psi, left_ops, right_ops, left_qn, right_qn, pair_slot, slot_target):
    rows, blocks, halves = sizes
    sectors, width = psi.shape[0], psi.shape[1]
    operators, left_local = left_ops.shape[0], left_ops.shape[1]
    slot_count = rows * CAP
    slots = pair_slot.T
    smem = pl.BlockSpec(memory_space=pltpu.SMEM)
    vmem = pl.BlockSpec(memory_space=pltpu.VMEM)
    hbm = pl.BlockSpec(memory_space=pltpu.HBM)
    slot_shape = (slot_count, width, width)
    half_shape = pltpu.VMEM((2, BLOCK_K, GROUP // 2, width, 2 * width), jnp.bfloat16)
    order_shape = pltpu.SMEM((sectors + GROUP,), jnp.int32)
    params = pltpu.CompilerParams(vmem_limit_bytes=40 * 2**20)

    def cost(share):
        flops = int(16 * operators * sectors * width**3 * share)
        return pl.CostEstimate(flops=flops, bytes_accessed=4 * 2**20, transcendentals=0)

    first = lax.rem(lax.axis_index("sector"), 2) * (operators // 2)
    quarter = operators // 4
    swap = [(i, i ^ 1) for i in range(rows)]
    sent = [lax.dynamic_slice_in_dim(left_ops, first + i * quarter, quarter, 0) for i in range(2)]
    near = [
        [lax.ppermute(part, "blk", [((b + d) % blocks, b) for b in range(blocks)]) for d in range(1, blocks)]
        for part in sent
    ]
    far = [[lax.ppermute(part, "sector", swap) for part in parts] for parts in near]
    near, far = ([jnp.stack(parts) for parts in side] for side in (near, far))

    total = pl.pallas_call(
        own_kernel,
        out_shape=jax.ShapeDtypeStruct(slot_shape, jnp.float32),
        in_specs=[hbm] * 6,
        out_specs=vmem,
        scratch_shapes=[
            pltpu.SMEM(left_qn.shape, jnp.int32),
            pltpu.SMEM(right_qn.shape, jnp.int32),
            pltpu.SMEM(slots.shape, jnp.int32),
            pltpu.VMEM(psi.shape, psi.dtype),
            pltpu.VMEM(right_ops.shape, right_ops.dtype),
            pltpu.VMEM(left_ops.shape, left_ops.dtype),
            half_shape,
            order_shape,
            pltpu.SemaphoreType.DMA((8,)),
        ],
        compiler_params=pltpu.CompilerParams(vmem_limit_bytes=54 * 2**20),
        cost_estimate=cost(0.5),
        name="own_left",
    )(left_qn, right_qn, slots, psi, right_ops, left_ops)
    common = (left_qn, right_qn, slots, slot_target, psi, right_ops)
    total = pl.pallas_call(
        functools.partial(other_kernel, False, 0),
        out_shape=jax.ShapeDtypeStruct(slot_shape, jnp.float32),
        in_specs=[smem] * 4 + [vmem] * 5,
        out_specs=vmem,
        scratch_shapes=[half_shape, order_shape],
        compiler_params=params,
        cost_estimate=cost(0.25),
        name="other_left_near",
    )(*common, total, *near)
    partial = pl.pallas_call(
        functools.partial(other_kernel, True, 1),
        out_shape=[jax.ShapeDtypeStruct((CAP * width + TAIL, width), jnp.bfloat16)] * rows,
        in_specs=[smem] * 4 + [vmem] * 5,
        out_specs=[vmem] * rows,
        scratch_shapes=[half_shape, pltpu.VMEM(slot_shape, jnp.float32), order_shape],
        compiler_params=params,
        cost_estimate=cost(0.25),
        name="other_left_far",
    )(*common, total, *far)
    mine = [partial[0]] + [
        lax.ppermute(partial[d], "sector", [(i, (i + d) % rows) for i in range(rows)]) for d in range(1, rows)
    ]
    theirs = [lax.ppermute(block, "op", [(h, halves - 1 - h) for h in range(halves)]) for block in mine]
    return pl.pallas_call(
        functools.partial(assemble_kernel, rows),
        out_shape=jax.ShapeDtypeStruct((sectors, width, width), jnp.float32),
        in_specs=[vmem] * (2 * rows),
        out_specs=vmem,
        compiler_params=params,
        name="assemble",
    )(*mine, *theirs)


def solution(mesh):
    in_specs = (
        P(("groups", "sector", "blk"), None, None),
        P(("groups", "op"), "blk", None, None),
        P(("groups", "op"), None, None, None),
        P(("groups", "sector", "blk")),
        P(("groups", "sector", "blk")),
        P(("groups", "op"), ("sector", "blk")),
        P(("groups", "sector"), "blk", None),
    )
    out_specs = P(("groups", "sector", "blk"), None, None)
    sizes = tuple(mesh.shape[name] for name in ("sector", "blk", "op"))
    return jax.shard_map(
        functools.partial(shards, sizes), mesh=mesh, in_specs=in_specs, out_specs=out_specs, check_vma=False
    )
```

```python
import functools

import jax
import jax.numpy as jnp
from jax import lax
from jax.experimental import pallas as pl
from jax.experimental.pallas import tpu as pltpu
from jax.sharding import PartitionSpec as P

CAP = 4
GROUP = 4
BLOCK_K = 8
TAIL = 16
NT = (((1,), (1,)), ((), ()))


def arrange(left_qn, order, starts, blocks, left_local):
    mine = lax.axis_index("blk")
    count = left_qn.shape[0]

    def one_code(code, n):
        starts[code] = n
        owner = lax.rem(mine + lax.div(code, jnp.int32(left_local)), jnp.int32(blocks))
        wanted = owner * left_local + lax.rem(code, jnp.int32(left_local))

        def one_sector(s, n):
            order[n] = s
            return n + (left_qn[s] == wanted).astype(jnp.int32)

        return lax.fori_loop(0, count, one_sector, n)

    starts[blocks * left_local] = lax.fori_loop(0, blocks * left_local, one_code, jnp.int32(0))


def right_kernel(
    blocks, left_local, left_qn_in, right_qn_in, psi_in, right_in, half,
    left_qn, right_qn, psi, right, sources, order, starts, sems,
):
    sectors, width = psi.shape[0], psi.shape[1]
    right_count = right.shape[1]
    steps = right.shape[0] // BLOCK_K
    zero = jnp.zeros((width, width), jnp.bfloat16)

    def right_copy(i):
        at = pl.ds(i * BLOCK_K, BLOCK_K)
        return pltpu.make_async_copy(right_in.at[at], right.at[at], sems.at[3 + i])

    copies = [
        pltpu.make_async_copy(left_qn_in, left_qn, sems.at[0]),
        pltpu.make_async_copy(right_qn_in, right_qn, sems.at[1]),
        pltpu.make_async_copy(psi_in, psi, sems.at[2]),
    ]
    for copy in copies:
        copy.start()
    for i in range(steps):
        right_copy(i).start()
    copies[0].wait()
    copies[1].wait()
    arrange(left_qn, order, starts, blocks, left_local)
    copies[2].wait()
    for pair in range(sectors // 2):
        for e in range(2):
            s = order[2 * pair + e]
            block = psi[s]
            for r in range(right_count):
                sources[pair, e * width : (e + 1) * width, r * width : (r + 1) * width] = jnp.where(
                    right_qn[s] == r, block, zero
                )

    def one_step(i, unused):
        right_copy(i).wait()
        at = pl.ds(i * BLOCK_K, BLOCK_K)
        stream = jnp.concatenate([right[at, r].reshape(BLOCK_K * width, width) for r in range(right_count)], axis=1)
        for pair in range(sectors // 2):
            product = lax.dot_general(stream, sources[pair], NT, preferred_element_type=jnp.float32)
            half[pair // 2, at, pair % 2] = product.astype(jnp.bfloat16).reshape(BLOCK_K, width, 2 * width)
        return unused

    lax.fori_loop(0, steps, one_step, 0)


def accumulate(low, high, first, pieces, slots, half, total, order):
    width = total.shape[1]
    spare = total.shape[0] - 1
    zero = jnp.zeros((width, width), jnp.bfloat16)

    def one_group(g, unused):
        places = [g * GROUP + j for j in range(GROUP)]
        members = [order[at] for at in places]
        counts = [(low <= at) & (at < high) for at in places]
        k = 0
        for piece in pieces:
            for at in range(piece.shape[0]):
                block = piece[at]
                weights = jnp.concatenate(
                    [jnp.concatenate([block, zero], axis=1), jnp.concatenate([zero, block], axis=1)], axis=0
                )
                term = lax.dot_general(
                    half[g, first + k].reshape(GROUP // 2 * width, 2 * width),
                    weights,
                    NT,
                    preferred_element_type=jnp.float32,
                )
                for j in range(GROUP):
                    p, e = j // 2, j % 2
                    slot = jnp.where(counts[j], slots[members[j], first + k], spare)
                    total[slot] += term[p * width : (p + 1) * width, e * width : (e + 1) * width]
                k += 1
        return unused

    groups = jnp.where(low < high, lax.div(high + GROUP - 1, jnp.int32(GROUP)), 0)
    lax.fori_loop(lax.div(low, jnp.int32(GROUP)), groups, one_group, 0)


def own_kernel(blocks, left_qn, slots, half, left, total, order, starts):
    left_local = left.shape[1]
    total[...] = jnp.zeros_like(total)
    arrange(left_qn, order, starts, blocks, left_local)
    for l in range(left_local):
        accumulate(starts[l], starts[l + 1], 0, [left.at[:, l]], slots, half, total, order)


def other_kernel(last, offset, left_qn, slots, slot_target, half, start, *rest):
    lefts = rest[:2]
    if last:
        outs, (total, order, starts) = rest[2:-3], rest[-3:]
    else:
        total, order, starts = rest[2:]
    shifts, left_local = lefts[0].shape[0], lefts[0].shape[2]
    operators = slots.shape[1]
    total[...] = start[...]
    arrange(left_qn, order, starts, shifts + 1, left_local)
    row = lax.axis_index("sector")
    first = lax.rem(row + offset, jnp.int32(2)) * (operators // 2)

    def one_shift(d, unused):
        for l in range(left_local):
            code = (d + 1) * left_local + l
            pieces = [left.at[d, :, l] for left in lefts]
            accumulate(starts[code], starts[code + 1], first, pieces, slots, half, total, order)
        return unused

    lax.fori_loop(0, shifts, one_shift, 0)
    if not last:
        return
    width = total.shape[1]
    line = lax.broadcasted_iota(jnp.int32, (TAIL, width), 0)
    for d, out in enumerate(outs):
        owner = lax.rem(row + d, jnp.int32(len(outs)))
        ids = jnp.zeros((TAIL, width), jnp.int32)
        for m in range(CAP):
            out[m * width : (m + 1) * width, :] = total[owner * CAP + m].astype(jnp.bfloat16)
            ids = jnp.where(line == m, slot_target[0, 0, owner * CAP + m], ids)
        out[CAP * width :, :] = ids.astype(jnp.float32).astype(jnp.bfloat16)


def assemble_kernel(rows, *rest):
    mine, theirs, out = rest[:rows], rest[rows : 2 * rows], rest[-1]
    width = out.shape[1]
    out[...] = jnp.zeros_like(out)
    for d in range(rows):
        ids = mine[d][CAP * width :, :].astype(jnp.float32)
        for m in range(CAP):
            at = pl.ds(m * width, width)
            block = mine[d][at, :].astype(jnp.float32) + theirs[d][at, :].astype(jnp.float32)
            target = jnp.max(ids[m : m + 1, :]).astype(jnp.int32)
            out[target] += block.T


def shards(sizes, psi, left_ops, right_ops, left_qn, right_qn, pair_slot, slot_target):
    rows, blocks, halves = sizes
    sectors, width = psi.shape[0], psi.shape[1]
    operators, left_local = left_ops.shape[0], left_ops.shape[1]
    slots = pair_slot.T
    smem = pl.BlockSpec(memory_space=pltpu.SMEM)
    vmem = pl.BlockSpec(memory_space=pltpu.VMEM)
    hbm = pl.BlockSpec(memory_space=pltpu.HBM)
    total_shape = (rows * CAP + 1, width, width)
    right_count = right_ops.shape[1]
    lists = [pltpu.SMEM((sectors + 1,), jnp.int32), pltpu.SMEM((blocks * left_local + 1,), jnp.int32)]
    params = pltpu.CompilerParams(vmem_limit_bytes=12 * 2**20)

    def cost(share):
        flops = int(16 * operators * sectors * width**3 * share)
        return pl.CostEstimate(flops=flops, bytes_accessed=4 * 2**20, transcendentals=0)

    first = lax.rem(lax.axis_index("sector"), 2) * (operators // 2)
    quarter = operators // 4
    swap = [(i, i ^ 1) for i in range(rows)]
    sent = [lax.dynamic_slice_in_dim(left_ops, first + i * quarter, quarter, 0) for i in range(2)]
    near = [
        [lax.ppermute(part, "blk", [((b + d) % blocks, b) for b in range(blocks)]) for d in range(1, blocks)]
        for part in sent
    ]
    half = pl.pallas_call(
        functools.partial(right_kernel, blocks, left_local),
        out_shape=jax.ShapeDtypeStruct((sectors // GROUP, operators, GROUP // 2, width, 2 * width), jnp.bfloat16),
        in_specs=[hbm] * 4,
        out_specs=vmem,
        scratch_shapes=[
            pltpu.SMEM(left_qn.shape, jnp.int32),
            pltpu.SMEM(right_qn.shape, jnp.int32),
            pltpu.VMEM(psi.shape, psi.dtype),
            pltpu.VMEM(right_ops.shape, right_ops.dtype),
            pltpu.VMEM((sectors // 2, 2 * width, right_count * width), jnp.bfloat16),
            *lists,
            pltpu.SemaphoreType.DMA((3 + operators // BLOCK_K,)),
        ],
        compiler_params=params,
        cost_estimate=cost(0.5),
        name="right_side",
    )(*(pltpu.with_memory_space_constraint(x, pltpu.HBM) for x in (left_qn, right_qn, psi, right_ops)))
    half, near = lax.optimization_barrier((half, near))
    far = [[lax.ppermute(part, "sector", swap) for part in parts] for parts in near]
    near, far = ([jnp.stack(parts) for parts in side] for side in (near, far))
    total = pl.pallas_call(
        functools.partial(own_kernel, blocks),
        out_shape=jax.ShapeDtypeStruct(total_shape, jnp.float32),
        in_specs=[smem] * 2 + [vmem] * 2,
        out_specs=vmem,
        scratch_shapes=lists,
        compiler_params=params,
        cost_estimate=cost(0.25),
        name="own_left",
    )(left_qn, slots, half, left_ops)
    common = (left_qn, slots, slot_target, half)
    total = pl.pallas_call(
        functools.partial(other_kernel, False, 0),
        out_shape=jax.ShapeDtypeStruct(total_shape, jnp.float32),
        in_specs=[smem] * 3 + [vmem] * 4,
        out_specs=vmem,
        scratch_shapes=lists,
        compiler_params=params,
        cost_estimate=cost(0.125),
        name="other_left_near",
    )(*common, total, *near)
    partial = pl.pallas_call(
        functools.partial(other_kernel, True, 1),
        out_shape=[jax.ShapeDtypeStruct((CAP * width + TAIL, width), jnp.bfloat16)] * rows,
        in_specs=[smem] * 3 + [vmem] * 4,
        out_specs=[vmem] * rows,
        scratch_shapes=[pltpu.VMEM(total_shape, jnp.float32), *lists],
        compiler_params=params,
        cost_estimate=cost(0.125),
        name="other_left_far",
    )(*common, total, *far)
    mine = [partial[0]] + [
        lax.ppermute(partial[d], "sector", [(i, (i + d) % rows) for i in range(rows)]) for d in range(1, rows)
    ]
    theirs = [lax.ppermute(block, "op", [(h, halves - 1 - h) for h in range(halves)]) for block in mine]
    return pl.pallas_call(
        functools.partial(assemble_kernel, rows),
        out_shape=jax.ShapeDtypeStruct((sectors, width, width), jnp.float32),
        in_specs=[vmem] * (2 * rows),
        out_specs=vmem,
        compiler_params=params,
        name="assemble",
    )(*mine, *theirs)


def solution(mesh):
    in_specs = (
        P(("groups", "sector", "blk"), None, None),
        P(("groups", "op"), "blk", None, None),
        P(("groups", "op"), None, None, None),
        P(("groups", "sector", "blk")),
        P(("groups", "sector", "blk")),
        P(("groups", "op"), ("sector", "blk")),
        P(("groups", "sector"), "blk", None),
    )
    out_specs = P(("groups", "sector", "blk"), None, None)
    sizes = tuple(mesh.shape[name] for name in ("sector", "blk", "op"))
    return jax.shard_map(
        functools.partial(shards, sizes), mesh=mesh, in_specs=in_specs, out_specs=out_specs, check_vma=False
    )
```

```python
import functools

import jax
import jax.numpy as jnp
from jax import lax
from jax.experimental import pallas as pl
from jax.experimental.pallas import tpu as pltpu
from jax.sharding import PartitionSpec as P

CAP = 4
GROUP = 4
SETS = 4
MOST_SLOTS = 64
BLOCK_K = 8
TAIL = 16
NT = (((1,), (1,)), ((), ()))


def arrange(left_qn, plan, blocks, left_local):
    mine = lax.axis_index("blk")
    count = left_qn.shape[0]

    def one_code(code, n):
        plan[count + 1 + code] = n
        owner = lax.rem(mine + lax.div(code, jnp.int32(left_local)), jnp.int32(blocks))
        wanted = owner * left_local + lax.rem(code, jnp.int32(left_local))

        def one_sector(s, n):
            plan[n] = s
            return n + (left_qn[s] == wanted).astype(jnp.int32)

        return lax.fori_loop(0, count, one_sector, n)

    plan[count + 1 + blocks * left_local] = lax.fori_loop(0, blocks * left_local, one_code, jnp.int32(0))


def right_kernel(
    blocks, left_local, left_qn_in, right_qn_in, psi_in, right_in, half, plan,
    left_qn, right_qn, psi, right, sources, sems,
):
    sectors, width = psi.shape[0], psi.shape[1]
    right_count = right.shape[1]
    steps = right.shape[0] // BLOCK_K
    zero = jnp.zeros((width, width), jnp.bfloat16)

    def right_copy(i):
        at = pl.ds(i * BLOCK_K, BLOCK_K)
        return pltpu.make_async_copy(right_in.at[at], right.at[at], sems.at[3 + i])

    copies = [
        pltpu.make_async_copy(left_qn_in, left_qn, sems.at[0]),
        pltpu.make_async_copy(right_qn_in, right_qn, sems.at[1]),
        pltpu.make_async_copy(psi_in, psi, sems.at[2]),
    ]
    for copy in copies:
        copy.start()
    for i in range(steps):
        right_copy(i).start()
    copies[0].wait()
    copies[1].wait()
    arrange(left_qn, plan, blocks, left_local)
    copies[2].wait()
    for pair in range(sectors // 2):
        for e in range(2):
            s = plan[2 * pair + e]
            block = psi[s]
            for r in range(right_count):
                sources[pair, e * width : (e + 1) * width, r * width : (r + 1) * width] = jnp.where(
                    right_qn[s] == r, block, zero
                )

    def one_step(i, unused):
        right_copy(i).wait()
        at = pl.ds(i * BLOCK_K, BLOCK_K)
        stream = jnp.concatenate([right[at, r].reshape(BLOCK_K * width, width) for r in range(right_count)], axis=1)
        for pair in range(sectors // 2):
            product = lax.dot_general(stream, sources[pair], NT, preferred_element_type=jnp.float32)
            half[pair // 2, at, pair % 2] = product.astype(jnp.bfloat16).reshape(BLOCK_K, width, 2 * width)
        return unused

    lax.fori_loop(0, steps, one_step, 0)


def accumulate(code, pieces, plan, slots, half, totals):
    sectors, width = slots.shape[0], totals[0].shape[1]
    spare = totals[0].shape[0] - 1
    low, high = plan[sectors + 1 + code], plan[sectors + 2 + code]
    zero = jnp.zeros((width, width), jnp.bfloat16)

    def one_group(g, unused):
        places = [g * GROUP + j for j in range(GROUP)]
        members = [plan[at] for at in places]
        counts = [(low <= at) & (at < high) for at in places]
        for first, left in pieces:
            for i in range(left.shape[0]):
                k = first + i
                block = left[i]
                weights = jnp.concatenate(
                    [jnp.concatenate([block, zero], axis=1), jnp.concatenate([zero, block], axis=1)], axis=0
                )
                term = lax.dot_general(
                    half[g, k].reshape(GROUP // 2 * width, 2 * width),
                    weights,
                    NT,
                    preferred_element_type=jnp.float32,
                )
                for j in range(GROUP):
                    p, e = j // 2, j % 2
                    slot = jnp.where(counts[j], slots[members[j], k], spare)
                    totals[j % len(totals)][slot] += term[p * width : (p + 1) * width, e * width : (e + 1) * width]
        return unused

    groups = jnp.where(low < high, lax.div(high + GROUP - 1, jnp.int32(GROUP)), 0)
    lax.fori_loop(lax.div(low, jnp.int32(GROUP)), groups, one_group, 0)


def own_kernel(plan, slots, half, left, *totals):
    for total in totals:
        total[...] = jnp.zeros_like(total)
    for l in range(left.shape[1]):
        accumulate(l, [(0, left.at[:, l])], plan, slots, half, totals)


def other_kernel(rows, sets, plan, slots, half, swapped, direct, middle, *rest):
    totals, (keep, give) = rest[sets : 2 * sets], rest[2 * sets :]
    shifts, quarter, left_local = swapped.shape[0], swapped.shape[1], swapped.shape[2]
    row, side = lax.axis_index("sector"), lax.axis_index("op")
    operators, width = slots.shape[1], totals[0].shape[1]
    odd = lax.rem(row, jnp.int32(2))
    near = odd * (operators - quarter)
    far = (1 - odd) * (operators - quarter)

    def one_shift(d, unused):
        for l in range(left_local):
            pieces = [
                (near, direct.at[d, :, l]), (quarter, middle.at[d, :, l]), (far, swapped.at[d, :, l])
            ]
            accumulate((d + 1) * left_local + l, pieces, plan, slots, half, totals)
        return unused

    lax.fori_loop(0, shifts, one_shift, 0)
    part = CAP // 2
    for owner in range(rows):
        for m in range(part):
            at = owner * CAP + side * part + m
            keep[owner * part + m] = sum(total[at] for total in totals)
            at = owner * CAP + (1 - side) * part + m
            give[owner * part + m] = sum(total[at] for total in totals).astype(jnp.bfloat16)


def combine_kernel(slot_target, keep, taken, *outs):
    part, width = CAP // 2, keep.shape[1]
    row, side = lax.axis_index("sector"), lax.axis_index("op")
    line = lax.broadcasted_iota(jnp.int32, (TAIL, width), 0)
    for d, out in enumerate(outs):
        owner = lax.rem(row + d, jnp.int32(len(outs)))
        ids = jnp.zeros((TAIL, width), jnp.int32)
        for m in range(part):
            block = keep[owner * part + m] + taken[owner * part + m].astype(jnp.float32)
            out[m * width : (m + 1) * width, :] = block.astype(jnp.bfloat16)
            ids = jnp.where(line == m, slot_target[0, 0, owner * CAP + side * part + m], ids)
        out[part * width :, :] = ids.astype(jnp.float32).astype(jnp.bfloat16)


def assemble_kernel(rows, *rest):
    mine, theirs, out = rest[:rows], rest[rows : 2 * rows], rest[-1]
    part, width = CAP // 2, out.shape[1]
    side = lax.axis_index("op")
    out[...] = jnp.zeros_like(out)
    for d in range(rows):
        for h in range(2):
            ids = jnp.where(side == h, mine[d][part * width :, :], theirs[d][part * width :, :]).astype(jnp.float32)
            for m in range(part):
                at = pl.ds(m * width, width)
                block = jnp.where(side == h, mine[d][at, :], theirs[d][at, :]).astype(jnp.float32)
                target = jnp.max(ids[m : m + 1, :]).astype(jnp.int32)
                out[target] += block.T


def shards(sizes, psi, left_ops, right_ops, left_qn, right_qn, pair_slot, slot_target):
    rows, blocks, halves = sizes
    sectors, width = psi.shape[0], psi.shape[1]
    operators, left_local = left_ops.shape[0], left_ops.shape[1]
    slots = pair_slot.T
    smem = pl.BlockSpec(memory_space=pltpu.SMEM)
    vmem = pl.BlockSpec(memory_space=pltpu.VMEM)
    hbm = pl.BlockSpec(memory_space=pltpu.HBM)
    sets = max(1, min(SETS, MOST_SLOTS // (rows * CAP)))
    total_shape = (rows * CAP + 1, width, width)
    right_count = right_ops.shape[1]
    params = pltpu.CompilerParams(vmem_limit_bytes=12 * 2**20)

    def cost(share):
        flops = int(16 * operators * sectors * width**3 * share)
        return pl.CostEstimate(flops=flops, bytes_accessed=4 * 2**20, transcendentals=0)

    odd = lax.rem(lax.axis_index("sector"), 2)
    quarter = operators // 4
    swap = [(i, i ^ 1) for i in range(rows)]

    def over_blocks(part):
        return [lax.ppermute(part, "blk", [((b + d) % blocks, b) for b in range(blocks)]) for d in range(1, blocks)]

    direct = over_blocks(lax.dynamic_slice_in_dim(left_ops, odd * (operators - quarter), quarter, 0))
    middle = over_blocks(left_ops[quarter : operators - quarter])

    half, plan = pl.pallas_call(
        functools.partial(right_kernel, blocks, left_local),
        out_shape=[
            jax.ShapeDtypeStruct((sectors // GROUP, operators, GROUP // 2, width, 2 * width), jnp.bfloat16),
            jax.ShapeDtypeStruct((sectors + 2 + blocks * left_local,), jnp.int32),
        ],
        in_specs=[hbm] * 4,
        out_specs=[vmem, smem],
        scratch_shapes=[
            pltpu.SMEM(left_qn.shape, jnp.int32),
            pltpu.SMEM(right_qn.shape, jnp.int32),
            pltpu.VMEM(psi.shape, psi.dtype),
            pltpu.VMEM(right_ops.shape, right_ops.dtype),
            pltpu.VMEM((sectors // 2, 2 * width, right_count * width), jnp.bfloat16),
            pltpu.SemaphoreType.DMA((3 + operators // BLOCK_K,)),
        ],
        compiler_params=params,
        cost_estimate=cost(0.5),
        name="right_side",
    )(*(pltpu.with_memory_space_constraint(x, pltpu.HBM) for x in (left_qn, right_qn, psi, right_ops)))
    half, direct = lax.optimization_barrier((half, direct))
    swapped = [lax.ppermute(part, "sector", swap) for part in direct]
    totals = pl.pallas_call(
        own_kernel,
        out_shape=[jax.ShapeDtypeStruct(total_shape, jnp.float32)] * sets,
        in_specs=[smem] * 2 + [vmem] * 2,
        out_specs=[vmem] * sets,
        compiler_params=params,
        cost_estimate=cost(0.25),
        name="own_left",
    )(plan, slots, half, left_ops)
    results = pl.pallas_call(
        functools.partial(other_kernel, rows, sets),
        out_shape=[jax.ShapeDtypeStruct(total_shape, jnp.float32)] * sets
        + [jax.ShapeDtypeStruct((rows * CAP // 2, width, width), kind) for kind in (jnp.float32, jnp.bfloat16)],
        in_specs=[smem] * 2 + [vmem] * (4 + sets),
        out_specs=[vmem] * (sets + 2),
        input_output_aliases={6 + j: j for j in range(sets)},
        compiler_params=params,
        cost_estimate=cost(0.25),
        name="other_left",
    )(plan, slots, half, jnp.stack(swapped), jnp.stack(direct), jnp.stack(middle), *totals)
    keep, give = results[sets:]

    def over_cores(block):
        return lax.ppermute(block, "op", [(h, halves - 1 - h) for h in range(halves)])

    partial = pl.pallas_call(
        combine_kernel,
        out_shape=[jax.ShapeDtypeStruct((CAP // 2 * width + TAIL, width), jnp.bfloat16)] * rows,
        in_specs=[smem] + [vmem] * 2,
        out_specs=[vmem] * rows,
        compiler_params=params,
        name="combine",
    )(slot_target, keep, over_cores(give))
    mine = [partial[0]] + [
        lax.ppermute(partial[d], "sector", [(i, (i + d) % rows) for i in range(rows)]) for d in range(1, rows)
    ]
    theirs = [over_cores(block) for block in mine]
    return pl.pallas_call(
        functools.partial(assemble_kernel, rows),
        out_shape=jax.ShapeDtypeStruct((sectors, width, width), jnp.float32),
        in_specs=[vmem] * (2 * rows),
        out_specs=vmem,
        compiler_params=params,
        name="assemble",
    )(*mine, *theirs)


def solution(mesh):
    in_specs = (
        P(("groups", "sector", "blk"), None, None),
        P(("groups", "op"), "blk", None, None),
        P(("groups", "op"), None, None, None),
        P(("groups", "sector", "blk")),
        P(("groups", "sector", "blk")),
        P(("groups", "op"), ("sector", "blk")),
        P(("groups", "sector"), "blk", None),
    )
    out_specs = P(("groups", "sector", "blk"), None, None)
    sizes = tuple(mesh.shape[name] for name in ("sector", "blk", "op"))
    return jax.shard_map(
        functools.partial(shards, sizes), mesh=mesh, in_specs=in_specs, out_specs=out_specs, check_vma=False
    )
```

```python
import functools

import jax
import jax.numpy as jnp
from jax import lax
from jax.experimental import pallas as pl
from jax.experimental.pallas import tpu as pltpu
from jax.sharding import PartitionSpec as P

CAP = 4
GROUP = 4
SETS = 2
MOST_SLOTS = 64
BLOCK_K = 8
TAIL = 16
NT = (((1,), (1,)), ((), ()))


def arrange(left_qn, plan, blocks, left_local):
    mine = lax.axis_index("blk")
    count = left_qn.shape[0]

    def one_code(code, n):
        plan[count + 1 + code] = n
        owner = lax.rem(mine + lax.div(code, jnp.int32(left_local)), jnp.int32(blocks))
        wanted = owner * left_local + lax.rem(code, jnp.int32(left_local))

        def one_sector(s, n):
            plan[n] = s
            return n + (left_qn[s] == wanted).astype(jnp.int32)

        return lax.fori_loop(0, count, one_sector, n)

    plan[count + 1 + blocks * left_local] = lax.fori_loop(0, blocks * left_local, one_code, jnp.int32(0))


def cut_kernel(left, direct, middle, sems):
    quarter, count = direct.shape[0], middle.shape[0]
    first = lax.rem(lax.axis_index("sector"), jnp.int32(2)) * (left.shape[0] - quarter)
    copies = [
        pltpu.make_async_copy(left.at[pl.ds(first, quarter)], direct, sems.at[0]),
        pltpu.make_async_copy(left.at[pl.ds(quarter, count)], middle, sems.at[1]),
    ]
    for copy in copies:
        copy.start()
    for copy in copies:
        copy.wait()


def right_kernel(
    blocks, left_local, left_qn_in, right_qn_in, psi_in, right_in, half, plan,
    left_qn, right_qn, psi, right, sources, sems,
):
    sectors, width = psi.shape[0], psi.shape[1]
    right_count = right.shape[1]
    steps = right.shape[0] // BLOCK_K
    zero = jnp.zeros((width, width), jnp.bfloat16)

    def right_copy(i):
        at = pl.ds(i * BLOCK_K, BLOCK_K)
        return pltpu.make_async_copy(right_in.at[at], right.at[at], sems.at[3 + i])

    copies = [
        pltpu.make_async_copy(left_qn_in, left_qn, sems.at[0]),
        pltpu.make_async_copy(right_qn_in, right_qn, sems.at[1]),
        pltpu.make_async_copy(psi_in, psi, sems.at[2]),
    ]
    for copy in copies:
        copy.start()
    for i in range(steps):
        right_copy(i).start()
    copies[0].wait()
    copies[1].wait()
    arrange(left_qn, plan, blocks, left_local)
    copies[2].wait()
    for pair in range(sectors // 2):
        for e in range(2):
            s = plan[2 * pair + e]
            block = psi[s]
            for r in range(right_count):
                sources[pair, e * width : (e + 1) * width, r * width : (r + 1) * width] = jnp.where(
                    right_qn[s] == r, block, zero
                )

    def one_step(i, unused):
        right_copy(i).wait()
        at = pl.ds(i * BLOCK_K, BLOCK_K)
        stream = jnp.concatenate([right[at, r].reshape(BLOCK_K * width, width) for r in range(right_count)], axis=1)
        for pair in range(sectors // 2):
            product = lax.dot_general(stream, sources[pair], NT, preferred_element_type=jnp.float32)
            half[pair // 2, at, pair % 2] = product.astype(jnp.bfloat16).reshape(BLOCK_K, width, 2 * width)
        return unused

    lax.fori_loop(0, steps, one_step, 0)


def accumulate(code, pieces, plan, slots, half, totals):
    sectors, width = slots.shape[0], totals[0].shape[1]
    spare = totals[0].shape[0] - 1
    low, high = plan[sectors + 1 + code], plan[sectors + 2 + code]
    zero = jnp.zeros((width, width), jnp.bfloat16)

    def one_group(g, unused):
        places = [g * GROUP + j for j in range(GROUP)]
        members = [plan[at] for at in places]
        counts = [(low <= at) & (at < high) for at in places]
        for first, left in pieces:
            for i in range(left.shape[0]):
                k = first + i
                block = left[i]
                weights = jnp.concatenate(
                    [jnp.concatenate([block, zero], axis=1), jnp.concatenate([zero, block], axis=1)], axis=0
                )
                term = lax.dot_general(
                    half[g, k].reshape(GROUP // 2 * width, 2 * width),
                    weights,
                    NT,
                    preferred_element_type=jnp.float32,
                )
                for j in range(GROUP):
                    p, e = j // 2, j % 2
                    slot = jnp.where(counts[j], slots[members[j], k], spare)
                    totals[j % len(totals)][slot] += term[p * width : (p + 1) * width, e * width : (e + 1) * width]
        return unused

    groups = jnp.where(low < high, lax.div(high + GROUP - 1, jnp.int32(GROUP)), 0)
    lax.fori_loop(lax.div(low, jnp.int32(GROUP)), groups, one_group, 0)


def own_kernel(plan, slots, half, left, *totals):
    for total in totals:
        total[...] = jnp.zeros_like(total)
    for l in range(left.shape[1]):
        accumulate(l, [(0, left.at[:, l])], plan, slots, half, totals)


def other_kernel(rows, sets, plan, slots, half, swapped, direct, middle, *rest):
    totals, (keep, give) = rest[sets : 2 * sets], rest[2 * sets :]
    shifts, quarter, left_local = swapped.shape[0], swapped.shape[1], swapped.shape[2]
    row, side = lax.axis_index("sector"), lax.axis_index("op")
    operators, width = slots.shape[1], totals[0].shape[1]
    odd = lax.rem(row, jnp.int32(2))
    near = odd * (operators - quarter)
    far = (1 - odd) * (operators - quarter)

    def one_shift(d, unused):
        for l in range(left_local):
            pieces = [
                (near, direct.at[d, :, l]), (quarter, middle.at[d, :, l]), (far, swapped.at[d, :, l])
            ]
            accumulate((d + 1) * left_local + l, pieces, plan, slots, half, totals)
        return unused

    lax.fori_loop(0, shifts, one_shift, 0)
    part = CAP // 2
    for owner in range(rows):
        for m in range(part):
            at = owner * CAP + side * part + m
            keep[owner * part + m] = sum(total[at] for total in totals)
            at = owner * CAP + (1 - side) * part + m
            give[owner * part + m] = sum(total[at] for total in totals).astype(jnp.bfloat16)


def combine_kernel(slot_target, keep, taken, *outs):
    part, width = CAP // 2, keep.shape[1]
    row, side = lax.axis_index("sector"), lax.axis_index("op")
    line = lax.broadcasted_iota(jnp.int32, (TAIL, width), 0)
    for d, out in enumerate(outs):
        owner = lax.bitwise_xor(row, jnp.int32(d))
        ids = jnp.zeros((TAIL, width), jnp.int32)
        for m in range(part):
            block = keep[owner * part + m] + taken[owner * part + m].astype(jnp.float32)
            out[m * width : (m + 1) * width, :] = block.astype(jnp.bfloat16)
            ids = jnp.where(line == m, slot_target[0, 0, owner * CAP + side * part + m], ids)
        out[part * width :, :] = ids.astype(jnp.float32).astype(jnp.bfloat16)


def assemble_kernel(rows, *rest):
    mine, theirs, out = rest[:rows], rest[rows : 2 * rows], rest[-1]
    part, width = CAP // 2, out.shape[1]
    side = lax.axis_index("op")
    out[...] = jnp.zeros_like(out)
    for d in range(rows):
        for h in range(2):
            ids = jnp.where(side == h, mine[d][part * width :, :], theirs[d][part * width :, :]).astype(jnp.float32)
            for m in range(part):
                at = pl.ds(m * width, width)
                block = jnp.where(side == h, mine[d][at, :], theirs[d][at, :]).astype(jnp.float32)
                target = jnp.max(ids[m : m + 1, :]).astype(jnp.int32)
                out[target] += block.T


def shards(sizes, psi, left_ops, right_ops, left_qn, right_qn, pair_slot, slot_target):
    rows, blocks, halves = sizes
    sectors, width = psi.shape[0], psi.shape[1]
    operators, left_local = left_ops.shape[0], left_ops.shape[1]
    slots = pair_slot.T
    smem = pl.BlockSpec(memory_space=pltpu.SMEM)
    vmem = pl.BlockSpec(memory_space=pltpu.VMEM)
    hbm = pl.BlockSpec(memory_space=pltpu.HBM)
    sets = max(1, min(SETS, MOST_SLOTS // (rows * CAP)))
    total_shape = (rows * CAP + 1, width, width)
    right_count = right_ops.shape[1]
    params = pltpu.CompilerParams(vmem_limit_bytes=12 * 2**20)

    def cost(share):
        flops = int(16 * operators * sectors * width**3 * share)
        return pl.CostEstimate(flops=flops, bytes_accessed=4 * 2**20, transcendentals=0)

    assert rows & (rows - 1) == 0
    quarter = operators // 4
    swap = [(i, i ^ 1) for i in range(rows)]

    def over_blocks(part):
        return [lax.ppermute(part, "blk", [((b + d) % blocks, b) for b in range(blocks)]) for d in range(1, blocks)]

    direct, middle = pl.pallas_call(
        cut_kernel,
        out_shape=[
            jax.ShapeDtypeStruct((count, *left_ops.shape[1:]), left_ops.dtype)
            for count in (quarter, operators - 2 * quarter)
        ],
        in_specs=[hbm],
        out_specs=[vmem] * 2,
        scratch_shapes=[pltpu.SemaphoreType.DMA((2,))],
        compiler_params=params,
        name="cut_left",
    )(pltpu.with_memory_space_constraint(left_ops, pltpu.HBM))
    direct, middle = over_blocks(direct), over_blocks(middle)

    half, plan = pl.pallas_call(
        functools.partial(right_kernel, blocks, left_local),
        out_shape=[
            jax.ShapeDtypeStruct((sectors // GROUP, operators, GROUP // 2, width, 2 * width), jnp.bfloat16),
            jax.ShapeDtypeStruct((sectors + 2 + blocks * left_local,), jnp.int32),
        ],
        in_specs=[hbm] * 4,
        out_specs=[vmem, smem],
        scratch_shapes=[
            pltpu.SMEM(left_qn.shape, jnp.int32),
            pltpu.SMEM(right_qn.shape, jnp.int32),
            pltpu.VMEM(psi.shape, psi.dtype),
            pltpu.VMEM(right_ops.shape, right_ops.dtype),
            pltpu.VMEM((sectors // 2, 2 * width, right_count * width), jnp.bfloat16),
            pltpu.SemaphoreType.DMA((3 + operators // BLOCK_K,)),
        ],
        compiler_params=params,
        cost_estimate=cost(0.5),
        name="right_side",
    )(*(pltpu.with_memory_space_constraint(x, pltpu.HBM) for x in (left_qn, right_qn, psi, right_ops)))
    half, direct = lax.optimization_barrier((half, direct))
    swapped = [lax.ppermute(part, "sector", swap) for part in direct]
    totals = pl.pallas_call(
        own_kernel,
        out_shape=[jax.ShapeDtypeStruct(total_shape, jnp.float32)] * sets,
        in_specs=[smem] * 2 + [vmem] * 2,
        out_specs=[vmem] * sets,
        compiler_params=params,
        cost_estimate=cost(0.25),
        name="own_left",
    )(plan, slots, half, left_ops)
    results = pl.pallas_call(
        functools.partial(other_kernel, rows, sets),
        out_shape=[jax.ShapeDtypeStruct(total_shape, jnp.float32)] * sets
        + [jax.ShapeDtypeStruct((rows * CAP // 2, width, width), kind) for kind in (jnp.float32, jnp.bfloat16)],
        in_specs=[smem] * 2 + [vmem] * (4 + sets),
        out_specs=[vmem] * (sets + 2),
        input_output_aliases={6 + j: j for j in range(sets)},
        compiler_params=params,
        cost_estimate=cost(0.25),
        name="other_left",
    )(plan, slots, half, jnp.stack(swapped), jnp.stack(direct), jnp.stack(middle), *totals)
    keep, give = results[sets:]

    def over_cores(block):
        return lax.ppermute(block, "op", [(h, halves - 1 - h) for h in range(halves)])

    partial = pl.pallas_call(
        combine_kernel,
        out_shape=[jax.ShapeDtypeStruct((CAP // 2 * width + TAIL, width), jnp.bfloat16)] * rows,
        in_specs=[smem] + [vmem] * 2,
        out_specs=[vmem] * rows,
        compiler_params=params,
        name="combine",
    )(slot_target, keep, over_cores(give))
    crossed = {
        d: lax.ppermute(partial[d], "sector", [(i, i ^ d) for i in range(rows)]) for d in reversed(range(1, rows))
    }
    mine = [partial[0]] + [crossed[d] for d in range(1, rows)]
    theirs = [over_cores(block) for block in mine]
    return pl.pallas_call(
        functools.partial(assemble_kernel, rows),
        out_shape=jax.ShapeDtypeStruct((sectors, width, width), jnp.float32),
        in_specs=[vmem] * (2 * rows),
        out_specs=vmem,
        compiler_params=params,
        name="assemble",
    )(*mine, *theirs)


def solution(mesh):
    in_specs = (
        P(("groups", "sector", "blk"), None, None),
        P(("groups", "op"), "blk", None, None),
        P(("groups", "op"), None, None, None),
        P(("groups", "sector", "blk")),
        P(("groups", "sector", "blk")),
        P(("groups", "op"), ("sector", "blk")),
        P(("groups", "sector"), "blk", None),
    )
    out_specs = P(("groups", "sector", "blk"), None, None)
    sizes = tuple(mesh.shape[name] for name in ("sector", "blk", "op"))
    return jax.shard_map(
        functools.partial(shards, sizes), mesh=mesh, in_specs=in_specs, out_specs=out_specs, check_vma=False
    )
```

```python
import functools

import jax
import jax.numpy as jnp
from jax import lax
from jax.experimental import pallas as pl
from jax.experimental.pallas import tpu as pltpu
from jax.sharding import PartitionSpec as P

CAP = 4
GROUP = 4
SETS = 4
MOST_SLOTS = 64
BLOCK_K = 8
TAIL = 16
NT = (((1,), (1,)), ((), ()))


def arrange(left_qn, right_qn, plan, blocks, left_local):
    mine = lax.axis_index("blk")
    count = left_qn.shape[0]

    def one_code(code, n):
        plan[2 * count + 2 + code] = n
        owner = lax.rem(mine + lax.div(code, jnp.int32(left_local)), jnp.int32(blocks))
        wanted = owner * left_local + lax.rem(code, jnp.int32(left_local))

        def one_sector(s, n):
            plan[n] = s
            plan[count + 1 + n] = right_qn[s]
            return n + (left_qn[s] == wanted).astype(jnp.int32)

        return lax.fori_loop(0, count, one_sector, n)

    plan[2 * count + 2 + blocks * left_local] = lax.fori_loop(0, blocks * left_local, one_code, jnp.int32(0))


def first_kernel(blocks, left_qn_in, right_qn_in, psi_in, right_in, left, direct, middle, psi, head, plan, *rest):
    totals, (left_qn, right_qn, sems) = rest[:-3], rest[-3:]
    relayed, count = direct.shape[0], middle.shape[0]
    first = lax.rem(lax.axis_index("sector"), jnp.int32(2)) * (left.shape[0] - relayed)
    pairs = [
        (left_qn_in, left_qn),
        (right_qn_in, right_qn),
        (left.at[pl.ds(first, relayed)], direct),
        (left.at[pl.ds(relayed, count)], middle),
        (psi_in, psi),
        (right_in.at[pl.ds(0, head.shape[0])], head),
    ]
    copies = [pltpu.make_async_copy(src, dst, sems.at[i]) for i, (src, dst) in enumerate(pairs)]
    for copy in copies:
        copy.start()
    for total in totals:
        total[...] = jnp.zeros_like(total)
    copies[0].wait()
    copies[1].wait()
    arrange(left_qn, right_qn, plan, blocks, left.shape[1])
    for copy in copies[2:]:
        copy.wait()


def right_kernel(plan, psi, head, right_in, half, right, sources, sems):
    sectors, width = psi.shape[0], psi.shape[1]
    right_count = right.shape[1]
    steps = right_in.shape[0] // BLOCK_K
    zero = jnp.zeros((width, width), jnp.bfloat16)

    def right_copy(i):
        src = right_in.at[pl.ds(i * BLOCK_K, BLOCK_K)]
        dst = right.at[pl.ds((i - 1) * BLOCK_K, BLOCK_K)]
        return pltpu.make_async_copy(src, dst, sems.at[i - 1])

    for i in range(1, steps):
        right_copy(i).start()
    for pair in range(sectors // 2):
        for e in range(2):
            block = psi[plan[2 * pair + e]]
            quantum = plan[sectors + 1 + 2 * pair + e]
            for r in range(right_count):
                sources[pair, e * width : (e + 1) * width, r * width : (r + 1) * width] = jnp.where(
                    quantum == r, block, zero
                )

    def products(blocks, first):
        stream = jnp.concatenate([block.reshape(BLOCK_K * width, width) for block in blocks], axis=1)
        for pair in range(sectors // 2):
            product = lax.dot_general(stream, sources[pair], NT, preferred_element_type=jnp.float32)
            half[pair // 2, pl.ds(first, BLOCK_K), pair % 2] = product.astype(jnp.bfloat16).reshape(
                BLOCK_K, width, 2 * width
            )

    products([head[:, r] for r in range(right_count)], 0)

    def one_step(i, unused):
        right_copy(i).wait()
        at = pl.ds((i - 1) * BLOCK_K, BLOCK_K)
        products([right[at, r] for r in range(right_count)], i * BLOCK_K)
        return unused

    lax.fori_loop(1, steps, one_step, 0)


def accumulate(code, pieces, plan, slots, half, totals):
    sectors, width = slots.shape[0], totals[0].shape[1]
    spare = totals[0].shape[0] - 1
    low, high = plan[2 * sectors + 2 + code], plan[2 * sectors + 3 + code]
    zero = jnp.zeros((width, width), jnp.bfloat16)

    def terms(place, count, rows):
        members = [plan[place + j] for j in range(count)]
        counts = [(low <= place + j) & (place + j < high) for j in range(count)]
        for first, left in pieces:
            for i in range(left.shape[0]):
                k = first + i
                block = left[i]
                weights = jnp.concatenate(
                    [jnp.concatenate([block, zero], axis=1), jnp.concatenate([zero, block], axis=1)], axis=0
                )
                term = lax.dot_general(rows(k), weights, NT, preferred_element_type=jnp.float32)
                for j in range(count):
                    p, e = j // 2, j % 2
                    slot = jnp.where(counts[j], slots[members[j], k], spare)
                    totals[j % len(totals)][slot] += term[
                        p * width : (p + 1) * width, e * width : (e + 1) * width
                    ]

    def one_group(g, unused):
        terms(g * GROUP, GROUP, lambda k: half[g, k].reshape(GROUP // 2 * width, 2 * width))
        return unused

    def one_pair(i, unused):
        pair = jnp.where((odd_start == 1) & (i == 0), start, stop - 1)
        terms(pair * 2, 2, lambda k: half[lax.div(pair, 2), k, lax.rem(pair, 2)])
        return unused

    some = low < high
    start = jnp.where(some, lax.div(low, 2), 0)
    stop = jnp.where(some, lax.div(high + 1, 2), 0)
    odd_start, odd_stop = lax.rem(start, 2), lax.rem(stop, 2)
    lax.fori_loop(lax.div(start + 1, 2), lax.div(stop, 2), one_group, 0)
    lax.fori_loop(0, odd_start + odd_stop, one_pair, 0)


def own_kernel(plan, slots, half, left, *rest):
    totals = rest[len(rest) // 2 :]
    for l in range(left.shape[1]):
        accumulate(l, [(0, left.at[:, l])], plan, slots, half, totals)


def other_kernel(rows, sets, plan, slots, half, swapped, direct, middle, *rest):
    totals, (keep, give) = rest[sets : 2 * sets], rest[2 * sets :]
    shifts, relayed, left_local = swapped.shape[0], swapped.shape[1], swapped.shape[2]
    row, side = lax.axis_index("sector"), lax.axis_index("op")
    operators, width = slots.shape[1], totals[0].shape[1]
    odd = lax.rem(row, jnp.int32(2))
    near = odd * (operators - relayed)
    far = (1 - odd) * (operators - relayed)

    def one_shift(d, unused):
        for l in range(left_local):
            pieces = [
                (near, direct.at[d, :, l]), (relayed, middle.at[d, :, l]), (far, swapped.at[d, :, l])
            ]
            accumulate((d + 1) * left_local + l, pieces, plan, slots, half, totals)
        return unused

    lax.fori_loop(0, shifts, one_shift, 0)
    part = CAP // 2
    for owner in range(rows):
        for m in range(part):
            at = owner * CAP + side * part + m
            keep[owner * part + m] = sum(total[at] for total in totals)
            at = owner * CAP + (1 - side) * part + m
            give[owner * part + m] = sum(total[at] for total in totals).astype(jnp.bfloat16)


def combine_kernel(slot_target, keep, taken, *outs):
    part, width = CAP // 2, keep.shape[1]
    row, side = lax.axis_index("sector"), lax.axis_index("op")
    line = lax.broadcasted_iota(jnp.int32, (TAIL, width), 0)
    for d, out in enumerate(outs):
        owner = lax.rem(row + d, jnp.int32(len(outs)))
        ids = jnp.zeros((TAIL, width), jnp.int32)
        for m in range(part):
            block = keep[owner * part + m] + taken[owner * part + m].astype(jnp.float32)
            out[m * width : (m + 1) * width, :] = block.astype(jnp.bfloat16)
            ids = jnp.where(line == m, slot_target[0, 0, owner * CAP + side * part + m], ids)
        out[part * width :, :] = ids.astype(jnp.float32).astype(jnp.bfloat16)


def assemble_kernel(rows, *rest):
    mine, theirs, out = rest[:rows], rest[rows : 2 * rows], rest[-1]
    part, width = CAP // 2, out.shape[1]
    side = lax.axis_index("op")
    out[...] = jnp.zeros_like(out)
    for d in range(rows):
        for h in range(2):
            ids = jnp.where(side == h, mine[d][part * width :, :], theirs[d][part * width :, :]).astype(jnp.float32)
            for m in range(part):
                at = pl.ds(m * width, width)
                block = jnp.where(side == h, mine[d][at, :], theirs[d][at, :]).astype(jnp.float32)
                target = jnp.max(ids[m : m + 1, :]).astype(jnp.int32)
                out[target] += block.T


def shards(sizes, psi, left_ops, right_ops, left_qn, right_qn, pair_slot, slot_target):
    rows, blocks, halves = sizes
    sectors, width = psi.shape[0], psi.shape[1]
    operators, left_local = left_ops.shape[0], left_ops.shape[1]
    slots = pair_slot.T
    smem = pl.BlockSpec(memory_space=pltpu.SMEM)
    vmem = pl.BlockSpec(memory_space=pltpu.VMEM)
    hbm = pl.BlockSpec(memory_space=pltpu.HBM)
    sets = max(1, min(SETS, MOST_SLOTS // (rows * CAP)))
    total_shape = (rows * CAP + 1, width, width)
    right_count = right_ops.shape[1]
    params = pltpu.CompilerParams(vmem_limit_bytes=8 * 2**20)

    def cost(share):
        flops = int(16 * operators * sectors * width**3 * share)
        return pl.CostEstimate(flops=flops, bytes_accessed=4 * 2**20, transcendentals=0)

    assert rows % 2 == 0
    relayed = operators * 5 // 16
    swap = [(i, i ^ 1) for i in range(rows)]

    def over_blocks(part):
        return [lax.ppermute(part, "blk", [((b + d) % blocks, b) for b in range(blocks)]) for d in range(1, blocks)]

    direct, middle, psi_near, head, plan, *totals = pl.pallas_call(
        functools.partial(first_kernel, blocks),
        out_shape=[
            jax.ShapeDtypeStruct((relayed, *left_ops.shape[1:]), left_ops.dtype),
            jax.ShapeDtypeStruct((operators - 2 * relayed, *left_ops.shape[1:]), left_ops.dtype),
            jax.ShapeDtypeStruct(psi.shape, psi.dtype),
            jax.ShapeDtypeStruct((BLOCK_K, *right_ops.shape[1:]), right_ops.dtype),
            jax.ShapeDtypeStruct((2 * sectors + 3 + blocks * left_local,), jnp.int32),
            *[jax.ShapeDtypeStruct(total_shape, jnp.float32)] * sets,
        ],
        in_specs=[hbm] * 5,
        out_specs=[vmem] * 4 + [smem] + [vmem] * sets,
        scratch_shapes=[
            pltpu.SMEM(left_qn.shape, jnp.int32),
            pltpu.SMEM(right_qn.shape, jnp.int32),
            pltpu.SemaphoreType.DMA((6,)),
        ],
        compiler_params=params,
        name="first_loads",
    )(*(pltpu.with_memory_space_constraint(x, pltpu.HBM) for x in (left_qn, right_qn, psi, right_ops, left_ops)))
    direct, middle = over_blocks(direct), over_blocks(middle)

    half = pl.pallas_call(
        right_kernel,
        out_shape=jax.ShapeDtypeStruct((sectors // GROUP, operators, GROUP // 2, width, 2 * width), jnp.bfloat16),
        in_specs=[smem, vmem, vmem, hbm],
        out_specs=vmem,
        scratch_shapes=[
            pltpu.VMEM((operators - BLOCK_K, *right_ops.shape[1:]), right_ops.dtype),
            pltpu.VMEM((sectors // 2, 2 * width, right_count * width), jnp.bfloat16),
            pltpu.SemaphoreType.DMA((operators // BLOCK_K - 1,)),
        ],
        compiler_params=params,
        cost_estimate=cost(0.5),
        name="right_side",
    )(plan, psi_near, head, pltpu.with_memory_space_constraint(right_ops, pltpu.HBM))
    half, direct = lax.optimization_barrier((half, direct))
    swapped = [lax.ppermute(part, "sector", swap) for part in direct]
    totals = pl.pallas_call(
        own_kernel,
        out_shape=[jax.ShapeDtypeStruct(total_shape, jnp.float32)] * sets,
        in_specs=[smem] * 2 + [vmem] * (2 + sets),
        out_specs=[vmem] * sets,
        input_output_aliases={4 + j: j for j in range(sets)},
        compiler_params=params,
        cost_estimate=cost(0.25),
        name="own_left",
    )(plan, slots, half, left_ops, *totals)
    results = pl.pallas_call(
        functools.partial(other_kernel, rows, sets),
        out_shape=[jax.ShapeDtypeStruct(total_shape, jnp.float32)] * sets
        + [jax.ShapeDtypeStruct((rows * CAP // 2, width, width), kind) for kind in (jnp.float32, jnp.bfloat16)],
        in_specs=[smem] * 2 + [vmem] * (4 + sets),
        out_specs=[vmem] * (sets + 2),
        input_output_aliases={6 + j: j for j in range(sets)},
        compiler_params=params,
        cost_estimate=cost(0.25),
        name="other_left",
    )(plan, slots, half, jnp.stack(swapped), jnp.stack(direct), jnp.stack(middle), *totals)
    keep, give = results[sets:]

    def over_cores(block):
        return lax.ppermute(block, "op", [(h, halves - 1 - h) for h in range(halves)])

    partial = pl.pallas_call(
        combine_kernel,
        out_shape=[jax.ShapeDtypeStruct((CAP // 2 * width + TAIL, width), jnp.bfloat16)] * rows,
        in_specs=[smem] + [vmem] * 2,
        out_specs=[vmem] * rows,
        compiler_params=params,
        name="combine",
    )(slot_target, keep, over_cores(give))
    crossed = {
        d: lax.ppermute(partial[d], "sector", [(i, (i + d) % rows) for i in range(rows)]) for d in range(1, rows)
    }
    mine = [partial[0]] + [crossed[d] for d in range(1, rows)]
    theirs = [over_cores(block) for block in mine]
    return pl.pallas_call(
        functools.partial(assemble_kernel, rows),
        out_shape=jax.ShapeDtypeStruct((sectors, width, width), jnp.float32),
        in_specs=[vmem] * (2 * rows),
        out_specs=vmem,
        compiler_params=params,
        name="assemble",
    )(*mine, *theirs)


def solution(mesh):
    in_specs = (
        P(("groups", "sector", "blk"), None, None),
        P(("groups", "op"), "blk", None, None),
        P(("groups", "op"), None, None, None),
        P(("groups", "sector", "blk")),
        P(("groups", "sector", "blk")),
        P(("groups", "op"), ("sector", "blk")),
        P(("groups", "sector"), "blk", None),
    )
    out_specs = P(("groups", "sector", "blk"), None, None)
    sizes = tuple(mesh.shape[name] for name in ("sector", "blk", "op"))
    return jax.shard_map(
        functools.partial(shards, sizes), mesh=mesh, in_specs=in_specs, out_specs=out_specs, check_vma=False
    )
```

```python
import functools

import jax
import jax.numpy as jnp
from jax import lax
from jax.experimental import pallas as pl
from jax.experimental.pallas import tpu as pltpu
from jax.sharding import PartitionSpec as P

CAP = 4
GROUP = 4
SETS = 4
MOST_SLOTS = 64
BLOCK_K = 16
TAIL = 16
NT = (((1,), (1,)), ((), ()))


def arrange(left_qn, plan, blocks, left_local):
    mine = lax.axis_index("blk")
    count = left_qn.shape[0]

    def one_code(code, n):
        plan[count + 1 + code] = n
        owner = lax.rem(mine + lax.div(code, jnp.int32(left_local)), jnp.int32(blocks))
        wanted = owner * left_local + lax.rem(code, jnp.int32(left_local))

        def one_sector(s, n):
            plan[n] = s
            return n + (left_qn[s] == wanted).astype(jnp.int32)

        return lax.fori_loop(0, count, one_sector, n)

    plan[count + 1 + blocks * left_local] = lax.fori_loop(0, blocks * left_local, one_code, jnp.int32(0))


def cut_kernel(left, direct, middle, sems):
    quarter, count = direct.shape[0], middle.shape[0]
    first = lax.rem(lax.axis_index("sector"), jnp.int32(2)) * (left.shape[0] - quarter)
    copies = [
        pltpu.make_async_copy(left.at[pl.ds(first, quarter)], direct, sems.at[0]),
        pltpu.make_async_copy(left.at[pl.ds(quarter, count)], middle, sems.at[1]),
    ]
    for copy in copies:
        copy.start()
    for copy in copies:
        copy.wait()


def right_kernel(
    blocks, left_local, left_qn_in, right_qn_in, psi_in, right_in, half, plan,
    left_qn, right_qn, psi, right, sources, sems,
):
    sectors, width = psi.shape[0], psi.shape[1]
    right_count = right.shape[1]
    steps = right.shape[0] // BLOCK_K
    zero = jnp.zeros((width, width), jnp.bfloat16)

    def right_copy(i):
        at = pl.ds(i * BLOCK_K, BLOCK_K)
        return pltpu.make_async_copy(right_in.at[at], right.at[at], sems.at[3 + i])

    copies = [
        pltpu.make_async_copy(left_qn_in, left_qn, sems.at[0]),
        pltpu.make_async_copy(right_qn_in, right_qn, sems.at[1]),
        pltpu.make_async_copy(psi_in, psi, sems.at[2]),
    ]
    for copy in copies:
        copy.start()
    for i in range(steps):
        right_copy(i).start()
    copies[0].wait()
    copies[1].wait()
    arrange(left_qn, plan, blocks, left_local)
    copies[2].wait()
    for pair in range(sectors // 2):
        for e in range(2):
            s = plan[2 * pair + e]
            block = psi[s].T
            for r in range(right_count):
                sources[pair, r * width : (r + 1) * width, e * width : (e + 1) * width] = jnp.where(
                    right_qn[s] == r, block, zero
                )

    def one_step(i, unused):
        right_copy(i).wait()
        at = pl.ds(i * BLOCK_K, BLOCK_K)
        stream = jnp.concatenate([right[at, r].reshape(BLOCK_K * width, width) for r in range(right_count)], axis=1)
        for pair in range(sectors // 2):
            product = jnp.dot(stream, sources[pair], preferred_element_type=jnp.float32)
            half[pair // 2, at, pair % 2] = product.astype(jnp.bfloat16).reshape(BLOCK_K, width, 2 * width)
        return unused

    lax.fori_loop(0, steps, one_step, 0)


def accumulate(code, pieces, plan, slots, half, totals):
    sectors, width = slots.shape[0], totals[0].shape[1]
    spare = totals[0].shape[0] - 1
    low, high = plan[sectors + 1 + code], plan[sectors + 2 + code]
    zero = jnp.zeros((width, width), jnp.bfloat16)

    def one_group(g, unused):
        places = [g * GROUP + j for j in range(GROUP)]
        members = [plan[at] for at in places]
        counts = [(low <= at) & (at < high) for at in places]
        for first, left in pieces:
            for i in range(left.shape[0]):
                k = first + i
                block = left[i]
                weights = jnp.concatenate(
                    [jnp.concatenate([block, zero], axis=1), jnp.concatenate([zero, block], axis=1)], axis=0
                )
                term = lax.dot_general(
                    half[g, k].reshape(GROUP // 2 * width, 2 * width),
                    weights,
                    NT,
                    preferred_element_type=jnp.float32,
                )
                for j in range(GROUP):
                    p, e = j // 2, j % 2
                    slot = jnp.where(counts[j], slots[members[j], k], spare)
                    totals[j % len(totals)][slot] += term[p * width : (p + 1) * width, e * width : (e + 1) * width]
        return unused

    groups = jnp.where(low < high, lax.div(high + GROUP - 1, jnp.int32(GROUP)), 0)
    lax.fori_loop(lax.div(low, jnp.int32(GROUP)), groups, one_group, 0)


def own_kernel(plan, slots, half, left, *totals):
    for total in totals:
        total[...] = jnp.zeros_like(total)
    for l in range(left.shape[1]):
        accumulate(l, [(0, left.at[:, l])], plan, slots, half, totals)


def other_kernel(rows, sets, plan, slots, half, swapped, direct, middle, *rest):
    totals, (keep, give) = rest[sets : 2 * sets], rest[2 * sets :]
    shifts, quarter, left_local = swapped.shape[0], swapped.shape[1], swapped.shape[2]
    row, side = lax.axis_index("sector"), lax.axis_index("op")
    operators, width = slots.shape[1], totals[0].shape[1]
    odd = lax.rem(row, jnp.int32(2))
    near = odd * (operators - quarter)
    far = (1 - odd) * (operators - quarter)

    def one_shift(d, unused):
        for l in range(left_local):
            pieces = [
                (near, direct.at[d, :, l]), (quarter, middle.at[d, :, l]), (far, swapped.at[d, :, l])
            ]
            accumulate((d + 1) * left_local + l, pieces, plan, slots, half, totals)
        return unused

    lax.fori_loop(0, shifts, one_shift, 0)
    part = CAP // 2
    for owner in range(rows):
        for m in range(part):
            at = owner * CAP + side * part + m
            keep[owner * part + m] = sum(total[at] for total in totals)
            at = owner * CAP + (1 - side) * part + m
            give[owner * part + m] = sum(total[at] for total in totals).astype(jnp.bfloat16)


def combine_kernel(slot_target, keep, taken, *outs):
    part, width = CAP // 2, keep.shape[1]
    row, side = lax.axis_index("sector"), lax.axis_index("op")
    line = lax.broadcasted_iota(jnp.int32, (TAIL, width), 0)
    for d, out in enumerate(outs):
        owner = lax.rem(row + d, jnp.int32(len(outs)))
        ids = jnp.zeros((TAIL, width), jnp.int32)
        for m in range(part):
            block = keep[owner * part + m] + taken[owner * part + m].astype(jnp.float32)
            out[m * width : (m + 1) * width, :] = block.astype(jnp.bfloat16)
            ids = jnp.where(line == m, slot_target[0, 0, owner * CAP + side * part + m], ids)
        out[part * width :, :] = ids.astype(jnp.float32).astype(jnp.bfloat16)


def assemble_kernel(rows, *rest):
    mine, theirs, out = rest[:rows], rest[rows : 2 * rows], rest[-1]
    part, width = CAP // 2, out.shape[1]
    side = lax.axis_index("op")
    out[...] = jnp.zeros_like(out)
    for d in range(rows):
        for h in range(2):
            ids = jnp.where(side == h, mine[d][part * width :, :], theirs[d][part * width :, :]).astype(jnp.float32)
            for m in range(part):
                at = pl.ds(m * width, width)
                block = jnp.where(side == h, mine[d][at, :], theirs[d][at, :]).astype(jnp.float32)
                target = jnp.max(ids[m : m + 1, :]).astype(jnp.int32)
                out[target] += block.T


def shards(sizes, psi, left_ops, right_ops, left_qn, right_qn, pair_slot, slot_target):
    rows, blocks, halves = sizes
    sectors, width = psi.shape[0], psi.shape[1]
    operators, left_local = left_ops.shape[0], left_ops.shape[1]
    slots = pair_slot.T
    smem = pl.BlockSpec(memory_space=pltpu.SMEM)
    vmem = pl.BlockSpec(memory_space=pltpu.VMEM)
    hbm = pl.BlockSpec(memory_space=pltpu.HBM)
    sets = max(1, min(SETS, MOST_SLOTS // (rows * CAP)))
    total_shape = (rows * CAP + 1, width, width)
    right_count = right_ops.shape[1]
    params = pltpu.CompilerParams(vmem_limit_bytes=12 * 2**20)

    def cost(share):
        flops = int(16 * operators * sectors * width**3 * share)
        return pl.CostEstimate(flops=flops, bytes_accessed=4 * 2**20, transcendentals=0)

    assert rows % 2 == 0
    quarter = operators // 4
    swap = [(i, i ^ 1) for i in range(rows)]

    def over_blocks(part):
        return [lax.ppermute(part, "blk", [((b + d) % blocks, b) for b in range(blocks)]) for d in range(1, blocks)]

    direct, middle = pl.pallas_call(
        cut_kernel,
        out_shape=[
            jax.ShapeDtypeStruct((count, *left_ops.shape[1:]), left_ops.dtype)
            for count in (quarter, operators - 2 * quarter)
        ],
        in_specs=[hbm],
        out_specs=[vmem] * 2,
        scratch_shapes=[pltpu.SemaphoreType.DMA((2,))],
        compiler_params=params,
        name="cut_left",
    )(pltpu.with_memory_space_constraint(left_ops, pltpu.HBM))
    direct, middle = over_blocks(direct), over_blocks(middle)

    half, plan = pl.pallas_call(
        functools.partial(right_kernel, blocks, left_local),
        out_shape=[
            jax.ShapeDtypeStruct((sectors // GROUP, operators, GROUP // 2, width, 2 * width), jnp.bfloat16),
            jax.ShapeDtypeStruct((sectors + 2 + blocks * left_local,), jnp.int32),
        ],
        in_specs=[hbm] * 4,
        out_specs=[vmem, smem],
        scratch_shapes=[
            pltpu.SMEM(left_qn.shape, jnp.int32),
            pltpu.SMEM(right_qn.shape, jnp.int32),
            pltpu.VMEM(psi.shape, psi.dtype),
            pltpu.VMEM(right_ops.shape, right_ops.dtype),
            pltpu.VMEM((sectors // 2, right_count * width, 2 * width), jnp.bfloat16),
            pltpu.SemaphoreType.DMA((3 + operators // BLOCK_K,)),
        ],
        compiler_params=params,
        cost_estimate=cost(0.5),
        name="right_side",
    )(*(pltpu.with_memory_space_constraint(x, pltpu.HBM) for x in (left_qn, right_qn, psi, right_ops)))
    half, direct = lax.optimization_barrier((half, direct))
    swapped = [lax.ppermute(part, "sector", swap) for part in direct]
    totals = pl.pallas_call(
        own_kernel,
        out_shape=[jax.ShapeDtypeStruct(total_shape, jnp.float32)] * sets,
        in_specs=[smem] * 2 + [vmem] * 2,
        out_specs=[vmem] * sets,
        compiler_params=params,
        cost_estimate=cost(0.25),
        name="own_left",
    )(plan, slots, half, left_ops)
    results = pl.pallas_call(
        functools.partial(other_kernel, rows, sets),
        out_shape=[jax.ShapeDtypeStruct(total_shape, jnp.float32)] * sets
        + [jax.ShapeDtypeStruct((rows * CAP // 2, width, width), kind) for kind in (jnp.float32, jnp.bfloat16)],
        in_specs=[smem] * 2 + [vmem] * (4 + sets),
        out_specs=[vmem] * (sets + 2),
        input_output_aliases={6 + j: j for j in range(sets)},
        compiler_params=params,
        cost_estimate=cost(0.25),
        name="other_left",
    )(plan, slots, half, jnp.stack(swapped), jnp.stack(direct), jnp.stack(middle), *totals)
    keep, give = results[sets:]

    def over_cores(block):
        return lax.ppermute(block, "op", [(h, halves - 1 - h) for h in range(halves)])

    partial = pl.pallas_call(
        combine_kernel,
        out_shape=[jax.ShapeDtypeStruct((CAP // 2 * width + TAIL, width), jnp.bfloat16)] * rows,
        in_specs=[smem] + [vmem] * 2,
        out_specs=[vmem] * rows,
        compiler_params=params,
        name="combine",
    )(slot_target, keep, over_cores(give))
    crossed = {
        d: lax.ppermute(partial[d], "sector", [(i, (i + d) % rows) for i in range(rows)]) for d in range(1, rows)
    }
    mine = [partial[0]] + [crossed[d] for d in range(1, rows)]
    theirs = [over_cores(block) for block in mine]
    return pl.pallas_call(
        functools.partial(assemble_kernel, rows),
        out_shape=jax.ShapeDtypeStruct((sectors, width, width), jnp.float32),
        in_specs=[vmem] * (2 * rows),
        out_specs=vmem,
        compiler_params=params,
        name="assemble",
    )(*mine, *theirs)


def solution(mesh):
    in_specs = (
        P(("groups", "sector", "blk"), None, None),
        P(("groups", "op"), "blk", None, None),
        P(("groups", "op"), None, None, None),
        P(("groups", "sector", "blk")),
        P(("groups", "sector", "blk")),
        P(("groups", "op"), ("sector", "blk")),
        P(("groups", "sector"), "blk", None),
    )
    out_specs = P(("groups", "sector", "blk"), None, None)
    sizes = tuple(mesh.shape[name] for name in ("sector", "blk", "op"))
    return jax.shard_map(
        functools.partial(shards, sizes), mesh=mesh, in_specs=in_specs, out_specs=out_specs, check_vma=False
    )
```

```python
import functools

import jax
import jax.numpy as jnp
from jax import lax
from jax.experimental import pallas as pl
from jax.experimental.pallas import tpu as pltpu
from jax.sharding import PartitionSpec as P

CAP = 4
GROUP = 4
SETS = 4
MOST_SLOTS = 64
BLOCK_K = 16
TAIL = 16
NT = (((1,), (1,)), ((), ()))


def arrange(left_qn, plan, blocks, left_local):
    mine = lax.axis_index("blk")
    count = left_qn.shape[0]

    def one_code(code, n):
        plan[count + 1 + code] = n
        owner = lax.rem(mine + lax.div(code, jnp.int32(left_local)), jnp.int32(blocks))
        wanted = owner * left_local + lax.rem(code, jnp.int32(left_local))

        def one_sector(s, n):
            plan[n] = s
            return n + (left_qn[s] == wanted).astype(jnp.int32)

        return lax.fori_loop(0, count, one_sector, n)

    plan[count + 1 + blocks * left_local] = lax.fori_loop(0, blocks * left_local, one_code, jnp.int32(0))


def cut_kernel(left, direct, middle, sems):
    quarter, count = direct.shape[0], middle.shape[0]
    first = lax.rem(lax.axis_index("sector"), jnp.int32(2)) * (left.shape[0] - quarter)
    copies = [
        pltpu.make_async_copy(left.at[pl.ds(first, quarter)], direct, sems.at[0]),
        pltpu.make_async_copy(left.at[pl.ds(quarter, count)], middle, sems.at[1]),
    ]
    for copy in copies:
        copy.start()
    for copy in copies:
        copy.wait()


def right_kernel(
    blocks, left_local, left_qn_in, right_qn_in, psi_in, right_in, half, plan,
    left_qn, right_qn, psi, right, sources, sems,
):
    sectors, width = psi.shape[0], psi.shape[1]
    right_count = right.shape[1]
    steps = right.shape[0] // BLOCK_K
    zero = jnp.zeros((width, width), jnp.bfloat16)

    def right_copy(i):
        at = pl.ds(i * BLOCK_K, BLOCK_K)
        return pltpu.make_async_copy(right_in.at[at], right.at[at], sems.at[3 + i])

    copies = [
        pltpu.make_async_copy(left_qn_in, left_qn, sems.at[0]),
        pltpu.make_async_copy(right_qn_in, right_qn, sems.at[1]),
        pltpu.make_async_copy(psi_in, psi, sems.at[2]),
    ]
    for copy in copies:
        copy.start()
    for i in range(steps):
        right_copy(i).start()
    copies[0].wait()
    copies[1].wait()
    arrange(left_qn, plan, blocks, left_local)
    copies[2].wait()
    for pair in range(sectors // 2):
        for e in range(2):
            s = plan[2 * pair + e]
            block = psi[s].T
            for r in range(right_count):
                sources[pair, r * width : (r + 1) * width, e * width : (e + 1) * width] = jnp.where(
                    right_qn[s] == r, block, zero
                )

    def one_step(i, unused):
        right_copy(i).wait()
        at = pl.ds(i * BLOCK_K, BLOCK_K)
        stream = jnp.concatenate([right[at, r].reshape(BLOCK_K * width, width) for r in range(right_count)], axis=1)
        for pair in range(sectors // 2):
            product = jnp.dot(stream, sources[pair], preferred_element_type=jnp.float32)
            half[pair // 2, at, pair % 2] = product.astype(jnp.bfloat16).reshape(BLOCK_K, width, 2 * width)
        return unused

    lax.fori_loop(0, steps, one_step, 0)


def accumulate(code, pieces, plan, slots, half, totals):
    sectors, width = slots.shape[0], totals[0].shape[1]
    spare = totals[0].shape[0] - 1
    low, high = plan[sectors + 1 + code], plan[sectors + 2 + code]
    zero = jnp.zeros((width, width), jnp.bfloat16)

    def one_group(g, unused):
        places = [g * GROUP + j for j in range(GROUP)]
        members = [plan[at] for at in places]
        counts = [(low <= at) & (at < high) for at in places]
        for first, left in pieces:
            for i in range(left.shape[0]):
                k = first + i
                block = left[i]
                weights = jnp.concatenate(
                    [jnp.concatenate([block, zero], axis=1), jnp.concatenate([zero, block], axis=1)], axis=0
                )
                term = lax.dot_general(
                    half[g, k].reshape(GROUP // 2 * width, 2 * width),
                    weights,
                    NT,
                    preferred_element_type=jnp.float32,
                )
                for j in range(GROUP):
                    p, e = j // 2, j % 2
                    slot = jnp.where(counts[j], slots[members[j], k], spare)
                    totals[j % len(totals)][slot] += term[p * width : (p + 1) * width, e * width : (e + 1) * width]
        return unused

    groups = jnp.where(low < high, lax.div(high + GROUP - 1, jnp.int32(GROUP)), 0)
    lax.fori_loop(lax.div(low, jnp.int32(GROUP)), groups, one_group, 0)


def own_kernel(plan, slots, half, left, direct, *totals):
    shifts, quarter, left_local = direct.shape[0], direct.shape[1], direct.shape[2]
    near = lax.rem(lax.axis_index("sector"), jnp.int32(2)) * (left.shape[0] - quarter)
    for total in totals:
        total[...] = jnp.zeros_like(total)
    for l in range(left_local):
        accumulate(l, [(0, left.at[:, l])], plan, slots, half, totals)

    def one_shift(d, unused):
        for l in range(left_local):
            accumulate((d + 1) * left_local + l, [(near, direct.at[d, :, l])], plan, slots, half, totals)
        return unused

    lax.fori_loop(0, shifts, one_shift, 0)


def other_kernel(rows, sets, plan, slots, half, swapped, middle, *rest):
    totals, (keep, give) = rest[sets : 2 * sets], rest[2 * sets :]
    shifts, quarter, left_local = swapped.shape[0], swapped.shape[1], swapped.shape[2]
    row, side = lax.axis_index("sector"), lax.axis_index("op")
    operators, width = slots.shape[1], totals[0].shape[1]
    far = (1 - lax.rem(row, jnp.int32(2))) * (operators - quarter)

    def one_shift(d, unused):
        for l in range(left_local):
            pieces = [(quarter, middle.at[d, :, l]), (far, swapped.at[d, :, l])]
            accumulate((d + 1) * left_local + l, pieces, plan, slots, half, totals)
        return unused

    lax.fori_loop(0, shifts, one_shift, 0)
    part = CAP // 2
    for owner in range(rows):
        for m in range(part):
            at = owner * CAP + side * part + m
            keep[owner * part + m] = sum(total[at] for total in totals)
            at = owner * CAP + (1 - side) * part + m
            give[owner * part + m] = sum(total[at] for total in totals).astype(jnp.bfloat16)


def combine_kernel(slot_target, keep, taken, *outs):
    part, width = CAP // 2, keep.shape[1]
    row, side = lax.axis_index("sector"), lax.axis_index("op")
    line = lax.broadcasted_iota(jnp.int32, (TAIL, width), 0)
    for d, out in enumerate(outs):
        owner = lax.rem(row + d, jnp.int32(len(outs)))
        ids = jnp.zeros((TAIL, width), jnp.int32)
        for m in range(part):
            block = keep[owner * part + m] + taken[owner * part + m].astype(jnp.float32)
            out[m * width : (m + 1) * width, :] = block.astype(jnp.bfloat16)
            ids = jnp.where(line == m, slot_target[0, 0, owner * CAP + side * part + m], ids)
        out[part * width :, :] = ids.astype(jnp.float32).astype(jnp.bfloat16)


def assemble_kernel(rows, *rest):
    mine, theirs, out = rest[:rows], rest[rows : 2 * rows], rest[-1]
    part, width = CAP // 2, out.shape[1]
    side = lax.axis_index("op")
    out[...] = jnp.zeros_like(out)
    for d in range(rows):
        for h in range(2):
            ids = jnp.where(side == h, mine[d][part * width :, :], theirs[d][part * width :, :]).astype(jnp.float32)
            for m in range(part):
                at = pl.ds(m * width, width)
                block = jnp.where(side == h, mine[d][at, :], theirs[d][at, :]).astype(jnp.float32)
                target = jnp.max(ids[m : m + 1, :]).astype(jnp.int32)
                out[target] += block.T


def shards(sizes, psi, left_ops, right_ops, left_qn, right_qn, pair_slot, slot_target):
    rows, blocks, halves = sizes
    sectors, width = psi.shape[0], psi.shape[1]
    operators, left_local = left_ops.shape[0], left_ops.shape[1]
    slots = pair_slot.T
    smem = pl.BlockSpec(memory_space=pltpu.SMEM)
    vmem = pl.BlockSpec(memory_space=pltpu.VMEM)
    hbm = pl.BlockSpec(memory_space=pltpu.HBM)
    sets = max(1, min(SETS, MOST_SLOTS // (rows * CAP)))
    total_shape = (rows * CAP + 1, width, width)
    right_count = right_ops.shape[1]
    params = pltpu.CompilerParams(vmem_limit_bytes=12 * 2**20)

    def cost(share):
        flops = int(16 * operators * sectors * width**3 * share)
        return pl.CostEstimate(flops=flops, bytes_accessed=4 * 2**20, transcendentals=0)

    assert rows % 2 == 0
    quarter = operators // 4
    swap = [(i, i ^ 1) for i in range(rows)]

    def over_blocks(part):
        return [lax.ppermute(part, "blk", [((b + d) % blocks, b) for b in range(blocks)]) for d in range(1, blocks)]

    direct, middle = pl.pallas_call(
        cut_kernel,
        out_shape=[
            jax.ShapeDtypeStruct((count, *left_ops.shape[1:]), left_ops.dtype)
            for count in (quarter, operators - 2 * quarter)
        ],
        in_specs=[hbm],
        out_specs=[vmem] * 2,
        scratch_shapes=[pltpu.SemaphoreType.DMA((2,))],
        compiler_params=params,
        name="cut_left",
    )(pltpu.with_memory_space_constraint(left_ops, pltpu.HBM))
    direct, middle = over_blocks(direct), over_blocks(middle)

    half, plan = pl.pallas_call(
        functools.partial(right_kernel, blocks, left_local),
        out_shape=[
            jax.ShapeDtypeStruct((sectors // GROUP, operators, GROUP // 2, width, 2 * width), jnp.bfloat16),
            jax.ShapeDtypeStruct((sectors + 2 + blocks * left_local,), jnp.int32),
        ],
        in_specs=[hbm] * 4,
        out_specs=[vmem, smem],
        scratch_shapes=[
            pltpu.SMEM(left_qn.shape, jnp.int32),
            pltpu.SMEM(right_qn.shape, jnp.int32),
            pltpu.VMEM(psi.shape, psi.dtype),
            pltpu.VMEM(right_ops.shape, right_ops.dtype),
            pltpu.VMEM((sectors // 2, right_count * width, 2 * width), jnp.bfloat16),
            pltpu.SemaphoreType.DMA((3 + operators // BLOCK_K,)),
        ],
        compiler_params=params,
        cost_estimate=cost(0.5),
        name="right_side",
    )(*(pltpu.with_memory_space_constraint(x, pltpu.HBM) for x in (left_qn, right_qn, psi, right_ops)))
    half, direct = lax.optimization_barrier((half, direct))
    swapped = [lax.ppermute(part, "sector", swap) for part in direct]
    totals = pl.pallas_call(
        own_kernel,
        out_shape=[jax.ShapeDtypeStruct(total_shape, jnp.float32)] * sets,
        in_specs=[smem] * 2 + [vmem] * 3,
        out_specs=[vmem] * sets,
        compiler_params=params,
        cost_estimate=cost(0.25),
        name="own_left",
    )(plan, slots, half, left_ops, jnp.stack(direct))
    results = pl.pallas_call(
        functools.partial(other_kernel, rows, sets),
        out_shape=[jax.ShapeDtypeStruct(total_shape, jnp.float32)] * sets
        + [jax.ShapeDtypeStruct((rows * CAP // 2, width, width), kind) for kind in (jnp.float32, jnp.bfloat16)],
        in_specs=[smem] * 2 + [vmem] * (3 + sets),
        out_specs=[vmem] * (sets + 2),
        input_output_aliases={5 + j: j for j in range(sets)},
        compiler_params=params,
        cost_estimate=cost(0.25),
        name="other_left",
    )(plan, slots, half, jnp.stack(swapped), jnp.stack(middle), *totals)
    keep, give = results[sets:]

    def over_cores(block):
        return lax.ppermute(block, "op", [(h, halves - 1 - h) for h in range(halves)])

    partial = pl.pallas_call(
        combine_kernel,
        out_shape=[jax.ShapeDtypeStruct((CAP // 2 * width + TAIL, width), jnp.bfloat16)] * rows,
        in_specs=[smem] + [vmem] * 2,
        out_specs=[vmem] * rows,
        compiler_params=params,
        name="combine",
    )(slot_target, keep, over_cores(give))
    crossed = {
        d: lax.ppermute(partial[d], "sector", [(i, (i + d) % rows) for i in range(rows)]) for d in range(1, rows)
    }
    mine = [partial[0]] + [crossed[d] for d in range(1, rows)]
    theirs = [over_cores(block) for block in mine]
    return pl.pallas_call(
        functools.partial(assemble_kernel, rows),
        out_shape=jax.ShapeDtypeStruct((sectors, width, width), jnp.float32),
        in_specs=[vmem] * (2 * rows),
        out_specs=vmem,
        compiler_params=params,
        name="assemble",
    )(*mine, *theirs)


def solution(mesh):
    in_specs = (
        P(("groups", "sector", "blk"), None, None),
        P(("groups", "op"), "blk", None, None),
        P(("groups", "op"), None, None, None),
        P(("groups", "sector", "blk")),
        P(("groups", "sector", "blk")),
        P(("groups", "op"), ("sector", "blk")),
        P(("groups", "sector"), "blk", None),
    )
    out_specs = P(("groups", "sector", "blk"), None, None)
    sizes = tuple(mesh.shape[name] for name in ("sector", "blk", "op"))
    return jax.shard_map(
        functools.partial(shards, sizes), mesh=mesh, in_specs=in_specs, out_specs=out_specs, check_vma=False
    )
```

```python
import functools

import jax
import jax.numpy as jnp
from jax import lax
from jax.experimental import pallas as pl
from jax.experimental.pallas import tpu as pltpu
from jax.sharding import PartitionSpec as P

CAP = 4
GROUP = 4
SETS = 4
MOST_SLOTS = 64
BLOCK_K = 16
TAIL = 16
NT = (((1,), (1,)), ((), ()))


def arrange(left_qn, plan, blocks, left_local):
    mine = lax.axis_index("blk")
    count = left_qn.shape[0]

    def one_code(code, n):
        plan[count + 1 + code] = n
        owner = lax.rem(mine + lax.div(code, jnp.int32(left_local)), jnp.int32(blocks))
        wanted = owner * left_local + lax.rem(code, jnp.int32(left_local))

        def one_sector(s, n):
            plan[n] = s
            return n + (left_qn[s] == wanted).astype(jnp.int32)

        return lax.fori_loop(0, count, one_sector, n)

    plan[count + 1 + blocks * left_local] = lax.fori_loop(0, blocks * left_local, one_code, jnp.int32(0))


def cut_kernel(left, direct, middle, sems):
    quarter, count = direct.shape[0], middle.shape[0]
    first = lax.rem(lax.axis_index("sector"), jnp.int32(2)) * (left.shape[0] - quarter)
    copies = [
        pltpu.make_async_copy(left.at[pl.ds(first, quarter)], direct, sems.at[0]),
        pltpu.make_async_copy(left.at[pl.ds(quarter, count)], middle, sems.at[1]),
    ]
    for copy in copies:
        copy.start()
    for copy in copies:
        copy.wait()


def right_kernel(
    blocks, left_local, left_qn_in, right_qn_in, psi_in, right_in, half, plan,
    left_qn, right_qn, psi, right, sources, sems,
):
    sectors, width = psi.shape[0], psi.shape[1]
    right_count = right.shape[1]
    steps = right.shape[0] // BLOCK_K
    zero = jnp.zeros((width, width), jnp.bfloat16)

    def right_copy(i):
        at = pl.ds(i * BLOCK_K, BLOCK_K)
        return pltpu.make_async_copy(right_in.at[at], right.at[at], sems.at[3 + i])

    copies = [
        pltpu.make_async_copy(left_qn_in, left_qn, sems.at[0]),
        pltpu.make_async_copy(right_qn_in, right_qn, sems.at[1]),
        pltpu.make_async_copy(psi_in, psi, sems.at[2]),
    ]
    for copy in copies:
        copy.start()
    for i in range(steps):
        right_copy(i).start()
    copies[0].wait()
    copies[1].wait()
    arrange(left_qn, plan, blocks, left_local)
    copies[2].wait()
    for pair in range(sectors // 2):
        for e in range(2):
            s = plan[2 * pair + e]
            block = psi[s].T
            for r in range(right_count):
                sources[pair, r * width : (r + 1) * width, e * width : (e + 1) * width] = jnp.where(
                    right_qn[s] == r, block, zero
                )

    def one_step(i, unused):
        right_copy(i).wait()
        at = pl.ds(i * BLOCK_K, BLOCK_K)
        stream = jnp.concatenate([right[at, r].reshape(BLOCK_K * width, width) for r in range(right_count)], axis=1)
        for pair in range(sectors // 2):
            product = jnp.dot(stream, sources[pair], preferred_element_type=jnp.float32)
            half[pair // 2, at, pair % 2] = product.astype(jnp.bfloat16).reshape(BLOCK_K, width, 2 * width)
        return unused

    lax.fori_loop(0, steps, one_step, 0)


def accumulate(code, pieces, plan, slots, half, totals):
    sectors, width = slots.shape[0], totals[0].shape[1]
    spare = totals[0].shape[0] - 1
    low, high = plan[sectors + 1 + code], plan[sectors + 2 + code]
    zero = jnp.zeros((width, width), jnp.bfloat16)

    def terms(g, count):
        places = [g * GROUP + j for j in range(count * GROUP)]
        members = [plan[at] for at in places]
        counts = [(low <= at) & (at < high) for at in places]
        for first, left in pieces:
            for i in range(left.shape[0]):
                k = first + i
                block = left[i]
                weights = jnp.concatenate(
                    [jnp.concatenate([block, zero], axis=1), jnp.concatenate([zero, block], axis=1)], axis=0
                )
                term = lax.dot_general(
                    half[pl.ds(g, count), k].reshape(count * GROUP // 2 * width, 2 * width),
                    weights,
                    NT,
                    preferred_element_type=jnp.float32,
                )
                for j in range(count * GROUP):
                    p, e = j // 2, j % 2
                    slot = jnp.where(counts[j], slots[members[j], k], spare)
                    totals[j % len(totals)][slot] += term[
                        p * width : (p + 1) * width, e * width : (e + 1) * width
                    ]

    def two_groups(i, unused):
        terms(start + 2 * i, 2)
        return unused

    def last_group(i, unused):
        terms(start + groups - 1, 1)
        return unused

    start = lax.div(low, jnp.int32(GROUP))
    groups = jnp.where(low < high, lax.div(high + GROUP - 1, jnp.int32(GROUP)) - start, 0)
    lax.fori_loop(0, lax.div(groups, 2), two_groups, 0)
    lax.fori_loop(0, lax.rem(groups, 2), last_group, 0)


def own_kernel(plan, slots, half, left, direct, *totals):
    shifts, quarter, left_local = direct.shape[0], direct.shape[1], direct.shape[2]
    near = lax.rem(lax.axis_index("sector"), jnp.int32(2)) * (left.shape[0] - quarter)
    for total in totals:
        total[...] = jnp.zeros_like(total)
    for l in range(left_local):
        accumulate(l, [(0, left.at[:, l])], plan, slots, half, totals)

    def one_shift(d, unused):
        for l in range(left_local):
            accumulate((d + 1) * left_local + l, [(near, direct.at[d, :, l])], plan, slots, half, totals)
        return unused

    lax.fori_loop(0, shifts, one_shift, 0)


def other_kernel(rows, sets, plan, slots, half, swapped, middle, *rest):
    totals, (keep, give) = rest[sets : 2 * sets], rest[2 * sets :]
    shifts, quarter, left_local = swapped.shape[0], swapped.shape[1], swapped.shape[2]
    row, side = lax.axis_index("sector"), lax.axis_index("op")
    operators, width = slots.shape[1], totals[0].shape[1]
    far = (1 - lax.rem(row, jnp.int32(2))) * (operators - quarter)

    def one_shift(d, unused):
        for l in range(left_local):
            pieces = [(quarter, middle.at[d, :, l]), (far, swapped.at[d, :, l])]
            accumulate((d + 1) * left_local + l, pieces, plan, slots, half, totals)
        return unused

    lax.fori_loop(0, shifts, one_shift, 0)
    part = CAP // 2
    for owner in range(rows):
        for m in range(part):
            at = owner * CAP + side * part + m
            keep[owner * part + m] = sum(total[at] for total in totals)
            at = owner * CAP + (1 - side) * part + m
            give[owner * part + m] = sum(total[at] for total in totals).astype(jnp.bfloat16)


def combine_kernel(slot_target, keep, taken, *outs):
    part, width = CAP // 2, keep.shape[1]
    row, side = lax.axis_index("sector"), lax.axis_index("op")
    line = lax.broadcasted_iota(jnp.int32, (TAIL, width), 0)
    for d, out in enumerate(outs):
        owner = lax.rem(row + d, jnp.int32(len(outs)))
        ids = jnp.zeros((TAIL, width), jnp.int32)
        for m in range(part):
            block = keep[owner * part + m] + taken[owner * part + m].astype(jnp.float32)
            out[m * width : (m + 1) * width, :] = block.astype(jnp.bfloat16)
            ids = jnp.where(line == m, slot_target[0, 0, owner * CAP + side * part + m], ids)
        out[part * width :, :] = ids.astype(jnp.float32).astype(jnp.bfloat16)


def assemble_kernel(rows, *rest):
    mine, theirs, out = rest[:rows], rest[rows : 2 * rows], rest[-1]
    part, width = CAP // 2, out.shape[1]
    side = lax.axis_index("op")
    out[...] = jnp.zeros_like(out)
    for d in range(rows):
        for h in range(2):
            ids = jnp.where(side == h, mine[d][part * width :, :], theirs[d][part * width :, :]).astype(jnp.float32)
            for m in range(part):
                at = pl.ds(m * width, width)
                block = jnp.where(side == h, mine[d][at, :], theirs[d][at, :]).astype(jnp.float32)
                target = jnp.max(ids[m : m + 1, :]).astype(jnp.int32)
                out[target] += block.T


def shards(sizes, psi, left_ops, right_ops, left_qn, right_qn, pair_slot, slot_target):
    rows, blocks, halves = sizes
    sectors, width = psi.shape[0], psi.shape[1]
    operators, left_local = left_ops.shape[0], left_ops.shape[1]
    slots = pair_slot.T
    smem = pl.BlockSpec(memory_space=pltpu.SMEM)
    vmem = pl.BlockSpec(memory_space=pltpu.VMEM)
    hbm = pl.BlockSpec(memory_space=pltpu.HBM)
    sets = max(1, min(SETS, MOST_SLOTS // (rows * CAP)))
    total_shape = (rows * CAP + 1, width, width)
    right_count = right_ops.shape[1]
    params = pltpu.CompilerParams(vmem_limit_bytes=12 * 2**20)

    def cost(share):
        flops = int(16 * operators * sectors * width**3 * share)
        return pl.CostEstimate(flops=flops, bytes_accessed=4 * 2**20, transcendentals=0)

    assert rows % 2 == 0
    quarter = operators // 4
    swap = [(i, i ^ 1) for i in range(rows)]

    def over_blocks(part):
        return [lax.ppermute(part, "blk", [((b + d) % blocks, b) for b in range(blocks)]) for d in range(1, blocks)]

    direct, middle = pl.pallas_call(
        cut_kernel,
        out_shape=[
            jax.ShapeDtypeStruct((count, *left_ops.shape[1:]), left_ops.dtype)
            for count in (quarter, operators - 2 * quarter)
        ],
        in_specs=[hbm],
        out_specs=[vmem] * 2,
        scratch_shapes=[pltpu.SemaphoreType.DMA((2,))],
        compiler_params=params,
        name="cut_left",
    )(pltpu.with_memory_space_constraint(left_ops, pltpu.HBM))
    direct, middle = over_blocks(direct), over_blocks(middle)

    half, plan = pl.pallas_call(
        functools.partial(right_kernel, blocks, left_local),
        out_shape=[
            jax.ShapeDtypeStruct((sectors // GROUP, operators, GROUP // 2, width, 2 * width), jnp.bfloat16),
            jax.ShapeDtypeStruct((sectors + 2 + blocks * left_local,), jnp.int32),
        ],
        in_specs=[hbm] * 4,
        out_specs=[vmem, smem],
        scratch_shapes=[
            pltpu.SMEM(left_qn.shape, jnp.int32),
            pltpu.SMEM(right_qn.shape, jnp.int32),
            pltpu.VMEM(psi.shape, psi.dtype),
            pltpu.VMEM(right_ops.shape, right_ops.dtype),
            pltpu.VMEM((sectors // 2, right_count * width, 2 * width), jnp.bfloat16),
            pltpu.SemaphoreType.DMA((3 + operators // BLOCK_K,)),
        ],
        compiler_params=params,
        cost_estimate=cost(0.5),
        name="right_side",
    )(*(pltpu.with_memory_space_constraint(x, pltpu.HBM) for x in (left_qn, right_qn, psi, right_ops)))
    half, direct = lax.optimization_barrier((half, direct))
    swapped = [lax.ppermute(part, "sector", swap) for part in direct]
    totals = pl.pallas_call(
        own_kernel,
        out_shape=[jax.ShapeDtypeStruct(total_shape, jnp.float32)] * sets,
        in_specs=[smem] * 2 + [vmem] * 3,
        out_specs=[vmem] * sets,
        compiler_params=params,
        cost_estimate=cost(0.25),
        name="own_left",
    )(plan, slots, half, left_ops, jnp.stack(direct))
    results = pl.pallas_call(
        functools.partial(other_kernel, rows, sets),
        out_shape=[jax.ShapeDtypeStruct(total_shape, jnp.float32)] * sets
        + [jax.ShapeDtypeStruct((rows * CAP // 2, width, width), kind) for kind in (jnp.float32, jnp.bfloat16)],
        in_specs=[smem] * 2 + [vmem] * (3 + sets),
        out_specs=[vmem] * (sets + 2),
        input_output_aliases={5 + j: j for j in range(sets)},
        compiler_params=params,
        cost_estimate=cost(0.25),
        name="other_left",
    )(plan, slots, half, jnp.stack(swapped), jnp.stack(middle), *totals)
    keep, give = results[sets:]

    def over_cores(block):
        return lax.ppermute(block, "op", [(h, halves - 1 - h) for h in range(halves)])

    partial = pl.pallas_call(
        combine_kernel,
        out_shape=[jax.ShapeDtypeStruct((CAP // 2 * width + TAIL, width), jnp.bfloat16)] * rows,
        in_specs=[smem] + [vmem] * 2,
        out_specs=[vmem] * rows,
        compiler_params=params,
        name="combine",
    )(slot_target, keep, over_cores(give))
    crossed = {
        d: lax.ppermute(partial[d], "sector", [(i, (i + d) % rows) for i in range(rows)]) for d in range(1, rows)
    }
    mine = [partial[0]] + [crossed[d] for d in range(1, rows)]
    theirs = [over_cores(block) for block in mine]
    return pl.pallas_call(
        functools.partial(assemble_kernel, rows),
        out_shape=jax.ShapeDtypeStruct((sectors, width, width), jnp.float32),
        in_specs=[vmem] * (2 * rows),
        out_specs=vmem,
        compiler_params=params,
        name="assemble",
    )(*mine, *theirs)


def solution(mesh):
    in_specs = (
        P(("groups", "sector", "blk"), None, None),
        P(("groups", "op"), "blk", None, None),
        P(("groups", "op"), None, None, None),
        P(("groups", "sector", "blk")),
        P(("groups", "sector", "blk")),
        P(("groups", "op"), ("sector", "blk")),
        P(("groups", "sector"), "blk", None),
    )
    out_specs = P(("groups", "sector", "blk"), None, None)
    sizes = tuple(mesh.shape[name] for name in ("sector", "blk", "op"))
    return jax.shard_map(
        functools.partial(shards, sizes), mesh=mesh, in_specs=in_specs, out_specs=out_specs, check_vma=False
    )
```

```python
import functools

import jax
import jax.numpy as jnp
from jax import lax
from jax.experimental import pallas as pl
from jax.experimental.pallas import tpu as pltpu
from jax.sharding import PartitionSpec as P

CAP = 4
GROUP = 4
SETS = 4
MOST_SLOTS = 64
BLOCK_K = 16
BLOCK_PAIRS = 4
TAIL = 16
NT = (((1,), (1,)), ((), ()))


def arrange(left_qn, plan, blocks, left_local):
    mine = lax.axis_index("blk")
    count = left_qn.shape[0]

    def one_code(code, n):
        plan[count + 1 + code] = n
        owner = lax.rem(mine + lax.div(code, jnp.int32(left_local)), jnp.int32(blocks))
        wanted = owner * left_local + lax.rem(code, jnp.int32(left_local))

        def one_sector(s, n):
            plan[n] = s
            return n + (left_qn[s] == wanted).astype(jnp.int32)

        return lax.fori_loop(0, count, one_sector, n)

    plan[count + 1 + blocks * left_local] = lax.fori_loop(0, blocks * left_local, one_code, jnp.int32(0))


def cut_kernel(left, direct, middle, sems):
    quarter, count = direct.shape[0], middle.shape[0]
    first = lax.rem(lax.axis_index("sector"), jnp.int32(2)) * (left.shape[0] - quarter)
    copies = [
        pltpu.make_async_copy(left.at[pl.ds(first, quarter)], direct, sems.at[0]),
        pltpu.make_async_copy(left.at[pl.ds(quarter, count)], middle, sems.at[1]),
    ]
    for copy in copies:
        copy.start()
    for copy in copies:
        copy.wait()


def right_kernel(
    blocks, left_local, left_qn_in, right_qn_in, psi_in, right_in, half, plan,
    left_qn, right_qn, psi, right, sources, sems,
):
    sectors, width = psi.shape[0], psi.shape[1]
    right_count = right.shape[1]
    steps = right.shape[0] // BLOCK_K
    zero = jnp.zeros((width, width), jnp.bfloat16)

    def right_copy(i):
        at = pl.ds(i * BLOCK_K, BLOCK_K)
        return pltpu.make_async_copy(right_in.at[at], right.at[at], sems.at[3 + i])

    copies = [
        pltpu.make_async_copy(left_qn_in, left_qn, sems.at[0]),
        pltpu.make_async_copy(right_qn_in, right_qn, sems.at[1]),
        pltpu.make_async_copy(psi_in, psi, sems.at[2]),
    ]
    for copy in copies:
        copy.start()
    for i in range(steps):
        right_copy(i).start()
    copies[0].wait()
    copies[1].wait()
    arrange(left_qn, plan, blocks, left_local)
    copies[2].wait()
    for pair in range(sectors // 2):
        for e in range(2):
            s = plan[2 * pair + e]
            block = psi[s].T
            for r in range(right_count):
                sources[pair, r * width : (r + 1) * width, e * width : (e + 1) * width] = jnp.where(
                    right_qn[s] == r, block, zero
                )

    def one_step(i, unused):
        right_copy(i).wait()
        at = pl.ds(i * BLOCK_K, BLOCK_K)

        def stream():
            return jnp.concatenate([right[at, r].reshape(BLOCK_K * width, width) for r in range(right_count)], axis=1)

        def some_pairs(j, inner):
            for i in range(BLOCK_PAIRS):
                pair = j * BLOCK_PAIRS + i
                product = jnp.dot(stream(), sources[pair], preferred_element_type=jnp.float32)
                half[j * (BLOCK_PAIRS // 2) + i // 2, at, i % 2] = product.astype(jnp.bfloat16).reshape(
                    BLOCK_K, width, 2 * width
                )
            return inner

        lax.fori_loop(0, sectors // 2 // BLOCK_PAIRS, some_pairs, 0)
        return unused

    lax.fori_loop(0, steps, one_step, 0)


def accumulate(code, pieces, plan, slots, half, totals):
    sectors, width = slots.shape[0], totals[0].shape[1]
    spare = totals[0].shape[0] - 1
    low, high = plan[sectors + 1 + code], plan[sectors + 2 + code]
    zero = jnp.zeros((width, width), jnp.bfloat16)

    def one_group(g, unused):
        places = [g * GROUP + j for j in range(GROUP)]
        members = [plan[at] for at in places]
        counts = [(low <= at) & (at < high) for at in places]

        def some_operators(first, left, count):
            def one_block(b, inner):
                for i in range(count):
                    at = b * count + i
                    k = first + at
                    block = left[at]
                    weights = jnp.concatenate(
                        [jnp.concatenate([block, zero], axis=1), jnp.concatenate([zero, block], axis=1)], axis=0
                    )
                    term = lax.dot_general(
                        half[g, k].reshape(GROUP // 2 * width, 2 * width),
                        weights,
                        NT,
                        preferred_element_type=jnp.float32,
                    )
                    for j in range(GROUP):
                        p, e = j // 2, j % 2
                        slot = jnp.where(counts[j], slots[members[j], k], spare)
                        totals[j % len(totals)][slot] += term[
                            p * width : (p + 1) * width, e * width : (e + 1) * width
                        ]
                return inner

            lax.fori_loop(0, left.shape[0] // count, one_block, 0)

        for first, left in pieces:
            some_operators(first, left, min(left.shape[0], BLOCK_K))
        return unused

    groups = jnp.where(low < high, lax.div(high + GROUP - 1, jnp.int32(GROUP)), 0)
    lax.fori_loop(lax.div(low, jnp.int32(GROUP)), groups, one_group, 0)


def own_kernel(plan, slots, half, left, direct, *totals):
    shifts, quarter, left_local = direct.shape[0], direct.shape[1], direct.shape[2]
    near = lax.rem(lax.axis_index("sector"), jnp.int32(2)) * (left.shape[0] - quarter)
    for total in totals:
        total[...] = jnp.zeros_like(total)
    for l in range(left_local):
        accumulate(l, [(0, left.at[:, l])], plan, slots, half, totals)

    def one_shift(d, unused):
        for l in range(left_local):
            accumulate((d + 1) * left_local + l, [(near, direct.at[d, :, l])], plan, slots, half, totals)
        return unused

    lax.fori_loop(0, shifts, one_shift, 0)


def other_kernel(rows, sets, plan, slots, half, swapped, middle, *rest):
    totals, (keep, give) = rest[sets : 2 * sets], rest[2 * sets :]
    shifts, quarter, left_local = swapped.shape[0], swapped.shape[1], swapped.shape[2]
    row, side = lax.axis_index("sector"), lax.axis_index("op")
    operators, width = slots.shape[1], totals[0].shape[1]
    far = (1 - lax.rem(row, jnp.int32(2))) * (operators - quarter)

    def one_shift(d, unused):
        for l in range(left_local):
            pieces = [(quarter, middle.at[d, :, l]), (far, swapped.at[d, :, l])]
            accumulate((d + 1) * left_local + l, pieces, plan, slots, half, totals)
        return unused

    lax.fori_loop(0, shifts, one_shift, 0)
    part = CAP // 2
    for owner in range(rows):
        for m in range(part):
            at = owner * CAP + side * part + m
            keep[owner * part + m] = sum(total[at] for total in totals)
            at = owner * CAP + (1 - side) * part + m
            give[owner * part + m] = sum(total[at] for total in totals).astype(jnp.bfloat16)


def combine_kernel(slot_target, keep, taken, *outs):
    part, width = CAP // 2, keep.shape[1]
    row, side = lax.axis_index("sector"), lax.axis_index("op")
    line = lax.broadcasted_iota(jnp.int32, (TAIL, width), 0)
    for d, out in enumerate(outs):
        owner = lax.rem(row + d, jnp.int32(len(outs)))
        ids = jnp.zeros((TAIL, width), jnp.int32)
        for m in range(part):
            block = keep[owner * part + m] + taken[owner * part + m].astype(jnp.float32)
            out[m * width : (m + 1) * width, :] = block.astype(jnp.bfloat16)
            ids = jnp.where(line == m, slot_target[0, 0, owner * CAP + side * part + m], ids)
        out[part * width :, :] = ids.astype(jnp.float32).astype(jnp.bfloat16)


def assemble_kernel(rows, *rest):
    mine, theirs, out = rest[:rows], rest[rows : 2 * rows], rest[-1]
    part, width = CAP // 2, out.shape[1]
    side = lax.axis_index("op")
    out[...] = jnp.zeros_like(out)
    for d in range(rows):
        for h in range(2):
            ids = jnp.where(side == h, mine[d][part * width :, :], theirs[d][part * width :, :]).astype(jnp.float32)
            for m in range(part):
                at = pl.ds(m * width, width)
                block = jnp.where(side == h, mine[d][at, :], theirs[d][at, :]).astype(jnp.float32)
                target = jnp.max(ids[m : m + 1, :]).astype(jnp.int32)
                out[target] += block.T


def shards(sizes, psi, left_ops, right_ops, left_qn, right_qn, pair_slot, slot_target):
    rows, blocks, halves = sizes
    sectors, width = psi.shape[0], psi.shape[1]
    operators, left_local = left_ops.shape[0], left_ops.shape[1]
    slots = pair_slot.T
    smem = pl.BlockSpec(memory_space=pltpu.SMEM)
    vmem = pl.BlockSpec(memory_space=pltpu.VMEM)
    hbm = pl.BlockSpec(memory_space=pltpu.HBM)
    sets = max(1, min(SETS, MOST_SLOTS // (rows * CAP)))
    total_shape = (rows * CAP + 1, width, width)
    right_count = right_ops.shape[1]
    params = pltpu.CompilerParams(vmem_limit_bytes=12 * 2**20)

    def cost(share):
        flops = int(16 * operators * sectors * width**3 * share)
        return pl.CostEstimate(flops=flops, bytes_accessed=4 * 2**20, transcendentals=0)

    assert rows % 2 == 0
    quarter = operators // 4
    swap = [(i, i ^ 1) for i in range(rows)]

    def over_blocks(part):
        return [lax.ppermute(part, "blk", [((b + d) % blocks, b) for b in range(blocks)]) for d in range(1, blocks)]

    direct, middle = pl.pallas_call(
        cut_kernel,
        out_shape=[
            jax.ShapeDtypeStruct((count, *left_ops.shape[1:]), left_ops.dtype)
            for count in (quarter, operators - 2 * quarter)
        ],
        in_specs=[hbm],
        out_specs=[vmem] * 2,
        scratch_shapes=[pltpu.SemaphoreType.DMA((2,))],
        compiler_params=params,
        name="cut_left",
    )(pltpu.with_memory_space_constraint(left_ops, pltpu.HBM))
    direct, middle = over_blocks(direct), over_blocks(middle)

    half, plan = pl.pallas_call(
        functools.partial(right_kernel, blocks, left_local),
        out_shape=[
            jax.ShapeDtypeStruct((sectors // GROUP, operators, GROUP // 2, width, 2 * width), jnp.bfloat16),
            jax.ShapeDtypeStruct((sectors + 2 + blocks * left_local,), jnp.int32),
        ],
        in_specs=[hbm] * 4,
        out_specs=[vmem, smem],
        scratch_shapes=[
            pltpu.SMEM(left_qn.shape, jnp.int32),
            pltpu.SMEM(right_qn.shape, jnp.int32),
            pltpu.VMEM(psi.shape, psi.dtype),
            pltpu.VMEM(right_ops.shape, right_ops.dtype),
            pltpu.VMEM((sectors // 2, right_count * width, 2 * width), jnp.bfloat16),
            pltpu.SemaphoreType.DMA((3 + operators // BLOCK_K,)),
        ],
        compiler_params=params,
        cost_estimate=cost(0.5),
        name="right_side",
    )(*(pltpu.with_memory_space_constraint(x, pltpu.HBM) for x in (left_qn, right_qn, psi, right_ops)))
    half, direct = lax.optimization_barrier((half, direct))
    swapped = [lax.ppermute(part, "sector", swap) for part in direct]
    totals = pl.pallas_call(
        own_kernel,
        out_shape=[jax.ShapeDtypeStruct(total_shape, jnp.float32)] * sets,
        in_specs=[smem] * 2 + [vmem] * 3,
        out_specs=[vmem] * sets,
        compiler_params=params,
        cost_estimate=cost(0.25),
        name="own_left",
    )(plan, slots, half, left_ops, jnp.stack(direct))
    results = pl.pallas_call(
        functools.partial(other_kernel, rows, sets),
        out_shape=[jax.ShapeDtypeStruct(total_shape, jnp.float32)] * sets
        + [jax.ShapeDtypeStruct((rows * CAP // 2, width, width), kind) for kind in (jnp.float32, jnp.bfloat16)],
        in_specs=[smem] * 2 + [vmem] * (3 + sets),
        out_specs=[vmem] * (sets + 2),
        input_output_aliases={5 + j: j for j in range(sets)},
        compiler_params=params,
        cost_estimate=cost(0.25),
        name="other_left",
    )(plan, slots, half, jnp.stack(swapped), jnp.stack(middle), *totals)
    keep, give = results[sets:]

    def over_cores(block):
        return lax.ppermute(block, "op", [(h, halves - 1 - h) for h in range(halves)])

    partial = pl.pallas_call(
        combine_kernel,
        out_shape=[jax.ShapeDtypeStruct((CAP // 2 * width + TAIL, width), jnp.bfloat16)] * rows,
        in_specs=[smem] + [vmem] * 2,
        out_specs=[vmem] * rows,
        compiler_params=params,
        name="combine",
    )(slot_target, keep, over_cores(give))
    crossed = {
        d: lax.ppermute(partial[d], "sector", [(i, (i + d) % rows) for i in range(rows)]) for d in range(1, rows)
    }
    mine = [partial[0]] + [crossed[d] for d in range(1, rows)]
    theirs = [over_cores(block) for block in mine]
    return pl.pallas_call(
        functools.partial(assemble_kernel, rows),
        out_shape=jax.ShapeDtypeStruct((sectors, width, width), jnp.float32),
        in_specs=[vmem] * (2 * rows),
        out_specs=vmem,
        compiler_params=params,
        name="assemble",
    )(*mine, *theirs)


def solution(mesh):
    in_specs = (
        P(("groups", "sector", "blk"), None, None),
        P(("groups", "op"), "blk", None, None),
        P(("groups", "op"), None, None, None),
        P(("groups", "sector", "blk")),
        P(("groups", "sector", "blk")),
        P(("groups", "op"), ("sector", "blk")),
        P(("groups", "sector"), "blk", None),
    )
    out_specs = P(("groups", "sector", "blk"), None, None)
    sizes = tuple(mesh.shape[name] for name in ("sector", "blk", "op"))
    return jax.shard_map(
        functools.partial(shards, sizes), mesh=mesh, in_specs=in_specs, out_specs=out_specs, check_vma=False
    )
```

```python
import functools

import jax
import jax.numpy as jnp
from jax import lax
from jax.experimental import pallas as pl
from jax.experimental.pallas import tpu as pltpu
from jax.sharding import PartitionSpec as P

CAP = 4
GROUP = 4
SETS = 4
MOST_SLOTS = 64
BLOCK_K = 16
TAIL = 16
NT = (((1,), (1,)), ((), ()))


def arrange(left_qn, plan, blocks, left_local):
    mine = lax.axis_index("blk")
    count = left_qn.shape[0]

    def one_code(code, n):
        plan[count + 1 + code] = n
        owner = lax.rem(mine + lax.div(code, jnp.int32(left_local)), jnp.int32(blocks))
        wanted = owner * left_local + lax.rem(code, jnp.int32(left_local))

        def one_sector(s, n):
            plan[n] = s
            return n + (left_qn[s] == wanted).astype(jnp.int32)

        return lax.fori_loop(0, count, one_sector, n)

    plan[count + 1 + blocks * left_local] = lax.fori_loop(0, blocks * left_local, one_code, jnp.int32(0))


def cut_kernel(left, direct, middle, sems):
    quarter, count = direct.shape[0], middle.shape[0]
    first = lax.rem(lax.axis_index("sector"), jnp.int32(2)) * (left.shape[0] - quarter)
    copies = [
        pltpu.make_async_copy(left.at[pl.ds(first, quarter)], direct, sems.at[0]),
        pltpu.make_async_copy(left.at[pl.ds(quarter, count)], middle, sems.at[1]),
    ]
    for copy in copies:
        copy.start()
    for copy in copies:
        copy.wait()


def right_kernel(
    blocks, left_local, left_qn_in, right_qn_in, psi_in, right_in, half, plan,
    left_qn, right_qn, psi, right, sources, sems,
):
    sectors, width = psi.shape[0], psi.shape[1]
    right_count = right.shape[1]
    steps = right.shape[0] // BLOCK_K
    zero = jnp.zeros((width, width), jnp.bfloat16)

    def right_copy(i):
        at = pl.ds(i * BLOCK_K, BLOCK_K)
        return pltpu.make_async_copy(right_in.at[at], right.at[at], sems.at[3 + i])

    copies = [
        pltpu.make_async_copy(left_qn_in, left_qn, sems.at[0]),
        pltpu.make_async_copy(right_qn_in, right_qn, sems.at[1]),
        pltpu.make_async_copy(psi_in, psi, sems.at[2]),
    ]
    for copy in copies:
        copy.start()
    for i in range(steps):
        right_copy(i).start()
    copies[0].wait()
    copies[1].wait()
    arrange(left_qn, plan, blocks, left_local)
    copies[2].wait()
    for pair in range(sectors // 2):
        for e in range(2):
            s = plan[2 * pair + e]
            block = psi[s].T
            for r in range(right_count):
                sources[pair, r * width : (r + 1) * width, e * width : (e + 1) * width] = jnp.where(
                    right_qn[s] == r, block, zero
                )

    for i in range(steps):
        right_copy(i).wait()
    operators = right.shape[0]
    stream = jnp.concatenate([right[:, r].reshape(operators * width, width) for r in range(right_count)], axis=1)
    for pair in range(sectors // 2):
        product = jnp.dot(stream, sources[pair], preferred_element_type=jnp.float32)
        half[pair // 2, :, pair % 2] = product.astype(jnp.bfloat16).reshape(operators, width, 2 * width)


def accumulate(code, pieces, plan, slots, half, totals):
    sectors, width = slots.shape[0], totals[0].shape[1]
    spare = totals[0].shape[0] - 1
    low, high = plan[sectors + 1 + code], plan[sectors + 2 + code]
    zero = jnp.zeros((width, width), jnp.bfloat16)

    def terms(g, count):
        places = [g * GROUP + j for j in range(count * GROUP)]
        members = [plan[at] for at in places]
        counts = [(low <= at) & (at < high) for at in places]
        for first, left in pieces:
            for i in range(left.shape[0]):
                k = first + i
                block = left[i]
                weights = jnp.concatenate(
                    [jnp.concatenate([block, zero], axis=1), jnp.concatenate([zero, block], axis=1)], axis=0
                )
                term = lax.dot_general(
                    half[pl.ds(g, count), k].reshape(count * GROUP // 2 * width, 2 * width),
                    weights,
                    NT,
                    preferred_element_type=jnp.float32,
                )
                for j in range(count * GROUP):
                    p, e = j // 2, j % 2
                    slot = jnp.where(counts[j], slots[members[j], k], spare)
                    totals[j % len(totals)][slot] += term[
                        p * width : (p + 1) * width, e * width : (e + 1) * width
                    ]

    def two_groups(i, unused):
        terms(start + 2 * i, 2)
        return unused

    def last_group(i, unused):
        terms(start + groups - 1, 1)
        return unused

    start = lax.div(low, jnp.int32(GROUP))
    groups = jnp.where(low < high, lax.div(high + GROUP - 1, jnp.int32(GROUP)) - start, 0)
    lax.fori_loop(0, lax.div(groups, 2), two_groups, 0)
    lax.fori_loop(0, lax.rem(groups, 2), last_group, 0)


def own_kernel(plan, slots, half, left, direct, *totals):
    shifts, quarter, left_local = direct.shape[0], direct.shape[1], direct.shape[2]
    near = lax.rem(lax.axis_index("sector"), jnp.int32(2)) * (left.shape[0] - quarter)
    for total in totals:
        total[...] = jnp.zeros_like(total)
    for l in range(left_local):
        accumulate(l, [(0, left.at[:, l])], plan, slots, half, totals)

    def one_shift(d, unused):
        for l in range(left_local):
            accumulate((d + 1) * left_local + l, [(near, direct.at[d, :, l])], plan, slots, half, totals)
        return unused

    lax.fori_loop(0, shifts, one_shift, 0)


def other_kernel(rows, sets, plan, slots, half, swapped, middle, *rest):
    totals, (keep, give) = rest[sets : 2 * sets], rest[2 * sets :]
    shifts, quarter, left_local = swapped.shape[0], swapped.shape[1], swapped.shape[2]
    row, side = lax.axis_index("sector"), lax.axis_index("op")
    operators, width = slots.shape[1], totals[0].shape[1]
    far = (1 - lax.rem(row, jnp.int32(2))) * (operators - quarter)

    def one_shift(d, unused):
        for l in range(left_local):
            pieces = [(quarter, middle.at[d, :, l]), (far, swapped.at[d, :, l])]
            accumulate((d + 1) * left_local + l, pieces, plan, slots, half, totals)
        return unused

    lax.fori_loop(0, shifts, one_shift, 0)
    part = CAP // 2
    for owner in range(rows):
        for m in range(part):
            at = owner * CAP + side * part + m
            keep[owner * part + m] = sum(total[at] for total in totals)
            at = owner * CAP + (1 - side) * part + m
            give[owner * part + m] = sum(total[at] for total in totals).astype(jnp.bfloat16)


def combine_kernel(slot_target, keep, taken, *outs):
    part, width = CAP // 2, keep.shape[1]
    row, side = lax.axis_index("sector"), lax.axis_index("op")
    line = lax.broadcasted_iota(jnp.int32, (TAIL, width), 0)
    for d, out in enumerate(outs):
        owner = lax.rem(row + d, jnp.int32(len(outs)))
        ids = jnp.zeros((TAIL, width), jnp.int32)
        for m in range(part):
            block = keep[owner * part + m] + taken[owner * part + m].astype(jnp.float32)
            out[m * width : (m + 1) * width, :] = block.astype(jnp.bfloat16)
            ids = jnp.where(line == m, slot_target[0, 0, owner * CAP + side * part + m], ids)
        out[part * width :, :] = ids.astype(jnp.float32).astype(jnp.bfloat16)


def assemble_kernel(rows, *rest):
    mine, theirs, out = rest[:rows], rest[rows : 2 * rows], rest[-1]
    part, width = CAP // 2, out.shape[1]
    side = lax.axis_index("op")
    out[...] = jnp.zeros_like(out)
    for d in range(rows):
        for h in range(2):
            ids = jnp.where(side == h, mine[d][part * width :, :], theirs[d][part * width :, :]).astype(jnp.float32)
            for m in range(part):
                at = pl.ds(m * width, width)
                block = jnp.where(side == h, mine[d][at, :], theirs[d][at, :])
                target = jnp.max(ids[m : m + 1, :]).astype(jnp.int32)
                out[target] += block.T.astype(jnp.float32)


def shards(sizes, psi, left_ops, right_ops, left_qn, right_qn, pair_slot, slot_target):
    rows, blocks, halves = sizes
    sectors, width = psi.shape[0], psi.shape[1]
    operators, left_local = left_ops.shape[0], left_ops.shape[1]
    slots = pair_slot.T
    smem = pl.BlockSpec(memory_space=pltpu.SMEM)
    vmem = pl.BlockSpec(memory_space=pltpu.VMEM)
    hbm = pl.BlockSpec(memory_space=pltpu.HBM)
    sets = max(1, min(SETS, MOST_SLOTS // (rows * CAP)))
    total_shape = (rows * CAP + 1, width, width)
    right_count = right_ops.shape[1]
    params = pltpu.CompilerParams(vmem_limit_bytes=12 * 2**20)

    def cost(share):
        flops = int(16 * operators * sectors * width**3 * share)
        return pl.CostEstimate(flops=flops, bytes_accessed=4 * 2**20, transcendentals=0)

    assert rows % 2 == 0
    quarter = operators // 4
    swap = [(i, i ^ 1) for i in range(rows)]

    def over_blocks(part):
        return [lax.ppermute(part, "blk", [((b + d) % blocks, b) for b in range(blocks)]) for d in range(1, blocks)]

    direct, middle = pl.pallas_call(
        cut_kernel,
        out_shape=[
            jax.ShapeDtypeStruct((count, *left_ops.shape[1:]), left_ops.dtype)
            for count in (quarter, operators - 2 * quarter)
        ],
        in_specs=[hbm],
        out_specs=[vmem] * 2,
        scratch_shapes=[pltpu.SemaphoreType.DMA((2,))],
        compiler_params=params,
        name="cut_left",
    )(pltpu.with_memory_space_constraint(left_ops, pltpu.HBM))
    direct, middle = over_blocks(direct), over_blocks(middle)

    half, plan = pl.pallas_call(
        functools.partial(right_kernel, blocks, left_local),
        out_shape=[
            jax.ShapeDtypeStruct((sectors // GROUP, operators, GROUP // 2, width, 2 * width), jnp.bfloat16),
            jax.ShapeDtypeStruct((sectors + 2 + blocks * left_local,), jnp.int32),
        ],
        in_specs=[hbm] * 4,
        out_specs=[vmem, smem],
        scratch_shapes=[
            pltpu.SMEM(left_qn.shape, jnp.int32),
            pltpu.SMEM(right_qn.shape, jnp.int32),
            pltpu.VMEM(psi.shape, psi.dtype),
            pltpu.VMEM(right_ops.shape, right_ops.dtype),
            pltpu.VMEM((sectors // 2, right_count * width, 2 * width), jnp.bfloat16),
            pltpu.SemaphoreType.DMA((3 + operators // BLOCK_K,)),
        ],
        compiler_params=params,
        cost_estimate=cost(0.5),
        name="right_side",
    )(*(pltpu.with_memory_space_constraint(x, pltpu.HBM) for x in (left_qn, right_qn, psi, right_ops)))
    half, direct = lax.optimization_barrier((half, direct))
    swapped = [lax.ppermute(part, "sector", swap) for part in direct]
    totals = pl.pallas_call(
        own_kernel,
        out_shape=[jax.ShapeDtypeStruct(total_shape, jnp.float32)] * sets,
        in_specs=[smem] * 2 + [vmem] * 3,
        out_specs=[vmem] * sets,
        compiler_params=params,
        cost_estimate=cost(0.25),
        name="own_left",
    )(plan, slots, half, left_ops, jnp.stack(direct))
    results = pl.pallas_call(
        functools.partial(other_kernel, rows, sets),
        out_shape=[jax.ShapeDtypeStruct(total_shape, jnp.float32)] * sets
        + [jax.ShapeDtypeStruct((rows * CAP // 2, width, width), kind) for kind in (jnp.float32, jnp.bfloat16)],
        in_specs=[smem] * 2 + [vmem] * (3 + sets),
        out_specs=[vmem] * (sets + 2),
        input_output_aliases={5 + j: j for j in range(sets)},
        compiler_params=params,
        cost_estimate=cost(0.25),
        name="other_left",
    )(plan, slots, half, jnp.stack(swapped), jnp.stack(middle), *totals)
    keep, give = results[sets:]

    def over_cores(block):
        return lax.ppermute(block, "op", [(h, halves - 1 - h) for h in range(halves)])

    partial = pl.pallas_call(
        combine_kernel,
        out_shape=[jax.ShapeDtypeStruct((CAP // 2 * width + TAIL, width), jnp.bfloat16)] * rows,
        in_specs=[smem] + [vmem] * 2,
        out_specs=[vmem] * rows,
        compiler_params=params,
        name="combine",
    )(slot_target, keep, over_cores(give))
    crossed = {
        d: lax.ppermute(partial[d], "sector", [(i, (i + d) % rows) for i in range(rows)]) for d in range(1, rows)
    }
    mine = [partial[0]] + [crossed[d] for d in range(1, rows)]
    theirs = [over_cores(block) for block in mine]
    return pl.pallas_call(
        functools.partial(assemble_kernel, rows),
        out_shape=jax.ShapeDtypeStruct((sectors, width, width), jnp.float32),
        in_specs=[vmem] * (2 * rows),
        out_specs=vmem,
        compiler_params=params,
        name="assemble",
    )(*mine, *theirs)


def solution(mesh):
    in_specs = (
        P(("groups", "sector", "blk"), None, None),
        P(("groups", "op"), "blk", None, None),
        P(("groups", "op"), None, None, None),
        P(("groups", "sector", "blk")),
        P(("groups", "sector", "blk")),
        P(("groups", "op"), ("sector", "blk")),
        P(("groups", "sector"), "blk", None),
    )
    out_specs = P(("groups", "sector", "blk"), None, None)
    sizes = tuple(mesh.shape[name] for name in ("sector", "blk", "op"))
    return jax.shard_map(
        functools.partial(shards, sizes), mesh=mesh, in_specs=in_specs, out_specs=out_specs, check_vma=False
    )
```

```python
import functools

import jax
import jax.numpy as jnp
from jax import lax
from jax.experimental import pallas as pl
from jax.experimental.pallas import tpu as pltpu
from jax.sharding import PartitionSpec as P

CAP = 4
GROUP = 4
SETS = 4
MOST_SLOTS = 64
BLOCK_K = 16
TAIL = 16
NT = (((1,), (1,)), ((), ()))


def arrange(left_qn, plan, blocks, left_local):
    mine = lax.axis_index("blk")
    count = left_qn.shape[0]

    def one_code(code, n):
        plan[count + 1 + code] = n
        owner = lax.rem(mine + lax.div(code, jnp.int32(left_local)), jnp.int32(blocks))
        wanted = owner * left_local + lax.rem(code, jnp.int32(left_local))

        for s in range(count):
            plan[n] = jnp.int32(s)
            n = n + (left_qn[s] == wanted).astype(jnp.int32)
        return n

    plan[count + 1 + blocks * left_local] = lax.fori_loop(0, blocks * left_local, one_code, jnp.int32(0))


def cut_kernel(left, direct, middle, sems):
    quarter, count = direct.shape[0], middle.shape[0]
    first = lax.rem(lax.axis_index("sector"), jnp.int32(2)) * (left.shape[0] - quarter)
    copies = [
        pltpu.make_async_copy(left.at[pl.ds(first, quarter)], direct, sems.at[0]),
        pltpu.make_async_copy(left.at[pl.ds(quarter, count)], middle, sems.at[1]),
    ]
    for copy in copies:
        copy.start()
    for copy in copies:
        copy.wait()


def right_kernel(
    blocks, left_local, left_qn_in, right_qn_in, psi_in, right_in, half, plan,
    left_qn, right_qn, psi, right, sources, sems,
):
    sectors, width = psi.shape[0], psi.shape[1]
    right_count = right.shape[1]
    steps = right.shape[0] // BLOCK_K
    zero = jnp.zeros((width, width), jnp.bfloat16)

    def right_copy(i):
        at = pl.ds(i * BLOCK_K, BLOCK_K)
        return pltpu.make_async_copy(right_in.at[at], right.at[at], sems.at[3 + i])

    copies = [
        pltpu.make_async_copy(left_qn_in, left_qn, sems.at[0]),
        pltpu.make_async_copy(right_qn_in, right_qn, sems.at[1]),
        pltpu.make_async_copy(psi_in, psi, sems.at[2]),
    ]
    for copy in copies:
        copy.start()
    for i in range(steps):
        right_copy(i).start()
    copies[0].wait()
    copies[1].wait()
    arrange(left_qn, plan, blocks, left_local)
    copies[2].wait()
    for pair in range(sectors // 2):
        for e in range(2):
            s = plan[2 * pair + e]
            block = psi[s].T
            for r in range(right_count):
                sources[pair, r * width : (r + 1) * width, e * width : (e + 1) * width] = jnp.where(
                    right_qn[s] == r, block, zero
                )

    for i in range(steps):
        right_copy(i).wait()
    operators = right.shape[0]
    stream = jnp.concatenate([right[:, r].reshape(operators * width, width) for r in range(right_count)], axis=1)
    for pair in range(sectors // 2):
        product = jnp.dot(stream, sources[pair], preferred_element_type=jnp.float32)
        half[pair // 2, :, pair % 2] = product.astype(jnp.bfloat16).reshape(operators, width, 2 * width)


def accumulate(code, pieces, plan, slots, half, totals):
    sectors, width = slots.shape[0], totals[0].shape[1]
    spare = totals[0].shape[0] - 1
    low, high = plan[sectors + 1 + code], plan[sectors + 2 + code]
    zero = jnp.zeros((width, width), jnp.bfloat16)

    def terms(g, count):
        places = [g * GROUP + j for j in range(count * GROUP)]
        members = [plan[at] for at in places]
        counts = [(low <= at) & (at < high) for at in places]
        for first, left in pieces:
            for i in range(left.shape[0]):
                k = first + i
                block = left[i]
                weights = jnp.concatenate(
                    [jnp.concatenate([block, zero], axis=1), jnp.concatenate([zero, block], axis=1)], axis=0
                )
                term = lax.dot_general(
                    half[pl.ds(g, count), k].reshape(count * GROUP // 2 * width, 2 * width),
                    weights,
                    NT,
                    preferred_element_type=jnp.float32,
                )
                for j in range(count * GROUP):
                    p, e = j // 2, j % 2
                    slot = jnp.where(counts[j], slots[members[j], k], spare)
                    totals[j % len(totals)][slot] += term[
                        p * width : (p + 1) * width, e * width : (e + 1) * width
                    ]

    def two_groups(i, unused):
        terms(start + 2 * i, 2)
        return unused

    def last_group(i, unused):
        terms(start + groups - 1, 1)
        return unused

    start = lax.div(low, jnp.int32(GROUP))
    groups = jnp.where(low < high, lax.div(high + GROUP - 1, jnp.int32(GROUP)) - start, 0)
    lax.fori_loop(0, lax.div(groups, 2), two_groups, 0)
    lax.fori_loop(0, lax.rem(groups, 2), last_group, 0)


def own_kernel(plan, slots, half, left, direct, *totals):
    shifts, quarter, left_local = direct.shape[0], direct.shape[1], direct.shape[2]
    near = lax.rem(lax.axis_index("sector"), jnp.int32(2)) * (left.shape[0] - quarter)
    for total in totals:
        total[...] = jnp.zeros_like(total)
    for l in range(left_local):
        accumulate(l, [(0, left.at[:, l])], plan, slots, half, totals)

    def one_shift(d, unused):
        for l in range(left_local):
            accumulate((d + 1) * left_local + l, [(near, direct.at[d, :, l])], plan, slots, half, totals)
        return unused

    lax.fori_loop(0, shifts, one_shift, 0)


def other_kernel(rows, sets, plan, slots, half, swapped, middle, *rest):
    totals, (keep, give) = rest[sets : 2 * sets], rest[2 * sets :]
    shifts, quarter, left_local = swapped.shape[0], swapped.shape[1], swapped.shape[2]
    row, side = lax.axis_index("sector"), lax.axis_index("op")
    operators, width = slots.shape[1], totals[0].shape[1]
    far = (1 - lax.rem(row, jnp.int32(2))) * (operators - quarter)

    def one_shift(d, unused):
        for l in range(left_local):
            pieces = [(quarter, middle.at[d, :, l]), (far, swapped.at[d, :, l])]
            accumulate((d + 1) * left_local + l, pieces, plan, slots, half, totals)
        return unused

    lax.fori_loop(0, shifts, one_shift, 0)
    for j in range(rows // 2):
        mine = lax.bitwise_xor(row, j + (1 - side) * (rows // 2)) * CAP
        other = lax.bitwise_xor(row, j + side * (rows // 2)) * CAP
        for m in range(CAP):
            keep[j * CAP + m] = sum(total[mine + m] for total in totals)
            give[j * CAP + m] = sum(total[other + m] for total in totals).astype(jnp.bfloat16)


def combine_kernel(slot_target, keep, taken, *outs):
    width = keep.shape[1]
    row, side = lax.axis_index("sector"), lax.axis_index("op")
    line = lax.broadcasted_iota(jnp.int32, (TAIL, width), 0)
    for j, out in enumerate(outs):
        owner = lax.bitwise_xor(row, j + (1 - side) * len(outs))
        ids = jnp.zeros((TAIL, width), jnp.int32)
        for m in range(CAP):
            block = keep[j * CAP + m] + taken[j * CAP + m].astype(jnp.float32)
            out[m * width : (m + 1) * width, :] = block.astype(jnp.bfloat16)
            ids = jnp.where(line == m, slot_target[0, 0, owner * CAP + m], ids)
        out[CAP * width :, :] = ids.astype(jnp.float32).astype(jnp.bfloat16)


def assemble_kernel(*refs):
    count = len(refs) // 2
    mine, theirs, out = refs[:count], refs[count : 2 * count], refs[-1]
    width = out.shape[1]
    side = lax.axis_index("op")
    out[...] = jnp.zeros_like(out)
    for j in range(count):
        for h in range(2):
            tail = pl.ds(CAP * width, TAIL)
            ids = jnp.where(side == h, mine[j][tail, :], theirs[j][tail, :]).astype(jnp.float32)
            for m in range(CAP):
                at = pl.ds(m * width, width)
                block = jnp.where(side == h, mine[j][at, :], theirs[j][at, :])
                target = jnp.max(ids[m : m + 1, :]).astype(jnp.int32)
                out[target] += block.T.astype(jnp.float32)


def shards(sizes, psi, left_ops, right_ops, left_qn, right_qn, pair_slot, slot_target):
    rows, blocks, halves = sizes
    sectors, width = psi.shape[0], psi.shape[1]
    operators, left_local = left_ops.shape[0], left_ops.shape[1]
    slots = pair_slot.T
    smem = pl.BlockSpec(memory_space=pltpu.SMEM)
    vmem = pl.BlockSpec(memory_space=pltpu.VMEM)
    hbm = pl.BlockSpec(memory_space=pltpu.HBM)
    sets = max(1, min(SETS, MOST_SLOTS // (rows * CAP)))
    total_shape = (rows * CAP + 1, width, width)
    right_count = right_ops.shape[1]
    params = pltpu.CompilerParams(vmem_limit_bytes=12 * 2**20)

    def cost(share):
        flops = int(16 * operators * sectors * width**3 * share)
        return pl.CostEstimate(flops=flops, bytes_accessed=4 * 2**20, transcendentals=0)

    assert rows % 2 == 0 and rows & (rows - 1) == 0 and halves == 2
    quarter = operators // 4
    swap = [(i, i ^ 1) for i in range(rows)]

    def over_blocks(part):
        return [lax.ppermute(part, "blk", [((b + d) % blocks, b) for b in range(blocks)]) for d in range(1, blocks)]

    direct, middle = pl.pallas_call(
        cut_kernel,
        out_shape=[
            jax.ShapeDtypeStruct((count, *left_ops.shape[1:]), left_ops.dtype)
            for count in (quarter, operators - 2 * quarter)
        ],
        in_specs=[hbm],
        out_specs=[vmem] * 2,
        scratch_shapes=[pltpu.SemaphoreType.DMA((2,))],
        compiler_params=params,
        name="cut_left",
    )(pltpu.with_memory_space_constraint(left_ops, pltpu.HBM))
    direct, middle = over_blocks(direct), over_blocks(middle)

    half, plan = pl.pallas_call(
        functools.partial(right_kernel, blocks, left_local),
        out_shape=[
            jax.ShapeDtypeStruct((sectors // GROUP, operators, GROUP // 2, width, 2 * width), jnp.bfloat16),
            jax.ShapeDtypeStruct((sectors + 2 + blocks * left_local,), jnp.int32),
        ],
        in_specs=[hbm] * 4,
        out_specs=[vmem, smem],
        scratch_shapes=[
            pltpu.SMEM(left_qn.shape, jnp.int32),
            pltpu.SMEM(right_qn.shape, jnp.int32),
            pltpu.VMEM(psi.shape, psi.dtype),
            pltpu.VMEM(right_ops.shape, right_ops.dtype),
            pltpu.VMEM((sectors // 2, right_count * width, 2 * width), jnp.bfloat16),
            pltpu.SemaphoreType.DMA((3 + operators // BLOCK_K,)),
        ],
        compiler_params=params,
        cost_estimate=cost(0.5),
        name="right_side",
    )(*(pltpu.with_memory_space_constraint(x, pltpu.HBM) for x in (left_qn, right_qn, psi, right_ops)))
    half, direct = lax.optimization_barrier((half, direct))
    swapped = [lax.ppermute(part, "sector", swap) for part in direct]
    totals = pl.pallas_call(
        own_kernel,
        out_shape=[jax.ShapeDtypeStruct(total_shape, jnp.float32)] * sets,
        in_specs=[smem] * 2 + [vmem] * 3,
        out_specs=[vmem] * sets,
        compiler_params=params,
        cost_estimate=cost(0.25),
        name="own_left",
    )(plan, slots, half, left_ops, jnp.stack(direct))
    results = pl.pallas_call(
        functools.partial(other_kernel, rows, sets),
        out_shape=[jax.ShapeDtypeStruct(total_shape, jnp.float32)] * sets
        + [jax.ShapeDtypeStruct((rows * CAP // 2, width, width), kind) for kind in (jnp.float32, jnp.bfloat16)],
        in_specs=[smem] * 2 + [vmem] * (3 + sets),
        out_specs=[vmem] * (sets + 2),
        input_output_aliases={5 + j: j for j in range(sets)},
        compiler_params=params,
        cost_estimate=cost(0.25),
        name="other_left",
    )(plan, slots, half, jnp.stack(swapped), jnp.stack(middle), *totals)
    keep, give = results[sets:]

    def over_cores(block):
        return lax.ppermute(block, "op", [(h, halves - 1 - h) for h in range(halves)])

    partial = pl.pallas_call(
        combine_kernel,
        out_shape=[jax.ShapeDtypeStruct((CAP * width + TAIL, width), jnp.bfloat16)] * (rows // 2),
        in_specs=[smem] + [vmem] * 2,
        out_specs=[vmem] * (rows // 2),
        compiler_params=params,
        name="combine",
    )(slot_target, keep, over_cores(give))
    def over_rows(block, j):
        goals = [(i, h, i ^ (j + (1 - h) * (rows // 2))) for i in range(rows) for h in range(halves)]
        return lax.ppermute(block, ("sector", "op"), [(i * halves + h, goal * halves + h) for i, h, goal in goals])

    mine = [over_rows(block, j) for j, block in enumerate(partial)]
    theirs = [over_cores(block) for block in mine]
    return pl.pallas_call(
        assemble_kernel,
        out_shape=jax.ShapeDtypeStruct((sectors, width, width), jnp.float32),
        in_specs=[vmem] * rows,
        out_specs=vmem,
        compiler_params=params,
        name="assemble",
    )(*mine, *theirs)


def solution(mesh):
    in_specs = (
        P(("groups", "sector", "blk"), None, None),
        P(("groups", "op"), "blk", None, None),
        P(("groups", "op"), None, None, None),
        P(("groups", "sector", "blk")),
        P(("groups", "sector", "blk")),
        P(("groups", "op"), ("sector", "blk")),
        P(("groups", "sector"), "blk", None),
    )
    out_specs = P(("groups", "sector", "blk"), None, None)
    sizes = tuple(mesh.shape[name] for name in ("sector", "blk", "op"))
    return jax.shard_map(
        functools.partial(shards, sizes), mesh=mesh, in_specs=in_specs, out_specs=out_specs, check_vma=False
    )
```

```python
import functools

import jax
import jax.numpy as jnp
from jax import lax
from jax.experimental import pallas as pl
from jax.experimental.pallas import tpu as pltpu
from jax.sharding import PartitionSpec as P

CAP = 4
GROUP = 4
SETS = 4
MOST_SLOTS = 64
BLOCK_K = 16
TAIL = 16
NT = (((1,), (1,)), ((), ()))


def arrange(left_qn, plan, blocks, left_local):
    mine = lax.axis_index("blk")
    count = left_qn.shape[0]

    def one_code(code, n):
        plan[count + 1 + code] = n
        owner = lax.rem(mine + lax.div(code, jnp.int32(left_local)), jnp.int32(blocks))
        wanted = owner * left_local + lax.rem(code, jnp.int32(left_local))

        for s in range(count):
            plan[n] = jnp.int32(s)
            n = n + (left_qn[s] == wanted).astype(jnp.int32)
        return n

    plan[count + 1 + blocks * left_local] = lax.fori_loop(0, blocks * left_local, one_code, jnp.int32(0))


def cut_kernel(left, direct, middle, sems):
    quarter, count = direct.shape[0], middle.shape[0]
    first = lax.rem(lax.axis_index("sector"), jnp.int32(2)) * (left.shape[0] - quarter)
    copies = [
        pltpu.make_async_copy(left.at[pl.ds(first, quarter)], direct, sems.at[0]),
        pltpu.make_async_copy(left.at[pl.ds(quarter, count)], middle, sems.at[1]),
    ]
    for copy in copies:
        copy.start()
    for copy in copies:
        copy.wait()


def right_kernel(
    blocks, left_local, left_qn_in, right_qn_in, psi_in, right_in, half, plan,
    left_qn, right_qn, psi, right, sources, sems,
):
    sectors, width = psi.shape[0], psi.shape[1]
    right_count = right.shape[1]
    steps = right.shape[0] // BLOCK_K
    zero = jnp.zeros((width, width), jnp.bfloat16)

    def right_copy(i):
        at = pl.ds(i * BLOCK_K, BLOCK_K)
        return pltpu.make_async_copy(right_in.at[at], right.at[at], sems.at[3 + i])

    copies = [
        pltpu.make_async_copy(left_qn_in, left_qn, sems.at[0]),
        pltpu.make_async_copy(right_qn_in, right_qn, sems.at[1]),
        pltpu.make_async_copy(psi_in, psi, sems.at[2]),
    ]
    for copy in copies:
        copy.start()
    for i in range(steps):
        right_copy(i).start()
    copies[0].wait()
    copies[1].wait()
    arrange(left_qn, plan, blocks, left_local)
    copies[2].wait()
    for pair in range(sectors // 2):
        for e in range(2):
            s = plan[2 * pair + e]
            block = psi[s].T
            for r in range(right_count):
                sources[pair, r * width : (r + 1) * width, e * width : (e + 1) * width] = jnp.where(
                    right_qn[s] == r, block, zero
                )

    for i in range(steps):
        right_copy(i).wait()
    operators = right.shape[0]
    stream = jnp.concatenate([right[:, r].reshape(operators * width, width) for r in range(right_count)], axis=1)
    for pair in range(sectors // 2):
        product = jnp.dot(stream, sources[pair], preferred_element_type=jnp.float32)
        half[pair // 2, :, pair % 2] = product.astype(jnp.bfloat16).reshape(operators, width, 2 * width)


def accumulate(code, pieces, plan, slots, half, totals):
    sectors, width = slots.shape[0], totals[0].shape[1]
    spare = totals[0].shape[0] - 1
    low, high = plan[sectors + 1 + code], plan[sectors + 2 + code]
    zero = jnp.zeros((width, width), jnp.bfloat16)

    def terms(g, count):
        places = [g * GROUP + j for j in range(count * GROUP)]
        members = [plan[at] for at in places]
        counts = [(low <= at) & (at < high) for at in places]
        for first, left in pieces:
            for i in range(left.shape[0]):
                k = first + i
                block = left[i]
                weights = jnp.concatenate(
                    [jnp.concatenate([block, zero], axis=1), jnp.concatenate([zero, block], axis=1)], axis=0
                )
                term = lax.dot_general(
                    half[pl.ds(g, count), k].reshape(count * GROUP // 2 * width, 2 * width),
                    weights,
                    NT,
                    preferred_element_type=jnp.float32,
                )
                for j in range(count * GROUP):
                    p, e = j // 2, j % 2
                    slot = jnp.where(counts[j], slots[members[j], k], spare)
                    totals[j % len(totals)][slot] += term[
                        p * width : (p + 1) * width, e * width : (e + 1) * width
                    ]

    def two_groups(i, unused):
        terms(start + 2 * i, 2)
        return unused

    def last_group(i, unused):
        terms(start + groups - 1, 1)
        return unused

    start = lax.div(low, jnp.int32(GROUP))
    groups = jnp.where(low < high, lax.div(high + GROUP - 1, jnp.int32(GROUP)) - start, 0)
    lax.fori_loop(0, lax.div(groups, 2), two_groups, 0)
    lax.fori_loop(0, lax.rem(groups, 2), last_group, 0)


def own_kernel(plan, slots, half, left, direct, *totals):
    shifts, quarter, left_local = direct.shape[0], direct.shape[1], direct.shape[2]
    near = lax.rem(lax.axis_index("sector"), jnp.int32(2)) * (left.shape[0] - quarter)
    for total in totals:
        total[...] = jnp.zeros_like(total)
    for l in range(left_local):
        accumulate(l, [(0, left.at[:, l])], plan, slots, half, totals)

    def one_shift(d, unused):
        for l in range(left_local):
            accumulate((d + 1) * left_local + l, [(near, direct.at[d, :, l])], plan, slots, half, totals)
        return unused

    lax.fori_loop(0, shifts, one_shift, 0)


def other_kernel(rows, sets, plan, slots, half, swapped, middle, *rest):
    totals, (keep, give) = rest[sets : 2 * sets], rest[2 * sets :]
    shifts, quarter, left_local = swapped.shape[0], swapped.shape[1], swapped.shape[2]
    row, side = lax.axis_index("sector"), lax.axis_index("op")
    operators, width = slots.shape[1], totals[0].shape[1]
    far = (1 - lax.rem(row, jnp.int32(2))) * (operators - quarter)

    def one_shift(d, unused):
        for l in range(left_local):
            pieces = [(quarter, middle.at[d, :, l]), (far, swapped.at[d, :, l])]
            accumulate((d + 1) * left_local + l, pieces, plan, slots, half, totals)
        return unused

    lax.fori_loop(0, shifts, one_shift, 0)
    part = CAP // 2
    for owner in range(rows):
        for m in range(part):
            at = owner * CAP + side * part + m
            keep[owner * part + m] = sum(total[at] for total in totals)
            at = owner * CAP + (1 - side) * part + m
            give[owner * part + m] = sum(total[at] for total in totals).astype(jnp.bfloat16)


def combine_kernel(shifts, slot_target, keep, taken, *outs):
    part, width = CAP // 2, keep.shape[1]
    row, side = lax.axis_index("sector"), lax.axis_index("op")
    line = lax.broadcasted_iota(jnp.int32, (TAIL, width), 0)
    for d, out in zip(shifts, outs):
        owner = lax.rem(row + d, jnp.int32(len(outs)))
        ids = jnp.zeros((TAIL, width), jnp.int32)
        for m in range(part):
            block = keep[owner * part + m] + taken[owner * part + m].astype(jnp.float32)
            out[m * width : (m + 1) * width, :] = block.astype(jnp.bfloat16)
            ids = jnp.where(line == m, slot_target[0, 0, owner * CAP + side * part + m], ids)
        out[part * width :, :] = ids.astype(jnp.float32).astype(jnp.bfloat16)


def assemble_kernel(rows, *rest):
    mine, theirs, out = rest[:rows], rest[rows : 2 * rows], rest[-1]
    part, width = CAP // 2, out.shape[1]
    side = lax.axis_index("op")
    out[...] = jnp.zeros_like(out)
    for d in range(rows):
        for h in range(2):
            ids = jnp.where(side == h, mine[d][part * width :, :], theirs[d][part * width :, :]).astype(jnp.float32)
            for m in range(part):
                at = pl.ds(m * width, width)
                block = jnp.where(side == h, mine[d][at, :], theirs[d][at, :])
                target = jnp.max(ids[m : m + 1, :]).astype(jnp.int32)
                out[target] += block.T.astype(jnp.float32)


def shards(sizes, psi, left_ops, right_ops, left_qn, right_qn, pair_slot, slot_target):
    rows, blocks, halves = sizes
    sectors, width = psi.shape[0], psi.shape[1]
    operators, left_local = left_ops.shape[0], left_ops.shape[1]
    slots = pair_slot.T
    smem = pl.BlockSpec(memory_space=pltpu.SMEM)
    vmem = pl.BlockSpec(memory_space=pltpu.VMEM)
    hbm = pl.BlockSpec(memory_space=pltpu.HBM)
    sets = max(1, min(SETS, MOST_SLOTS // (rows * CAP)))
    total_shape = (rows * CAP + 1, width, width)
    right_count = right_ops.shape[1]
    params = pltpu.CompilerParams(vmem_limit_bytes=12 * 2**20)

    def cost(share):
        flops = int(16 * operators * sectors * width**3 * share)
        return pl.CostEstimate(flops=flops, bytes_accessed=4 * 2**20, transcendentals=0)

    assert rows % 2 == 0
    quarter = operators // 4
    swap = [(i, i ^ 1) for i in range(rows)]

    def over_blocks(part):
        return [lax.ppermute(part, "blk", [((b + d) % blocks, b) for b in range(blocks)]) for d in range(1, blocks)]

    direct, middle = pl.pallas_call(
        cut_kernel,
        out_shape=[
            jax.ShapeDtypeStruct((count, *left_ops.shape[1:]), left_ops.dtype)
            for count in (quarter, operators - 2 * quarter)
        ],
        in_specs=[hbm],
        out_specs=[vmem] * 2,
        scratch_shapes=[pltpu.SemaphoreType.DMA((2,))],
        compiler_params=params,
        name="cut_left",
    )(pltpu.with_memory_space_constraint(left_ops, pltpu.HBM))
    direct, middle = over_blocks(direct), over_blocks(middle)

    half, plan = pl.pallas_call(
        functools.partial(right_kernel, blocks, left_local),
        out_shape=[
            jax.ShapeDtypeStruct((sectors // GROUP, operators, GROUP // 2, width, 2 * width), jnp.bfloat16),
            jax.ShapeDtypeStruct((sectors + 2 + blocks * left_local,), jnp.int32),
        ],
        in_specs=[hbm] * 4,
        out_specs=[vmem, smem],
        scratch_shapes=[
            pltpu.SMEM(left_qn.shape, jnp.int32),
            pltpu.SMEM(right_qn.shape, jnp.int32),
            pltpu.VMEM(psi.shape, psi.dtype),
            pltpu.VMEM(right_ops.shape, right_ops.dtype),
            pltpu.VMEM((sectors // 2, right_count * width, 2 * width), jnp.bfloat16),
            pltpu.SemaphoreType.DMA((3 + operators // BLOCK_K,)),
        ],
        compiler_params=params,
        cost_estimate=cost(0.5),
        name="right_side",
    )(*(pltpu.with_memory_space_constraint(x, pltpu.HBM) for x in (left_qn, right_qn, psi, right_ops)))
    half, direct = lax.optimization_barrier((half, direct))
    swapped = [lax.ppermute(part, "sector", swap) for part in direct]
    totals = pl.pallas_call(
        own_kernel,
        out_shape=[jax.ShapeDtypeStruct(total_shape, jnp.float32)] * sets,
        in_specs=[smem] * 2 + [vmem] * 3,
        out_specs=[vmem] * sets,
        compiler_params=params,
        cost_estimate=cost(0.25),
        name="own_left",
    )(plan, slots, half, left_ops, jnp.stack(direct))
    results = pl.pallas_call(
        functools.partial(other_kernel, rows, sets),
        out_shape=[jax.ShapeDtypeStruct(total_shape, jnp.float32)] * sets
        + [jax.ShapeDtypeStruct((rows * CAP // 2, width, width), kind) for kind in (jnp.float32, jnp.bfloat16)],
        in_specs=[smem] * 2 + [vmem] * (3 + sets),
        out_specs=[vmem] * (sets + 2),
        input_output_aliases={5 + j: j for j in range(sets)},
        compiler_params=params,
        cost_estimate=cost(0.25),
        name="other_left",
    )(plan, slots, half, jnp.stack(swapped), jnp.stack(middle), *totals)
    keep, give = results[sets:]

    def over_cores(block):
        return lax.ppermute(block, "op", [(h, halves - 1 - h) for h in range(halves)])

    shifts = sorted(range(1, rows), key=lambda d: (abs(d - rows // 2), d)) + [0]
    partial = pl.pallas_call(
        functools.partial(combine_kernel, shifts),
        out_shape=[jax.ShapeDtypeStruct((CAP // 2 * width + TAIL, width), jnp.bfloat16)] * rows,
        in_specs=[smem] + [vmem] * 2,
        out_specs=[vmem] * rows,
        compiler_params=params,
        name="combine",
    )(slot_target, keep, over_cores(give))
    mine = [
        lax.ppermute(block, "sector", [(i, (i + d) % rows) for i in range(rows)]) if d else block
        for d, block in zip(shifts, partial)
    ]
    theirs = [over_cores(block) for block in mine]
    return pl.pallas_call(
        functools.partial(assemble_kernel, rows),
        out_shape=jax.ShapeDtypeStruct((sectors, width, width), jnp.float32),
        in_specs=[vmem] * (2 * rows),
        out_specs=vmem,
        compiler_params=params,
        name="assemble",
    )(*mine, *theirs)


def solution(mesh):
    in_specs = (
        P(("groups", "sector", "blk"), None, None),
        P(("groups", "op"), "blk", None, None),
        P(("groups", "op"), None, None, None),
        P(("groups", "sector", "blk")),
        P(("groups", "sector", "blk")),
        P(("groups", "op"), ("sector", "blk")),
        P(("groups", "sector"), "blk", None),
    )
    out_specs = P(("groups", "sector", "blk"), None, None)
    sizes = tuple(mesh.shape[name] for name in ("sector", "blk", "op"))
    return jax.shard_map(
        functools.partial(shards, sizes), mesh=mesh, in_specs=in_specs, out_specs=out_specs, check_vma=False
    )
```

```python
import functools

import jax
import jax.numpy as jnp
from jax import lax
from jax.experimental import pallas as pl
from jax.experimental.pallas import tpu as pltpu
from jax.sharding import PartitionSpec as P

CAP = 4
GROUP = 4
SETS = 4
MOST_SLOTS = 64
BLOCK_K = 16
TAIL = 16
NT = (((1,), (1,)), ((), ()))


def arrange(left_qn, plan, blocks, left_local):
    mine = lax.axis_index("blk")
    count = left_qn.shape[0]

    def one_code(code, n):
        plan[count + 1 + code] = n
        owner = lax.rem(mine + lax.div(code, jnp.int32(left_local)), jnp.int32(blocks))
        wanted = owner * left_local + lax.rem(code, jnp.int32(left_local))

        for s in range(count):
            plan[n] = jnp.int32(s)
            n = n + (left_qn[s] == wanted).astype(jnp.int32)
        return n

    plan[count + 1 + blocks * left_local] = lax.fori_loop(0, blocks * left_local, one_code, jnp.int32(0))


def cut_kernel(left, direct, middle, sems):
    quarter, count = direct.shape[0], middle.shape[0]
    first = lax.rem(lax.axis_index("sector"), jnp.int32(2)) * (left.shape[0] - quarter)
    copies = [
        pltpu.make_async_copy(left.at[pl.ds(first, quarter)], direct, sems.at[0]),
        pltpu.make_async_copy(left.at[pl.ds(quarter, count)], middle, sems.at[1]),
    ]
    for copy in copies:
        copy.start()
    for copy in copies:
        copy.wait()


def right_kernel(
    blocks, left_local, left_qn_in, right_qn_in, psi_in, right_in, half, plan,
    left_qn, right_qn, psi, right, sources, sems,
):
    sectors, width = psi.shape[0], psi.shape[1]
    right_count = right.shape[1]
    steps = right.shape[0] // BLOCK_K
    zero = jnp.zeros((width, width), jnp.bfloat16)

    def right_copy(i):
        at = pl.ds(i * BLOCK_K, BLOCK_K)
        return pltpu.make_async_copy(right_in.at[at], right.at[at], sems.at[3 + i])

    copies = [
        pltpu.make_async_copy(left_qn_in, left_qn, sems.at[0]),
        pltpu.make_async_copy(right_qn_in, right_qn, sems.at[1]),
        pltpu.make_async_copy(psi_in, psi, sems.at[2]),
    ]
    for copy in copies:
        copy.start()
    for i in range(steps):
        right_copy(i).start()
    copies[0].wait()
    copies[1].wait()
    arrange(left_qn, plan, blocks, left_local)
    copies[2].wait()
    for pair in range(sectors // 2):
        for e in range(2):
            s = plan[2 * pair + e]
            block = psi[s].T
            for r in range(right_count):
                sources[pair, r * width : (r + 1) * width, e * width : (e + 1) * width] = jnp.where(
                    right_qn[s] == r, block, zero
                )

    def one_step(i, unused):
        right_copy(i).wait()
        at = pl.ds(i * BLOCK_K, BLOCK_K)
        stream = jnp.concatenate([right[at, r].reshape(BLOCK_K * width, width) for r in range(right_count)], axis=1)
        for pair in range(sectors // 2):
            product = jnp.dot(stream, sources[pair], preferred_element_type=jnp.float32)
            half[pair // 2, at, pair % 2] = product.astype(jnp.bfloat16).reshape(BLOCK_K, width, 2 * width)
        return unused

    lax.fori_loop(0, steps, one_step, 0)


def accumulate(code, pieces, plan, slots, half, totals):
    sectors, width = slots.shape[0], totals[0].shape[1]
    spare = totals[0].shape[0] - 1
    low, high = plan[sectors + 1 + code], plan[sectors + 2 + code]
    zero = jnp.zeros((width, width), jnp.bfloat16)

    def terms(g, count):
        places = [g * GROUP + j for j in range(count * GROUP)]
        members = [plan[at] for at in places]
        counts = [(low <= at) & (at < high) for at in places]
        for first, left in pieces:
            for i in range(left.shape[0]):
                k = first + i
                block = left[i]
                weights = jnp.concatenate(
                    [jnp.concatenate([block, zero], axis=1), jnp.concatenate([zero, block], axis=1)], axis=0
                )
                term = lax.dot_general(
                    half[pl.ds(g, count), k].reshape(count * GROUP // 2 * width, 2 * width),
                    weights,
                    NT,
                    preferred_element_type=jnp.float32,
                )
                for j in range(count * GROUP):
                    p, e = j // 2, j % 2
                    slot = jnp.where(counts[j], slots[members[j], k], spare)
                    totals[j % len(totals)][slot] += term[
                        p * width : (p + 1) * width, e * width : (e + 1) * width
                    ]

    def two_groups(i, unused):
        terms(start + 2 * i, 2)
        return unused

    def last_group(i, unused):
        terms(start + groups - 1, 1)
        return unused

    start = lax.div(low, jnp.int32(GROUP))
    groups = jnp.where(low < high, lax.div(high + GROUP - 1, jnp.int32(GROUP)) - start, 0)
    lax.fori_loop(0, lax.div(groups, 2), two_groups, 0)
    lax.fori_loop(0, lax.rem(groups, 2), last_group, 0)


def own_kernel(plan, slots, half, left, direct, *totals):
    shifts, quarter, left_local = direct.shape[0], direct.shape[1], direct.shape[2]
    near = lax.rem(lax.axis_index("sector"), jnp.int32(2)) * (left.shape[0] - quarter)
    for total in totals:
        total[...] = jnp.zeros_like(total)
    for l in range(left_local):
        accumulate(l, [(0, left.at[:, l])], plan, slots, half, totals)

    def one_shift(d, unused):
        for l in range(left_local):
            accumulate((d + 1) * left_local + l, [(near, direct.at[d, :, l])], plan, slots, half, totals)
        return unused

    lax.fori_loop(0, shifts, one_shift, 0)


def other_kernel(rows, sets, plan, slots, half, swapped, middle, *rest):
    totals, (keep, give) = rest[sets : 2 * sets], rest[2 * sets :]
    shifts, quarter, left_local = swapped.shape[0], swapped.shape[1], swapped.shape[2]
    row, side = lax.axis_index("sector"), lax.axis_index("op")
    operators, width = slots.shape[1], totals[0].shape[1]
    far = (1 - lax.rem(row, jnp.int32(2))) * (operators - quarter)

    def one_shift(d, unused):
        for l in range(left_local):
            pieces = [(quarter, middle.at[d, :, l]), (far, swapped.at[d, :, l])]
            accumulate((d + 1) * left_local + l, pieces, plan, slots, half, totals)
        return unused

    lax.fori_loop(0, shifts, one_shift, 0)
    part = CAP // 2
    for owner in range(rows):
        for m in range(part):
            at = owner * CAP + side * part + m
            keep[owner * part + m] = sum(total[at] for total in totals)
            at = owner * CAP + (1 - side) * part + m
            give[owner * part + m] = sum(total[at] for total in totals).astype(jnp.bfloat16)


def combine_kernel(shifts, slot_target, keep, taken, *outs):
    part, width = CAP // 2, keep.shape[1]
    row, side = lax.axis_index("sector"), lax.axis_index("op")
    line = lax.broadcasted_iota(jnp.int32, (TAIL, width), 0)
    for d, out in zip(shifts, outs):
        owner = lax.rem(row + d, jnp.int32(len(outs)))
        ids = jnp.zeros((TAIL, width), jnp.int32)
        for m in range(part):
            block = keep[owner * part + m] + taken[owner * part + m].astype(jnp.float32)
            out[m * width : (m + 1) * width, :] = block.astype(jnp.bfloat16)
            ids = jnp.where(line == m, slot_target[0, 0, owner * CAP + side * part + m], ids)
        out[part * width :, :] = ids.astype(jnp.float32).astype(jnp.bfloat16)


def assemble_kernel(rows, *rest):
    mine, theirs, out = rest[:rows], rest[rows : 2 * rows], rest[-1]
    part, width = CAP // 2, out.shape[1]
    side = lax.axis_index("op")
    out[...] = jnp.zeros_like(out)
    for d in range(rows):
        for h in range(2):
            ids = jnp.where(side == h, mine[d][part * width :, :], theirs[d][part * width :, :]).astype(jnp.float32)
            for m in range(part):
                at = pl.ds(m * width, width)
                block = jnp.where(side == h, mine[d][at, :], theirs[d][at, :])
                target = jnp.max(ids[m : m + 1, :]).astype(jnp.int32)
                out[target] += block.T.astype(jnp.float32)


def shards(sizes, psi, left_ops, right_ops, left_qn, right_qn, pair_slot, slot_target):
    rows, blocks, halves = sizes
    sectors, width = psi.shape[0], psi.shape[1]
    operators, left_local = left_ops.shape[0], left_ops.shape[1]
    slots = pair_slot.T
    smem = pl.BlockSpec(memory_space=pltpu.SMEM)
    vmem = pl.BlockSpec(memory_space=pltpu.VMEM)
    hbm = pl.BlockSpec(memory_space=pltpu.HBM)
    sets = max(1, min(SETS, MOST_SLOTS // (rows * CAP)))
    total_shape = (rows * CAP + 1, width, width)
    right_count = right_ops.shape[1]
    params = pltpu.CompilerParams(vmem_limit_bytes=12 * 2**20)

    def cost(share):
        flops = int(16 * operators * sectors * width**3 * share)
        return pl.CostEstimate(flops=flops, bytes_accessed=4 * 2**20, transcendentals=0)

    assert rows % 2 == 0
    quarter = operators // 4
    swap = [(i, i ^ 1) for i in range(rows)]

    def over_blocks(part):
        return [lax.ppermute(part, "blk", [((b + d) % blocks, b) for b in range(blocks)]) for d in range(1, blocks)]

    direct, middle = pl.pallas_call(
        cut_kernel,
        out_shape=[
            jax.ShapeDtypeStruct((count, *left_ops.shape[1:]), left_ops.dtype)
            for count in (quarter, operators - 2 * quarter)
        ],
        in_specs=[hbm],
        out_specs=[vmem] * 2,
        scratch_shapes=[pltpu.SemaphoreType.DMA((2,))],
        compiler_params=params,
        name="cut_left",
    )(pltpu.with_memory_space_constraint(left_ops, pltpu.HBM))
    direct, middle = over_blocks(direct), over_blocks(middle)

    half, plan = pl.pallas_call(
        functools.partial(right_kernel, blocks, left_local),
        out_shape=[
            jax.ShapeDtypeStruct((sectors // GROUP, operators, GROUP // 2, width, 2 * width), jnp.bfloat16),
            jax.ShapeDtypeStruct((sectors + 2 + blocks * left_local,), jnp.int32),
        ],
        in_specs=[hbm] * 4,
        out_specs=[vmem, smem],
        scratch_shapes=[
            pltpu.SMEM(left_qn.shape, jnp.int32),
            pltpu.SMEM(right_qn.shape, jnp.int32),
            pltpu.VMEM(psi.shape, psi.dtype),
            pltpu.VMEM(right_ops.shape, right_ops.dtype),
            pltpu.VMEM((sectors // 2, right_count * width, 2 * width), jnp.bfloat16),
            pltpu.SemaphoreType.DMA((3 + operators // BLOCK_K,)),
        ],
        compiler_params=params,
        cost_estimate=cost(0.5),
        name="right_side",
    )(*(pltpu.with_memory_space_constraint(x, pltpu.HBM) for x in (left_qn, right_qn, psi, right_ops)))
    half, direct = lax.optimization_barrier((half, direct))
    swapped = [lax.ppermute(part, "sector", swap) for part in direct]
    totals = pl.pallas_call(
        own_kernel,
        out_shape=[jax.ShapeDtypeStruct(total_shape, jnp.float32)] * sets,
        in_specs=[smem] * 2 + [vmem] * 3,
        out_specs=[vmem] * sets,
        compiler_params=params,
        cost_estimate=cost(0.25),
        name="own_left",
    )(plan, slots, half, left_ops, jnp.stack(direct))
    results = pl.pallas_call(
        functools.partial(other_kernel, rows, sets),
        out_shape=[jax.ShapeDtypeStruct(total_shape, jnp.float32)] * sets
        + [jax.ShapeDtypeStruct((rows * CAP // 2, width, width), kind) for kind in (jnp.float32, jnp.bfloat16)],
        in_specs=[smem] * 2 + [vmem] * (3 + sets),
        out_specs=[vmem] * (sets + 2),
        input_output_aliases={5 + j: j for j in range(sets)},
        compiler_params=params,
        cost_estimate=cost(0.25),
        name="other_left",
    )(plan, slots, half, jnp.stack(swapped), jnp.stack(middle), *totals)
    keep, give = results[sets:]

    def over_cores(block):
        return lax.ppermute(block, "op", [(h, halves - 1 - h) for h in range(halves)])

    shifts = sorted(range(1, rows), key=lambda d: (abs(d - rows // 2), d)) + [0]
    partial = pl.pallas_call(
        functools.partial(combine_kernel, shifts),
        out_shape=[jax.ShapeDtypeStruct((CAP // 2 * width + TAIL, width), jnp.bfloat16)] * rows,
        in_specs=[smem] + [vmem] * 2,
        out_specs=[vmem] * rows,
        compiler_params=params,
        name="combine",
    )(slot_target, keep, over_cores(give))
    mine = [
        lax.ppermute(block, "sector", [(i, (i + d) % rows) for i in range(rows)]) if d else block
        for d, block in zip(shifts, partial)
    ]
    theirs = [over_cores(block) for block in mine]
    return pl.pallas_call(
        functools.partial(assemble_kernel, rows),
        out_shape=jax.ShapeDtypeStruct((sectors, width, width), jnp.float32),
        in_specs=[vmem] * (2 * rows),
        out_specs=vmem,
        compiler_params=params,
        name="assemble",
    )(*mine, *theirs)


def solution(mesh):
    in_specs = (
        P(("groups", "sector", "blk"), None, None),
        P(("groups", "op"), "blk", None, None),
        P(("groups", "op"), None, None, None),
        P(("groups", "sector", "blk")),
        P(("groups", "sector", "blk")),
        P(("groups", "op"), ("sector", "blk")),
        P(("groups", "sector"), "blk", None),
    )
    out_specs = P(("groups", "sector", "blk"), None, None)
    sizes = tuple(mesh.shape[name] for name in ("sector", "blk", "op"))
    return jax.shard_map(
        functools.partial(shards, sizes), mesh=mesh, in_specs=in_specs, out_specs=out_specs, check_vma=False
    )
```

```python
import functools

import jax
import jax.numpy as jnp
from jax import lax
from jax.experimental import pallas as pl
from jax.experimental.pallas import tpu as pltpu
from jax.sharding import PartitionSpec as P

CAP = 4
GROUP = 4
SETS = 4
MOST_SLOTS = 64
BLOCK_K = 16
TAIL = 16
NT = (((1,), (1,)), ((), ()))


def arrange(left_qn, plan, blocks, left_local):
    mine = lax.axis_index("blk")
    count = left_qn.shape[0]

    def one_code(code, n):
        plan[count + 1 + code] = n
        owner = lax.rem(mine + lax.div(code, jnp.int32(left_local)), jnp.int32(blocks))
        wanted = owner * left_local + lax.rem(code, jnp.int32(left_local))

        for s in range(count):
            plan[n] = jnp.int32(s)
            n = n + (left_qn[s] == wanted).astype(jnp.int32)
        return n

    plan[count + 1 + blocks * left_local] = lax.fori_loop(0, blocks * left_local, one_code, jnp.int32(0))


def cut_kernel(left, direct, middle, sems):
    quarter, count = direct.shape[0], middle.shape[0]
    first = lax.rem(lax.axis_index("sector"), jnp.int32(2)) * (left.shape[0] - quarter)
    copies = [
        pltpu.make_async_copy(left.at[pl.ds(first, quarter)], direct, sems.at[0]),
        pltpu.make_async_copy(left.at[pl.ds(quarter, count)], middle, sems.at[1]),
    ]
    for copy in copies:
        copy.start()
    for copy in copies:
        copy.wait()


def right_kernel(
    blocks, left_local, left_qn_in, right_qn_in, psi_in, right_in, half, plan,
    left_qn, right_qn, psi, right, sources, sems,
):
    sectors, width = psi.shape[0], psi.shape[1]
    right_count = right.shape[1]
    steps = right.shape[0] // BLOCK_K
    zero = jnp.zeros((width, width), jnp.bfloat16)

    def right_copy(i):
        at = pl.ds(i * BLOCK_K, BLOCK_K)
        return pltpu.make_async_copy(right_in.at[at], right.at[at], sems.at[3 + i])

    copies = [
        pltpu.make_async_copy(left_qn_in, left_qn, sems.at[0]),
        pltpu.make_async_copy(right_qn_in, right_qn, sems.at[1]),
        pltpu.make_async_copy(psi_in, psi, sems.at[2]),
    ]
    for copy in copies:
        copy.start()
    for i in range(steps):
        right_copy(i).start()
    copies[0].wait()
    copies[1].wait()
    arrange(left_qn, plan, blocks, left_local)
    copies[2].wait()
    for pair in range(sectors // 2):
        for e in range(2):
            s = plan[2 * pair + e]
            block = psi[s].T
            for r in range(right_count):
                sources[pair, r * width : (r + 1) * width, e * width : (e + 1) * width] = jnp.where(
                    right_qn[s] == r, block, zero
                )

    def one_step(i, unused):
        right_copy(i).wait()
        at = pl.ds(i * BLOCK_K, BLOCK_K)
        stream = jnp.concatenate([right[at, r].reshape(BLOCK_K * width, width) for r in range(right_count)], axis=1)
        for pair in range(sectors // 2):
            product = jnp.dot(stream, sources[pair], preferred_element_type=jnp.float32)
            half[pair // 2, at, pair % 2] = product.astype(jnp.bfloat16).reshape(BLOCK_K, width, 2 * width)
        return unused

    lax.fori_loop(0, steps, one_step, 0)


def accumulate(code, pieces, plan, slots, half, totals):
    sectors, width = slots.shape[0], totals[0].shape[1]
    spare = totals[0].shape[0] - 1
    low, high = plan[sectors + 1 + code], plan[sectors + 2 + code]
    zero = jnp.zeros((width, width), jnp.bfloat16)

    def terms(g, count):
        places = [g * GROUP + j for j in range(count * GROUP)]
        members = [plan[at] for at in places]
        counts = [(low <= at) & (at < high) for at in places]
        for first, left in pieces:
            for i in range(left.shape[0]):
                k = first + i
                block = left[i]
                weights = jnp.concatenate(
                    [jnp.concatenate([block, zero], axis=1), jnp.concatenate([zero, block], axis=1)], axis=0
                )
                term = lax.dot_general(
                    half[pl.ds(g, count), k].reshape(count * GROUP // 2 * width, 2 * width),
                    weights,
                    NT,
                    preferred_element_type=jnp.float32,
                )
                for j in range(count * GROUP):
                    p, e = j // 2, j % 2
                    slot = jnp.where(counts[j], slots[members[j], k], spare)
                    totals[j % len(totals)][slot] += term[
                        p * width : (p + 1) * width, e * width : (e + 1) * width
                    ]

    def two_groups(i, unused):
        terms(start + 2 * i, 2)
        return unused

    def last_group(i, unused):
        terms(start + groups - 1, 1)
        return unused

    start = lax.div(low, jnp.int32(GROUP))
    groups = jnp.where(low < high, lax.div(high + GROUP - 1, jnp.int32(GROUP)) - start, 0)
    lax.fori_loop(0, lax.div(groups, 2), two_groups, 0)
    lax.fori_loop(0, lax.rem(groups, 2), last_group, 0)


def own_kernel(plan, slots, half, left, direct, *totals):
    shifts, quarter, left_local = direct.shape[0], direct.shape[1], direct.shape[2]
    near = lax.rem(lax.axis_index("sector"), jnp.int32(2)) * (left.shape[0] - quarter)
    for total in totals:
        total[...] = jnp.zeros_like(total)
    for l in range(left_local):
        accumulate(l, [(0, left.at[:, l])], plan, slots, half, totals)

    def one_shift(d, unused):
        for l in range(left_local):
            accumulate((d + 1) * left_local + l, [(near, direct.at[d, :, l])], plan, slots, half, totals)
        return unused

    lax.fori_loop(0, shifts, one_shift, 0)


def other_kernel(rows, sets, plan, slots, half, swapped, middle, *rest):
    totals, (keep, give) = rest[sets : 2 * sets], rest[2 * sets :]
    shifts, quarter, left_local = swapped.shape[0], swapped.shape[1], swapped.shape[2]
    row, side = lax.axis_index("sector"), lax.axis_index("op")
    operators, width = slots.shape[1], totals[0].shape[1]
    far = (1 - lax.rem(row, jnp.int32(2))) * (operators - quarter)

    def one_shift(d, unused):
        for l in range(left_local):
            pieces = [(quarter, middle.at[d, :, l]), (far, swapped.at[d, :, l])]
            accumulate((d + 1) * left_local + l, pieces, plan, slots, half, totals)
        return unused

    lax.fori_loop(0, shifts, one_shift, 0)
    part = CAP // 2
    for owner in range(rows):
        for m in range(part):
            at = owner * CAP + side * part + m
            keep[owner * part + m] = sum(total[at] for total in totals)
            at = owner * CAP + (1 - side) * part + m
            give[owner * part + m] = sum(total[at] for total in totals).astype(jnp.bfloat16)


def combine_kernel(shifts, slot_target, keep, taken, *outs):
    part, width = CAP // 2, keep.shape[1]
    row, side = lax.axis_index("sector"), lax.axis_index("op")
    line = lax.broadcasted_iota(jnp.int32, (TAIL, width), 0)
    for d, out in zip(shifts, outs):
        owner = lax.rem(row + d, jnp.int32(len(outs)))
        ids = jnp.zeros((TAIL, width), jnp.int32)
        for m in range(part):
            block = keep[owner * part + m] + taken[owner * part + m].astype(jnp.float32)
            out[m * width : (m + 1) * width, :] = block.astype(jnp.bfloat16)
            ids = jnp.where(line == m, slot_target[0, 0, owner * CAP + side * part + m], ids)
        out[part * width :, :] = ids.astype(jnp.float32).astype(jnp.bfloat16)


def assemble_kernel(rows, *rest):
    mine, theirs, out = rest[:rows], rest[rows : 2 * rows], rest[-1]
    part, width = CAP // 2, out.shape[1]
    side = lax.axis_index("op")
    out[...] = jnp.zeros_like(out)
    for d in range(rows):
        for h in range(2):
            ids = jnp.where(side == h, mine[d][part * width :, :], theirs[d][part * width :, :]).astype(jnp.float32)
            for m in range(part):
                at = pl.ds(m * width, width)
                block = jnp.where(side == h, mine[d][at, :], theirs[d][at, :])
                target = jnp.max(ids[m : m + 1, :]).astype(jnp.int32)
                out[target] += block.T.astype(jnp.float32)


def shards(sizes, psi, left_ops, right_ops, left_qn, right_qn, pair_slot, slot_target):
    rows, blocks, halves = sizes
    sectors, width = psi.shape[0], psi.shape[1]
    operators, left_local = left_ops.shape[0], left_ops.shape[1]
    slots = pair_slot.T
    smem = pl.BlockSpec(memory_space=pltpu.SMEM)
    vmem = pl.BlockSpec(memory_space=pltpu.VMEM)
    hbm = pl.BlockSpec(memory_space=pltpu.HBM)
    sets = max(1, min(SETS, MOST_SLOTS // (rows * CAP)))
    total_shape = (rows * CAP + 1, width, width)
    right_count = right_ops.shape[1]
    params = pltpu.CompilerParams(vmem_limit_bytes=12 * 2**20)

    def cost(share):
        flops = int(16 * operators * sectors * width**3 * share)
        return pl.CostEstimate(flops=flops, bytes_accessed=4 * 2**20, transcendentals=0)

    assert rows % 2 == 0
    quarter = operators * 9 // 32
    swap = [(i, i ^ 1) for i in range(rows)]

    def over_blocks(part):
        return [lax.ppermute(part, "blk", [((b + d) % blocks, b) for b in range(blocks)]) for d in range(1, blocks)]

    direct, middle = pl.pallas_call(
        cut_kernel,
        out_shape=[
            jax.ShapeDtypeStruct((count, *left_ops.shape[1:]), left_ops.dtype)
            for count in (quarter, operators - 2 * quarter)
        ],
        in_specs=[hbm],
        out_specs=[vmem] * 2,
        scratch_shapes=[pltpu.SemaphoreType.DMA((2,))],
        compiler_params=params,
        name="cut_left",
    )(pltpu.with_memory_space_constraint(left_ops, pltpu.HBM))
    direct, middle = over_blocks(direct), over_blocks(middle)

    half, plan = pl.pallas_call(
        functools.partial(right_kernel, blocks, left_local),
        out_shape=[
            jax.ShapeDtypeStruct((sectors // GROUP, operators, GROUP // 2, width, 2 * width), jnp.bfloat16),
            jax.ShapeDtypeStruct((sectors + 2 + blocks * left_local,), jnp.int32),
        ],
        in_specs=[hbm] * 4,
        out_specs=[vmem, smem],
        scratch_shapes=[
            pltpu.SMEM(left_qn.shape, jnp.int32),
            pltpu.SMEM(right_qn.shape, jnp.int32),
            pltpu.VMEM(psi.shape, psi.dtype),
            pltpu.VMEM(right_ops.shape, right_ops.dtype),
            pltpu.VMEM((sectors // 2, right_count * width, 2 * width), jnp.bfloat16),
            pltpu.SemaphoreType.DMA((3 + operators // BLOCK_K,)),
        ],
        compiler_params=params,
        cost_estimate=cost(0.5),
        name="right_side",
    )(*(pltpu.with_memory_space_constraint(x, pltpu.HBM) for x in (left_qn, right_qn, psi, right_ops)))
    half, direct = lax.optimization_barrier((half, direct))
    swapped = [lax.ppermute(part, "sector", swap) for part in direct]
    totals = pl.pallas_call(
        own_kernel,
        out_shape=[jax.ShapeDtypeStruct(total_shape, jnp.float32)] * sets,
        in_specs=[smem] * 2 + [vmem] * 3,
        out_specs=[vmem] * sets,
        compiler_params=params,
        cost_estimate=cost(0.25),
        name="own_left",
    )(plan, slots, half, left_ops, jnp.stack(direct))
    results = pl.pallas_call(
        functools.partial(other_kernel, rows, sets),
        out_shape=[jax.ShapeDtypeStruct(total_shape, jnp.float32)] * sets
        + [jax.ShapeDtypeStruct((rows * CAP // 2, width, width), kind) for kind in (jnp.float32, jnp.bfloat16)],
        in_specs=[smem] * 2 + [vmem] * (3 + sets),
        out_specs=[vmem] * (sets + 2),
        input_output_aliases={5 + j: j for j in range(sets)},
        compiler_params=params,
        cost_estimate=cost(0.25),
        name="other_left",
    )(plan, slots, half, jnp.stack(swapped), jnp.stack(middle), *totals)
    keep, give = results[sets:]

    def over_cores(block):
        return lax.ppermute(block, "op", [(h, halves - 1 - h) for h in range(halves)])

    shifts = sorted(range(1, rows), key=lambda d: (abs(d - rows // 2), d)) + [0]
    partial = pl.pallas_call(
        functools.partial(combine_kernel, shifts),
        out_shape=[jax.ShapeDtypeStruct((CAP // 2 * width + TAIL, width), jnp.bfloat16)] * rows,
        in_specs=[smem] + [vmem] * 2,
        out_specs=[vmem] * rows,
        compiler_params=params,
        name="combine",
    )(slot_target, keep, over_cores(give))
    mine = [
        lax.ppermute(block, "sector", [(i, (i + d) % rows) for i in range(rows)]) if d else block
        for d, block in zip(shifts, partial)
    ]
    theirs = [over_cores(block) for block in mine]
    return pl.pallas_call(
        functools.partial(assemble_kernel, rows),
        out_shape=jax.ShapeDtypeStruct((sectors, width, width), jnp.float32),
        in_specs=[vmem] * (2 * rows),
        out_specs=vmem,
        compiler_params=params,
        name="assemble",
    )(*mine, *theirs)


def solution(mesh):
    in_specs = (
        P(("groups", "sector", "blk"), None, None),
        P(("groups", "op"), "blk", None, None),
        P(("groups", "op"), None, None, None),
        P(("groups", "sector", "blk")),
        P(("groups", "sector", "blk")),
        P(("groups", "op"), ("sector", "blk")),
        P(("groups", "sector"), "blk", None),
    )
    out_specs = P(("groups", "sector", "blk"), None, None)
    sizes = tuple(mesh.shape[name] for name in ("sector", "blk", "op"))
    return jax.shard_map(
        functools.partial(shards, sizes), mesh=mesh, in_specs=in_specs, out_specs=out_specs, check_vma=False
    )
```
